128 devices in a mesh: cube: 32 (over x, z, y_hi), grid: 4 (over y_lo, core).
Axes of the slice: x: 4, y: 4 (y_hi: 2, y_lo: 2; y = y_hi * 2 + y_lo), z: 4, core: 2. Of those that a mesh axis runs over, the one named last changes fastest.
Arguments:
- front_root: float32 [16384, 16384], P('cube', 'grid'), as said below
- front_upper: float32 [16384, 8192], P('cube', 'grid'), as said below
- front_middle: float32 [16384, 4096], P('cube', 'grid'), as said below
- front_lower: float32 [16384, 2048], P('cube', 'grid'), as said below
- place_upper: int32 [2, 62], replicated, may hold values from 0 to 127, as said below
- place_middle: int32 [4, 30], replicated, may hold values from 0 to 63, as said below
- place_lower: int32 [8, 14], replicated, may hold values from 0 to 31, as said below
Outputs:
- factor_root: float32 [16384, 256], P('cube')
- factor_upper: float32 [16384, 256], P('cube')
- factor_middle: float32 [16384, 256], P('cube')
- factor_lower: float32 [16384, 256], P('cube')
- root_rest: float32 [16384, 16384], P('cube', 'grid')
The draws below stay inside these ranges and needn't reach their ends.
Inputs may be any that keep to these rules, and one draw needn't show every extreme that they name: `front_root`: each front is symmetric positive definite, with diagonal entries of at least 2 and all entries of magnitude at most 12. `front_upper`: each front is symmetric positive definite, with diagonal entries of at least 2 and all entries of magnitude at most 12. `front_middle`: each front is symmetric positive definite, with diagonal entries of at least 2 and all entries of magnitude at most 12. `front_lower`: each front is symmetric positive definite, with diagonal entries of at least 2 and all entries of magnitude at most 12. `place_upper`: row c lists the parent block row of child c's block row 2 + u; within a row the values are distinct, and each is congruent to 2 + u modulo max(16, G). `place_middle`: row c lists the parent block row of child c's block row 2 + u; within a row the values are distinct, and each is congruent to 2 + u modulo max(8, G). `place_lower`: row c lists the parent block row of child c's block row 2 + u; within a row the values are distinct, and each is congruent to 2 + u modulo max(4, G).
All inputs are finite; a program needn't handle non-finite values.
Results may differ from the reference program's by a relative error of at most 0.0001.
Values sent between devices are 32-bit elements; how exact they have to be, the bound alone decides.
No kernel may reach another device: no remote copies, remote signals or barrier semaphores. Data moves between devices by JAX's collectives and lax.ppermute only.
A program may use at most 192 MiB of HBM per device.

```python
import math
import jax
import jax.numpy as jnp
from jax import lax

BS = 128
PIVOTS = 2
ROWS = 4
SUB0 = 32
SUB1 = 16
SUB2 = 8
SUB3 = 4
ORDER0 = 128
ORDER1 = 64
ORDER2 = 32
ORDER3 = 16
N_CUBE = 32
N_GRID = 4


def symmetric_fronts(key, sub_size, block_order, low_scale, high_scale):
    fronts = N_CUBE // sub_size
    entry_count = block_order * BS
    inner = PIVOTS * BS
    factor_key, scale_key, diag_key = jax.random.split(key, 3)
    factor_part = jax.random.randint(factor_key, (fronts, entry_count, inner), -2, 3).astype(jnp.float32)
    products = jnp.einsum('fik,fjk->fij', factor_part, factor_part, precision=lax.Precision.HIGHEST)
    scales = jnp.exp(jax.random.uniform(scale_key, (fronts, entry_count), jnp.float32, math.log(low_scale), math.log(high_scale)))
    weights = scales[:, :, None] * scales[:, None, :] * (1.0 / inner)
    full_front = products * weights
    diagonal = jax.random.uniform(diag_key, (fronts, entry_count), jnp.float32, 2.0, 4.0)
    diag_index = jnp.arange(entry_count)
    full_front = full_front.at[:, diag_index, diag_index].add(diagonal)
    local_cols = block_order // N_GRID
    blocks = full_front.reshape(fronts, ROWS, sub_size, BS, local_cols, N_GRID, BS)
    blocks = blocks.transpose(0, 2, 1, 3, 5, 4, 6)
    return blocks.reshape(fronts * sub_size * ROWS * BS, N_GRID * local_cols * BS)


def child_places(key, child_count, child_order, modulus):
    classes = child_order // modulus
    key_list = jax.random.split(key, child_count * modulus)
    orders = jax.vmap(lambda one_key: jax.random.permutation(one_key, 2 * classes))(key_list)
    orders = orders.reshape(child_count, modulus, 2 * classes)
    child_rows = jnp.arange(PIVOTS, child_order)
    residue = child_rows % modulus
    rank_of = child_rows // modulus
    picked = orders[:, residue, rank_of]
    return (residue[None, :] + modulus * picked).astype(jnp.int32)


def draw_front_root(key, part):
    key = jax.random.fold_in(key, 11)
    return symmetric_fronts(key, SUB0, ORDER0, 1.0, 1.0)


def draw_front_upper(key, part):
    key = jax.random.fold_in(key, 12)
    return symmetric_fronts(key, SUB1, ORDER1, 1.0, 1.0)


def draw_front_middle(key, part):
    key = jax.random.fold_in(key, 13)
    return symmetric_fronts(key, SUB2, ORDER2, 1.0, 1.0)


def draw_front_lower(key, part):
    key = jax.random.fold_in(key, 14)
    return symmetric_fronts(key, SUB3, ORDER3, 1.0, 1.0)


def draw_place_upper(key, part):
    key = jax.random.fold_in(key, 21)
    return child_places(key, 2, ORDER1, max(SUB1, N_GRID))


def draw_place_middle(key, part):
    key = jax.random.fold_in(key, 22)
    return child_places(key, 4, ORDER2, max(SUB2, N_GRID))


def draw_place_lower(key, part):
    key = jax.random.fold_in(key, 23)
    return child_places(key, 8, ORDER3, max(SUB3, N_GRID))


def setup_inputs(seed: int = 0) -> dict:
    keys = jax.random.split(jax.random.key(seed), 8)
    front_root = draw_front_root(jax.random.fold_in(keys[7], 71), 0)
    front_upper = draw_front_upper(jax.random.fold_in(keys[7], 71), 0)
    front_middle = draw_front_middle(jax.random.fold_in(keys[7], 71), 0)
    front_lower = draw_front_lower(jax.random.fold_in(keys[7], 71), 0)
    place_upper = draw_place_upper(jax.random.fold_in(keys[7], 71), 0)
    place_middle = draw_place_middle(jax.random.fold_in(keys[7], 71), 0)
    place_lower = draw_place_lower(jax.random.fold_in(keys[7], 71), 0)
    return {"front_root": front_root, "front_upper": front_upper, "front_middle": front_middle, "front_lower": front_lower, "place_upper": place_upper, "place_middle": place_middle, "place_lower": place_lower}


HIGHEST = lax.Precision.HIGHEST

def dense_fronts(stored, sub_size, block_order):
    fronts = N_CUBE // sub_size
    local_cols = block_order // N_GRID
    blocks = stored.reshape(fronts, sub_size, ROWS, BS, N_GRID, local_cols, BS)
    blocks = blocks.transpose(0, 2, 1, 3, 5, 4, 6)
    return blocks.reshape(fronts, block_order * BS, block_order * BS)

def stored_fronts(full_fronts, sub_size, block_order):
    fronts = full_fronts.shape[0]
    local_cols = block_order // N_GRID
    blocks = full_fronts.reshape(fronts, ROWS, sub_size, BS, local_cols, N_GRID, BS)
    blocks = blocks.transpose(0, 2, 1, 3, 5, 4, 6)
    return blocks.reshape(fronts * sub_size * ROWS * BS, N_GRID * local_cols * BS)

def stored_factor(full_factor, sub_size):
    fronts = full_factor.shape[0]
    blocks = full_factor.reshape(fronts, ROWS, sub_size, BS, PIVOTS * BS).transpose(0, 2, 1, 3, 4)
    return blocks.reshape(fronts * sub_size * ROWS * BS, PIVOTS * BS)

def eliminate(full_front):
    entry_count = full_front.shape[0]
    block_ids = jnp.arange(entry_count) // BS
    factors = []
    for pivot_at in range(PIVOTS):
        low_edge = pivot_at * BS
        lower_tri = jnp.linalg.cholesky(full_front[low_edge:low_edge + BS, low_edge:low_edge + BS])
        column = full_front[:, low_edge:low_edge + BS]
        solved = jax.scipy.linalg.solve_triangular(lower_tri, column.T, lower=True).T
        solved = jnp.where((block_ids > pivot_at)[:, None], solved, jnp.float32(0.0))
        full_front = full_front - jnp.dot(solved, solved.T, precision=HIGHEST)
        factors.append(solved.at[low_edge:low_edge + BS].set(lower_tri))
    return (full_front, jnp.concatenate(factors, 1))

def extend_add(parent_front, child_front, mapping):
    parent_blocks = parent_front.shape[0] // BS
    child_blocks = child_front.shape[0] // BS
    child_part = child_front.reshape(child_blocks, BS, child_blocks, BS).transpose(0, 2, 1, 3)[PIVOTS:, PIVOTS:]
    blocks = parent_front.reshape(parent_blocks, BS, parent_blocks, BS).transpose(0, 2, 1, 3)
    blocks = blocks.at[mapping[:, None], mapping[None, :]].add(child_part)
    return blocks.transpose(0, 2, 1, 3).reshape(parent_blocks * BS, parent_blocks * BS)

def reference(front_root, front_upper, front_middle, front_lower, place_upper, place_middle, place_lower):
    stored = (front_root, front_upper, front_middle, front_lower)
    tables = (None, place_upper, place_middle, place_lower)
    factor_list = [None, None, None, None]
    below = None
    for depth_level in (3, 2, 1, 0):
        sub_size = N_CUBE >> depth_level
        block_order = ROWS * sub_size
        fronts = dense_fronts(stored[depth_level], sub_size, block_order)
        finished = []
        columns = []
        for front_at in range(N_CUBE // sub_size):
            full_front = fronts[front_at]
            if below is not None:
                for child_at in (2 * front_at, 2 * front_at + 1):
                    full_front = extend_add(full_front, below[child_at], tables[depth_level + 1][child_at])
            full_front, factor = eliminate(full_front)
            finished.append(full_front)
            columns.append(factor)
        below = finished
        factor_list[depth_level] = stored_factor(jnp.stack(columns), sub_size)
    root_front = below[0]
    keep_ids = jnp.arange(root_front.shape[0]) // BS >= PIVOTS
    root_front = jnp.where(keep_ids[:, None] & keep_ids[None, :], root_front, jnp.float32(0.0))
    rest = stored_fronts(root_front[None], N_CUBE, ORDER0)
    return (factor_list[0], factor_list[1], factor_list[2], factor_list[3], rest)
```

```python
import functools

import jax
import jax.numpy as jnp
from jax import lax
from jax.experimental import pallas as pl
from jax.experimental.pallas import tpu as pltpu
from jax.sharding import PartitionSpec as P

BS = 128
PIVOTS = 2
ROWS = 4
WIDE = PIVOTS * BS
HIGHEST = lax.Precision.HIGHEST
VMEM_LIMIT = 48 * 1024 * 1024


def dot_nn(a, b):
    return jnp.dot(a, b, precision=HIGHEST, preferred_element_type=jnp.float32)


def dot_nt(a, b):
    return lax.dot_general(
        a, b, (((1,), (1,)), ((), ())), precision=HIGHEST, preferred_element_type=jnp.float32
    )


def factor_block(block):
    n = BS
    rows = lax.broadcasted_iota(jnp.int32, (n, n), 0)
    eye = (rows == lax.broadcasted_iota(jnp.int32, (n, n), 1)).astype(jnp.float32)
    parts = [block, eye]
    for j in range(0, n, 2):
        c0 = jnp.broadcast_to(parts[0][:, j : j + 1], (n, n))
        c1 = jnp.broadcast_to(parts[0][:, j + 1 : j + 2], (n, n))
        d0, cross, d1 = c0[j : j + 1], c0[j + 1 : j + 2], c1[j + 1 : j + 2]
        r0 = 1.0 / d0
        ratio = cross * r0
        r1 = 1.0 / (d1 - ratio * cross)
        m0 = jnp.where(rows > j, c0 * r0, 0.0)
        m1 = jnp.where(rows > j + 1, (c1 - m0 * cross) * r1, 0.0)
        done = []
        for part in parts:
            first = part[j : j + 1]
            second = part[j + 1 : j + 2] - ratio * first
            done.append(part - m0 * first - m1 * second)
        parts = done
    diag = jnp.sum(jnp.where(eye > 0, parts[0], 0.0), 1, keepdims=True)
    scale = lax.rsqrt(diag)
    return (parts[0] * scale).T, parts[1] * scale


def pivot_kernel(rows_ref, low_ref, inv_ref):
    c0, i0 = factor_block(rows_ref[:BS, :BS])
    k10 = dot_nt(rows_ref[BS:, :BS], i0)
    c1, i1 = factor_block(rows_ref[BS:, BS:] - dot_nt(k10, k10))
    lane = lax.broadcasted_iota(jnp.int32, (BS, BS), 1)
    sub = lax.broadcasted_iota(jnp.int32, (BS, BS), 0)
    low = lane <= sub
    zero = jnp.zeros((BS, BS), jnp.float32)
    low_ref[:BS, :BS] = jnp.where(low, c0, 0.0)
    low_ref[:BS, BS:] = zero
    low_ref[BS:, :BS] = k10
    low_ref[BS:, BS:] = jnp.where(low, c1, 0.0)
    inv_ref[:BS, :BS] = i0
    inv_ref[:BS, BS:] = zero
    inv_ref[BS:, :BS] = -dot_nn(i1, dot_nn(k10, i0))
    inv_ref[BS:, BS:] = i1


def pivot_factor(pivot_rows):
    shape = jax.ShapeDtypeStruct((WIDE, WIDE), jnp.float32)
    whole = pl.BlockSpec(memory_space=pltpu.VMEM)
    return pl.pallas_call(
        pivot_kernel,
        out_shape=[shape, shape],
        in_specs=[whole],
        out_specs=[whole, whole],
        compiler_params=pltpu.CompilerParams(vmem_limit_bytes=VMEM_LIMIT),
        name="pivot_factor",
    )(pivot_rows)


def update_kernel(cols, has_children, is_root, info_ref, *refs):
    if has_children:
        front_ref, own_ref, other_ref, key_ref, panel_ref, inv_ref, out_ref = refs
    else:
        front_ref, key_ref, panel_ref, inv_ref, out_ref = refs
    at = pl.program_id(0)
    solved = dot_nt(panel_ref[0], inv_ref[...])
    terms = dot_nt(key_ref[...], solved)
    width = ROWS + cols
    for r in range(ROWS):
        span = slice(r * BS, (r + 1) * BS)
        block = front_ref[span, :] - terms[span, :]
        if has_children:
            for which, child_ref in ((0, own_ref), (1, other_ref)):
                source = info_ref[which * width + r]
                present = (source >= 0) & (info_ref[which * width + ROWS + at] >= 0)
                taken = child_ref[pl.ds(jnp.maximum(source, 0) * BS, BS), :]
                block = block + jnp.where(present, taken, 0.0)
        if is_root:
            keep = (info_ref[2 * width + r] >= PIVOTS) & (info_ref[2 * width + ROWS + at] >= PIVOTS)
            block = jnp.where(keep, block, 0.0)
        out_ref[span, :] = block


def update_front(front, own, other, key, panels, inverse, info, panel_of, is_root):
    cols = front.shape[1] // BS
    width = ROWS + cols
    has_children = own is not None
    height = ROWS * BS
    column = pl.BlockSpec((height, BS), lambda c, info: (0, c))
    specs, args = [column], [front]
    if has_children:
        for which, child in ((0, own), (1, other)):
            specs.append(
                pl.BlockSpec(
                    (height, BS),
                    lambda c, info, which=which: (0, jnp.maximum(info[which * width + ROWS + c], 0)),
                )
            )
            args.append(child)
    specs += [
        pl.BlockSpec((height, WIDE), lambda c, info: (0, 0)),
        pl.BlockSpec((1, BS, WIDE), lambda c, info: (panel_of(c), 0, 0)),
        pl.BlockSpec((WIDE, WIDE), lambda c, info: (0, 0)),
    ]
    args += [key, panels, inverse]
    return pl.pallas_call(
        functools.partial(update_kernel, cols, has_children, is_root),
        out_shape=jax.ShapeDtypeStruct(front.shape, jnp.float32),
        grid_spec=pltpu.PrefetchScalarGridSpec(
            num_scalar_prefetch=1, grid=(cols,), in_specs=specs, out_specs=column
        ),
        compiler_params=pltpu.CompilerParams(vmem_limit_bytes=VMEM_LIMIT),
        cost_estimate=pl.CostEstimate(
            flops=2 * height * WIDE * cols * BS * 2,
            bytes_accessed=16 * height * cols * BS,
            transcendentals=0,
        ),
        name="update_front",
    )(info, *args)


def send(block, route):
    pairs = [(a[0] * 4 + a[1], b[0] * 4 + b[1]) for a, b in route]
    return lax.ppermute(block, ("cube", "grid"), pairs)


def both_pivots(piece, cube_count, grid_at):
    got = []
    for step in (1, 2, 3):
        route = [((s, g), (s, g ^ step)) for s in range(cube_count) for g in (0, 1)]
        got.append(send(piece, route))
    near, far, cross = got
    first = jnp.where(grid_at == 0, piece, jnp.where(grid_at == 1, near, jnp.where(grid_at == 2, far, cross)))
    second = jnp.where(grid_at == 1, piece, jnp.where(grid_at == 0, near, jnp.where(grid_at == 3, far, cross)))
    return jnp.concatenate([first, second], -1)


def class_panels(own_rows, sub_size, cube_count, cube_at, grid_at):
    quarter = cube_at % 4
    mine = lax.dynamic_index_in_dim(own_rows, quarter, 0, keepdims=False)
    total = jnp.where(quarter == grid_at, mine, 0.0)
    for step in (1, 2, 3):
        route = [((s, s % 4), (s ^ step, s % 4)) for s in range(cube_count)]
        total = total + send(
            lax.dynamic_index_in_dim(own_rows, quarter ^ step, 0, keepdims=False), route
        )
    groups = None
    if sub_size < cube_count:
        groups = [[b + i for i in range(sub_size)] for b in range(0, cube_count, sub_size)]
    return lax.all_to_all(
        jnp.broadcast_to(total[None], (sub_size, BS, WIDE)), "cube", 0, 0, axis_index_groups=groups
    )


def child_sources(table, child_size, cube_at, grid_at):
    parent_size = 2 * child_size
    slot = cube_at % parent_size
    front = cube_at // child_size
    maps = jnp.stack([table[front], table[front ^ 1]])
    rows = jnp.arange(ROWS) * parent_size + slot
    cols = jnp.arange(parent_size) * 4 + grid_at
    child_ids = jnp.arange(PIVOTS, ROWS * child_size)
    row_hit = maps[:, None, :] == rows[None, :, None]
    col_hit = maps[:, None, :] == cols[None, :, None]
    row_from = jnp.sum(jnp.where(row_hit, child_ids // child_size + 1, 0), 2) - 1
    col_from = jnp.sum(jnp.where(col_hit, child_ids // 4 + 1, 0), 2) - 1
    return jnp.concatenate([row_from, col_from], 1).astype(jnp.int32)


def placed_rows(column, row_from, col_from):
    blocks = column.reshape(ROWS, BS, BS)
    taken = jnp.take(blocks, jnp.maximum(row_from, 0), axis=0)
    keep = (row_from >= 0) & (col_from >= 0)
    return jnp.where(keep[:, None, None], taken, 0.0).reshape(ROWS * BS, BS)


def on_device(
    front_root, front_upper, front_middle, front_lower, place_upper, place_middle, place_lower
):
    cube_count = lax.axis_size("cube")
    cube_at = lax.axis_index("cube")
    grid_at = lax.axis_index("grid")
    stored = (front_root, front_upper, front_middle, front_lower)
    tables = (None, place_upper, place_middle, place_lower)
    factor_list = [None, None, None, None]
    own = other = None
    for depth in (3, 2, 1, 0):
        sub_size = cube_count >> depth
        slot = cube_at % sub_size
        front = stored[depth]
        panel = front[:, :BS]
        row_ids = jnp.arange(ROWS) * sub_size + slot
        col_ids = jnp.arange(sub_size) * 4 + grid_at
        places = jnp.concatenate([row_ids, col_ids]).astype(jnp.int32)
        if own is None:
            info = places
        else:
            half = sub_size // 2
            sources = child_sources(tables[depth + 1], half, cube_at, grid_at)
            first_col = jnp.maximum(sources[:, ROWS], 0)
            mine = lax.dynamic_slice_in_dim(own, first_col[0] * BS, BS, 1)
            info = jnp.concatenate([sources.reshape(-1), places])
            got = send(
                mine,
                [((s, g), (s ^ half, g)) for s in range(cube_count) for g in (0, 1)],
            )
            other = send(own, [((s, g), (s ^ half, g)) for s in range(cube_count) for g in range(4)])
            panel = (
                panel
                + placed_rows(mine, sources[0, :ROWS], sources[0, ROWS])
                + placed_rows(got, sources[1, :ROWS], sources[1, ROWS])
            )
        own_rows = both_pivots(panel, cube_count, grid_at)
        if sub_size == 4:
            pieces = [own_rows]
            for step in (1, 2, 3):
                pieces.append(
                    send(
                        own_rows,
                        [((s, g), (s ^ step, g)) for s in range(cube_count) for g in range(4)],
                    )
                )
            pieces = jnp.stack(pieces)
            panels = lax.dynamic_index_in_dim(pieces, slot ^ grid_at, 0, keepdims=False)
            panels = panels.reshape(ROWS, BS, WIDE)
            pivot_rows = jnp.concatenate(
                [
                    lax.dynamic_index_in_dim(pieces, slot, 0, keepdims=False)[:BS],
                    lax.dynamic_index_in_dim(pieces, slot ^ 1, 0, keepdims=False)[:BS],
                ]
            )
            panel_of = lambda c: c
        else:
            panels = class_panels(
                own_rows.reshape(ROWS, BS, WIDE), sub_size, cube_count, cube_at, grid_at
            )
            pivot_rows = both_pivots(panels[0].reshape(BS, WIDE), cube_count, grid_at)
            pivot_rows = jnp.concatenate([pivot_rows[:, :WIDE], pivot_rows[:, WIDE:]])
            per_row = sub_size // 4
            panel_of = lambda c, per_row=per_row: lax.rem(c, per_row) * 4 + lax.div(c, per_row)
        low, inverse = pivot_factor(pivot_rows)
        solved = dot_nt(own_rows, inverse)
        pivot_slot = jnp.minimum(slot, PIVOTS - 1)
        head = jnp.where(
            slot < PIVOTS, lax.dynamic_slice_in_dim(low, pivot_slot * BS, BS, 0), solved[:BS]
        )
        solved = jnp.concatenate([head, solved[BS:]])
        factor_list[depth] = solved
        own = update_front(
            front, own, other, solved, panels, inverse, info, panel_of, depth == 0
        )
    return (factor_list[0], factor_list[1], factor_list[2], factor_list[3], own)


def solution(mesh):
    return jax.shard_map(
        on_device,
        mesh=mesh,
        in_specs=(
            P("cube", "grid"),
            P("cube", "grid"),
            P("cube", "grid"),
            P("cube", "grid"),
            P(),
            P(),
            P(),
        ),
        out_specs=(
            P("cube", None),
            P("cube", None),
            P("cube", None),
            P("cube", None),
            P("cube", "grid"),
        ),
        check_vma=False,
    )
```

```python
import functools

import jax
import jax.numpy as jnp
from jax import lax
from jax.experimental import pallas as pl
from jax.experimental.pallas import tpu as pltpu
from jax.sharding import PartitionSpec as P

BS = 128
PIVOTS = 2
ROWS = 4
WIDE = PIVOTS * BS
HIGHEST = lax.Precision.HIGHEST
VMEM_LIMIT = 48 * 1024 * 1024


def dot_nn(a, b):
    return jnp.dot(a, b, precision=HIGHEST, preferred_element_type=jnp.float32)


def dot_nt(a, b):
    return lax.dot_general(
        a, b, (((1,), (1,)), ((), ())), precision=HIGHEST, preferred_element_type=jnp.float32
    )


def factor_block(block):
    n = BS
    rows = lax.broadcasted_iota(jnp.int32, (n, n), 0)
    eye = (rows == lax.broadcasted_iota(jnp.int32, (n, n), 1)).astype(jnp.float32)
    parts = [block, eye]
    for j in range(0, n, 2):
        c0 = jnp.broadcast_to(parts[0][:, j : j + 1], (n, n))
        c1 = jnp.broadcast_to(parts[0][:, j + 1 : j + 2], (n, n))
        d0, cross, d1 = c0[j : j + 1], c0[j + 1 : j + 2], c1[j + 1 : j + 2]
        r0 = 1.0 / d0
        ratio = cross * r0
        r1 = 1.0 / (d1 - ratio * cross)
        m0 = jnp.where(rows > j, c0 * r0, 0.0)
        m1 = jnp.where(rows > j + 1, (c1 - m0 * cross) * r1, 0.0)
        done = []
        for part in parts:
            first = part[j : j + 1]
            second = part[j + 1 : j + 2] - ratio * first
            done.append(part - m0 * first - m1 * second)
        parts = done
    diag = jnp.sum(jnp.where(eye > 0, parts[0], 0.0), 1, keepdims=True)
    scale = lax.rsqrt(diag)
    return (parts[0] * scale).T, parts[1] * scale


def pivot_kernel(rows_ref, low_ref, inv_ref):
    c0, i0 = factor_block(rows_ref[:BS, :BS])
    k10 = dot_nt(rows_ref[BS:, :BS], i0)
    c1, i1 = factor_block(rows_ref[BS:, BS:] - dot_nt(k10, k10))
    lane = lax.broadcasted_iota(jnp.int32, (BS, BS), 1)
    sub = lax.broadcasted_iota(jnp.int32, (BS, BS), 0)
    low = lane <= sub
    zero = jnp.zeros((BS, BS), jnp.float32)
    low_ref[:BS, :BS] = jnp.where(low, c0, 0.0)
    low_ref[:BS, BS:] = zero
    low_ref[BS:, :BS] = k10
    low_ref[BS:, BS:] = jnp.where(low, c1, 0.0)
    inv_ref[:BS, :BS] = i0
    inv_ref[:BS, BS:] = zero
    inv_ref[BS:, :BS] = -dot_nn(i1, dot_nn(k10, i0))
    inv_ref[BS:, BS:] = i1


def pivot_factor(pivot_rows):
    shape = jax.ShapeDtypeStruct((WIDE, WIDE), jnp.float32)
    whole = pl.BlockSpec(memory_space=pltpu.VMEM)
    return pl.pallas_call(
        pivot_kernel,
        out_shape=[shape, shape],
        in_specs=[whole],
        out_specs=[whole, whole],
        compiler_params=pltpu.CompilerParams(vmem_limit_bytes=VMEM_LIMIT),
        name="pivot_factor",
    )(pivot_rows)


def split_key(a):
    high = a.astype(jnp.bfloat16)
    low = (a - high.astype(jnp.float32)).astype(jnp.bfloat16)
    return jnp.concatenate([high, low, high], 1)


def split_value(a):
    high = a.astype(jnp.bfloat16)
    low = (a - high.astype(jnp.float32)).astype(jnp.bfloat16)
    return jnp.concatenate([high, high, low], 1)


def dot_split(key, value):
    return lax.dot_general(key, value, (((1,), (1,)), ((), ())), preferred_element_type=jnp.float32)


def update_kernel(cols, per, has_children, is_root, col_of, info_ref, *refs):
    front_ref, refs = refs[0], refs[1:]
    child_refs = ((), ())
    if has_children:
        child_refs, refs = (refs[:per], refs[per : 2 * per]), refs[2 * per :]
    key_ref, panel_ref, inv_ref, out_ref, key_split, inv_split = refs
    step = pl.program_id(0)

    @pl.when(step == 0)
    def _():
        key_split[...] = split_key(key_ref[...])
        inv_split[...] = split_value(inv_ref[...])

    panel = panel_ref[...].reshape(per * BS, WIDE)
    solved = dot_split(split_key(panel), inv_split[...])
    terms = dot_split(key_split[...], split_value(solved))
    width = ROWS + cols
    places = 2 * width if has_children else 0
    for t in range(per):
        at = col_of(step, info_ref) * per + t
        lanes = slice(t * BS, (t + 1) * BS)
        for r in range(ROWS):
            span = slice(r * BS, (r + 1) * BS)
            block = front_ref[span, lanes] - terms[span, lanes]
            if has_children:
                for which in (0, 1):
                    source = info_ref[which * width + r]
                    present = (source >= 0) & (info_ref[which * width + ROWS + at] >= 0)
                    taken = child_refs[which][t][pl.ds(jnp.maximum(source, 0) * BS, BS), :]
                    block = block + jnp.where(present, taken, 0.0)
            if is_root:
                keep = (info_ref[places + r] >= PIVOTS) & (info_ref[places + ROWS + at] >= PIVOTS)
                block = jnp.where(keep, block, 0.0)
            out_ref[span, lanes] = block


def update_front(front, own, other, key, panels, inverse, info, is_root=False, single=False):
    cols = front.shape[1] // BS
    width = ROWS + cols
    has_children = own is not None
    height = ROWS * BS
    per = 1 if single else 2
    rel_at = (3 if has_children else 1) * width
    if single:
        col_of = lambda c, info: info[rel_at]
    else:
        col_of = lambda c, info: c
    outer, inner = panels.shape[:2]
    run = outer // per

    def panel_at(c, info):
        at = col_of(c, info)
        return (lax.rem(at, run), lax.div(at, run), 0, 0)

    column = pl.BlockSpec((height, per * BS), lambda c, info: (0, col_of(c, info)))
    specs, args = [column], [front]
    if has_children:
        for which, child in ((0, own), (1, other)):
            for t in range(per):
                specs.append(
                    pl.BlockSpec(
                        (height, BS),
                        lambda c, info, which=which, t=t: (
                            0,
                            jnp.maximum(info[which * width + ROWS + col_of(c, info) * per + t], 0),
                        ),
                    )
                )
                args.append(child)
    specs += [
        pl.BlockSpec((height, WIDE), lambda c, info: (0, 0)),
        pl.BlockSpec((per, 1, BS, WIDE), panel_at),
        pl.BlockSpec((WIDE, WIDE), lambda c, info: (0, 0)),
    ]
    args += [key, panels, inverse]
    steps = 1 if single else cols // per
    return pl.pallas_call(
        functools.partial(update_kernel, cols, per, has_children, is_root, col_of),
        out_shape=jax.ShapeDtypeStruct((height, steps * per * BS), jnp.float32),
        grid_spec=pltpu.PrefetchScalarGridSpec(
            num_scalar_prefetch=1,
            grid=(steps,),
            in_specs=specs,
            out_specs=pl.BlockSpec((height, per * BS), lambda c, info: (0, c)),
            scratch_shapes=[
                pltpu.VMEM((height, 3 * WIDE), jnp.bfloat16),
                pltpu.VMEM((WIDE, 3 * WIDE), jnp.bfloat16),
            ],
        ),
        compiler_params=pltpu.CompilerParams(vmem_limit_bytes=VMEM_LIMIT),
        cost_estimate=pl.CostEstimate(
            flops=2 * height * WIDE * steps * per * BS * 2,
            bytes_accessed=16 * height * steps * per * BS,
            transcendentals=0,
        ),
        name="update_front",
    )(info, *args)


def send(block, route):
    pairs = [(a[0] * 4 + a[1], b[0] * 4 + b[1]) for a, b in route]
    return lax.ppermute(block, ("cube", "grid"), pairs)


def both_pivots(piece, cube_count, grid_at):
    got = []
    for step in (1, 2, 3):
        route = [((s, g), (s, g ^ step)) for s in range(cube_count) for g in (0, 1)]
        got.append(send(piece, route))
    near, far, cross = got
    first = jnp.where(grid_at == 0, piece, jnp.where(grid_at == 1, near, jnp.where(grid_at == 2, far, cross)))
    second = jnp.where(grid_at == 1, piece, jnp.where(grid_at == 0, near, jnp.where(grid_at == 3, far, cross)))
    return jnp.concatenate([first, second], -1)


def shifted(block, bit, sources, sub_size, cube_count, grids=None):
    route = []
    for base in range(0, cube_count, sub_size):
        for s in range(sub_size):
            for g in range(4):
                if sources(s, g):
                    route.append(((base + s, g), (base + (s ^ bit), g)))
    return send(block, route)


def class_panels(own_rows, sub_size, cube_count, cube_at, grid_at):
    quarter = cube_at % 4
    mine_here = quarter == grid_at
    if sub_size == 4:
        total = jnp.where(mine_here, own_rows, 0.0)
        for step in (1, 2, 3):
            total = total + shifted(own_rows, step, lambda s, g: s == g, 4, cube_count)
        return total.reshape(ROWS, 1, BS, WIDE)
    total = jnp.where(
        mine_here, lax.dynamic_index_in_dim(own_rows, quarter, 0, keepdims=False), 0.0
    )
    for step in (1, 2, 3):
        total = total + shifted(
            lax.dynamic_index_in_dim(own_rows, quarter ^ step, 0, keepdims=False),
            step,
            lambda s, g: s % 4 == g,
            sub_size,
            cube_count,
        )
    groups = None
    if sub_size < cube_count:
        groups = [[b + i for i in range(sub_size)] for b in range(0, cube_count, sub_size)]
    gathered = lax.all_to_all(
        jnp.broadcast_to(total[None], (sub_size, BS, WIDE)), "cube", 0, 0, axis_index_groups=groups
    )
    return gathered.reshape(sub_size // 4, 4, BS, WIDE)


def pivot_rows_everywhere(own_rows, sub_size, cube_count, slot):
    row = own_rows[0]
    got = shifted(row, 1, lambda s, g: s < 2, sub_size, cube_count)
    both = jnp.where(slot == 0, jnp.concatenate([row, got]), jnp.concatenate([got, row]))
    known = 2
    while known < sub_size:
        bits = (known,) if 4 * known > sub_size else (known, 2 * known, 3 * known)
        moved = [shifted(both, bit, lambda s, g: s < known, sub_size, cube_count) for bit in bits]
        both = jnp.where(slot < known, both, sum(moved[1:], moved[0]))
        known *= len(bits) + 1
    return both


def child_sources(table, child_size, cube_at, grid_at):
    parent_size = 2 * child_size
    slot = cube_at % parent_size
    front = cube_at // child_size
    maps = jnp.stack([table[front], table[front ^ 1]])
    rows = jnp.arange(ROWS) * parent_size + slot
    cols = jnp.arange(parent_size) * 4 + grid_at
    child_ids = jnp.arange(PIVOTS, ROWS * child_size)
    row_hit = maps[:, None, :] == rows[None, :, None]
    col_hit = maps[:, None, :] == cols[None, :, None]
    row_from = jnp.sum(jnp.where(row_hit, child_ids // child_size + 1, 0), 2) - 1
    col_from = jnp.sum(jnp.where(col_hit, child_ids // 4 + 1, 0), 2) - 1
    return jnp.concatenate([row_from, col_from], 1).astype(jnp.int32)


def placed_rows(column, row_from, col_from):
    blocks = column.reshape(ROWS, BS, BS)
    taken = jnp.take(blocks, jnp.maximum(row_from, 0), axis=0)
    keep = (row_from >= 0) & (col_from >= 0)
    return jnp.where(keep[:, None, None], taken, 0.0).reshape(ROWS * BS, BS)


def on_device(
    front_root, front_upper, front_middle, front_lower, place_upper, place_middle, place_lower
):
    cube_count = lax.axis_size("cube")
    cube_at = lax.axis_index("cube")
    grid_at = lax.axis_index("grid")
    stored = (front_root, front_upper, front_middle, front_lower)
    tables = (None, place_upper, place_middle, place_lower)
    factor_list = [None, None, None, None]
    own = other = rel = sources = None
    for depth in (3, 2, 1, 0):
        sub_size = cube_count >> depth
        slot = cube_at % sub_size
        front = stored[depth]
        panel = front[:, :BS]
        row_ids = jnp.arange(ROWS) * sub_size + slot
        col_ids = jnp.arange(sub_size) * 4 + grid_at
        info = jnp.concatenate([row_ids, col_ids]).astype(jnp.int32)
        if own is not None:
            half = sub_size // 2
            got = shifted(rel, half, lambda s, g: g < 2, sub_size, cube_count)
            other = shifted(own, half, lambda s, g: True, sub_size, cube_count)
            panel = (
                panel
                + placed_rows(rel, sources[0, :ROWS], sources[0, ROWS])
                + placed_rows(got, sources[1, :ROWS], sources[1, ROWS])
            )
            info = jnp.concatenate([sources.reshape(-1), info])
        if depth > 0:
            sources = child_sources(tables[depth], sub_size, cube_at, grid_at)
            info = jnp.concatenate([info, jnp.maximum(sources[0, ROWS : ROWS + 1], 0)])
        own_rows = both_pivots(panel, cube_count, grid_at)
        blocks = own_rows.reshape(ROWS, BS, WIDE)
        low, inverse = pivot_factor(pivot_rows_everywhere(blocks, sub_size, cube_count, slot))
        panels = class_panels(blocks, sub_size, cube_count, cube_at, grid_at)
        solved = dot_nt(own_rows, inverse)
        pivot_slot = jnp.minimum(slot, PIVOTS - 1)
        head = jnp.where(
            slot < PIVOTS, lax.dynamic_slice_in_dim(low, pivot_slot * BS, BS, 0), solved[:BS]
        )
        solved = jnp.concatenate([head, solved[BS:]])
        factor_list[depth] = solved
        if depth > 0:
            rel = update_front(front, own, other, solved, panels, inverse, info, single=True)
        own = update_front(front, own, other, solved, panels, inverse, info, is_root=depth == 0)
    return (factor_list[0], factor_list[1], factor_list[2], factor_list[3], own)


def solution(mesh):
    return jax.shard_map(
        on_device,
        mesh=mesh,
        in_specs=(
            P("cube", "grid"),
            P("cube", "grid"),
            P("cube", "grid"),
            P("cube", "grid"),
            P(),
            P(),
            P(),
        ),
        out_specs=(
            P("cube", None),
            P("cube", None),
            P("cube", None),
            P("cube", None),
            P("cube", "grid"),
        ),
        check_vma=False,
    )
```

```python
import functools

import jax
import jax.numpy as jnp
from jax import lax
from jax.experimental import pallas as pl
from jax.experimental.pallas import tpu as pltpu
from jax.sharding import PartitionSpec as P

BS = 128
PIVOTS = 2
ROWS = 4
WIDE = PIVOTS * BS
HIGHEST = lax.Precision.HIGHEST
EARLY = 4
VMEM_LIMIT = 48 * 1024 * 1024


def dot_nn(a, b):
    return jnp.dot(a, b, precision=HIGHEST, preferred_element_type=jnp.float32)


def dot_nt(a, b):
    return lax.dot_general(
        a, b, (((1,), (1,)), ((), ())), precision=HIGHEST, preferred_element_type=jnp.float32
    )


def factor_block(block):
    n = BS
    rows = lax.broadcasted_iota(jnp.int32, (n, n), 0)
    eye = (rows == lax.broadcasted_iota(jnp.int32, (n, n), 1)).astype(jnp.float32)
    parts = [block, eye]
    for j in range(0, n, 2):
        c0 = jnp.broadcast_to(parts[0][:, j : j + 1], (n, n))
        c1 = jnp.broadcast_to(parts[0][:, j + 1 : j + 2], (n, n))
        d0, cross, d1 = c0[j : j + 1], c0[j + 1 : j + 2], c1[j + 1 : j + 2]
        r0 = 1.0 / d0
        ratio = cross * r0
        r1 = 1.0 / (d1 - ratio * cross)
        m0 = jnp.where(rows > j, c0 * r0, 0.0)
        m1 = jnp.where(rows > j + 1, (c1 - m0 * cross) * r1, 0.0)
        done = []
        for part in parts:
            first = part[j : j + 1]
            second = part[j + 1 : j + 2] - ratio * first
            done.append(part - m0 * first - m1 * second)
        parts = done
    diag = jnp.sum(jnp.where(eye > 0, parts[0], 0.0), 1, keepdims=True)
    scale = lax.rsqrt(diag)
    return (parts[0] * scale).T, parts[1] * scale


def pivot_kernel(rows_ref, low_ref, inv_ref):
    c0, i0 = factor_block(rows_ref[:BS, :BS])
    k10 = dot_nt(rows_ref[BS:, :BS], i0)
    c1, i1 = factor_block(rows_ref[BS:, BS:] - dot_nt(k10, k10))
    lane = lax.broadcasted_iota(jnp.int32, (BS, BS), 1)
    sub = lax.broadcasted_iota(jnp.int32, (BS, BS), 0)
    low = lane <= sub
    zero = jnp.zeros((BS, BS), jnp.float32)
    low_ref[:BS, :BS] = jnp.where(low, c0, 0.0)
    low_ref[:BS, BS:] = zero
    low_ref[BS:, :BS] = k10
    low_ref[BS:, BS:] = jnp.where(low, c1, 0.0)
    inv_ref[:BS, :BS] = i0
    inv_ref[:BS, BS:] = zero
    inv_ref[BS:, :BS] = -dot_nn(i1, dot_nn(k10, i0))
    inv_ref[BS:, BS:] = i1


def pivot_factor(pivot_rows):
    shape = jax.ShapeDtypeStruct((WIDE, WIDE), jnp.float32)
    whole = pl.BlockSpec(memory_space=pltpu.VMEM)
    return pl.pallas_call(
        pivot_kernel,
        out_shape=[shape, shape],
        in_specs=[whole],
        out_specs=[whole, whole],
        compiler_params=pltpu.CompilerParams(vmem_limit_bytes=VMEM_LIMIT),
        name="pivot_factor",
    )(pivot_rows)


ANY = pl.BlockSpec(memory_space=pl.ANY)


def parts_of(a):
    high = a.astype(jnp.bfloat16)
    return high, (a - high.astype(jnp.float32)).astype(jnp.bfloat16)


def split_left(a):
    high, low = parts_of(a)
    return jnp.concatenate([high, low, high], 1)


def split_right(a):
    high, low = parts_of(a)
    return jnp.concatenate([high, high, low], 0)


def dot_split(left, right):
    return jnp.dot(left, right, preferred_element_type=jnp.float32)


def update_kernel(cols, per, children, is_root, col_of, info_ref, *refs):
    front_ref, refs = refs[0], refs[1:]
    child_refs, refs = refs[: children * per], refs[children * per :]
    key_ref, panel_ref, inv_ref = refs[:3]
    out_ref, key_split, inv_split = refs[-3:]
    step = pl.program_id(0)

    @pl.when(step == 0)
    def _():
        key_split[...] = split_left(key_ref[...])
        inv_split[...] = split_left(inv_ref[...])

    panel = jnp.concatenate([panel_ref[t, 0, 0] for t in range(per)], 1)
    solved = dot_split(inv_split[...], split_right(panel))
    terms = dot_split(key_split[...], split_right(solved))
    width = ROWS + cols
    places = children * width
    for t in range(per):
        at = col_of(step, info_ref) * per + t
        lanes = slice(t * BS, (t + 1) * BS)
        for r in range(ROWS):
            span = slice(r * BS, (r + 1) * BS)
            block = front_ref[span, lanes] - terms[span, lanes]
            for which in range(children):
                source = info_ref[which * width + r]
                present = (source >= 0) & (info_ref[which * width + ROWS + at] >= 0)
                taken = child_refs[which * per + t][pl.ds(jnp.maximum(source, 0) * BS, BS), :]
                block = block + jnp.where(present, taken, 0.0)
            if is_root:
                keep = (info_ref[places + r] >= PIVOTS) & (info_ref[places + ROWS + at] >= PIVOTS)
                block = jnp.where(keep, block, 0.0)
            out_ref[span, lanes] = block


def update_front(front, children, key, panels, inverse, info, is_root=False, single=False, after=()):
    cols = front.shape[1] // BS
    width = ROWS + cols
    height = ROWS * BS
    per = 1 if single else 2
    rel_at = (len(children) + 1) * width
    if single:
        col_of = lambda c, info: info[rel_at]
    else:
        col_of = lambda c, info: c
    outer, inner = panels.shape[:2]
    run = outer // per

    def panel_at(c, info):
        at = col_of(c, info)
        if is_root:
            return (0, lax.div(at, 4), lax.rem(at, 4), 0, 0)
        return (lax.rem(at, run), lax.div(at, run), 0, 0, 0)

    column = pl.BlockSpec((height, per * BS), lambda c, info: (0, col_of(c, info)))
    specs, args = [column], [front]
    for which, child in enumerate(children):
        for t in range(per):
            specs.append(
                pl.BlockSpec(
                    (height, BS),
                    lambda c, info, which=which, t=t: (
                        0,
                        jnp.maximum(info[which * width + ROWS + col_of(c, info) * per + t], 0),
                    ),
                )
            )
            args.append(child)
    specs += [
        pl.BlockSpec((height, WIDE), lambda c, info: (0, 0)),
        pl.BlockSpec((per, 1, 1, WIDE, BS), panel_at),
        pl.BlockSpec((WIDE, WIDE), lambda c, info: (0, 0)),
    ] + [ANY] * len(after)
    args += [key, panels, inverse, *after]
    steps = 1 if single else cols // per
    return pl.pallas_call(
        functools.partial(update_kernel, cols, per, len(children), is_root, col_of),
        out_shape=jax.ShapeDtypeStruct((height, steps * per * BS), jnp.float32),
        grid_spec=pltpu.PrefetchScalarGridSpec(
            num_scalar_prefetch=1,
            grid=(steps,),
            in_specs=specs,
            out_specs=pl.BlockSpec((height, per * BS), lambda c, info: (0, c)),
            scratch_shapes=[
                pltpu.VMEM((height, 3 * WIDE), jnp.bfloat16),
                pltpu.VMEM((WIDE, 3 * WIDE), jnp.bfloat16),
            ],
        ),
        compiler_params=pltpu.CompilerParams(vmem_limit_bytes=VMEM_LIMIT),
        cost_estimate=pl.CostEstimate(
            flops=2 * height * WIDE * steps * per * BS * 2,
            bytes_accessed=16 * height * steps * per * BS,
            transcendentals=0,
        ),
        name="update_front",
    )(info, *args)


def panel_kernel(width, info_ref, front_ref, own_ref, other_ref, *refs):
    out_ref = refs[-1]
    for r in range(ROWS):
        block = front_ref[r * BS : (r + 1) * BS, :]
        for which, child_ref in ((0, own_ref), (1, other_ref)):
            source = info_ref[which * width + r]
            present = (source >= 0) & (info_ref[which * width + ROWS] >= 0)
            taken = child_ref[pl.ds(jnp.maximum(source, 0) * BS, BS), :]
            block = block + jnp.where(present, taken, 0.0)
        out_ref[r * BS : (r + 1) * BS, :] = block


def pivot_panel(front, own, other, info, after):
    piece = pl.BlockSpec((ROWS * BS, BS), lambda c, info: (0, 0))
    return pl.pallas_call(
        functools.partial(panel_kernel, ROWS + front.shape[1] // BS),
        out_shape=jax.ShapeDtypeStruct((ROWS * BS, BS), jnp.float32),
        grid_spec=pltpu.PrefetchScalarGridSpec(
            num_scalar_prefetch=1,
            grid=(1,),
            in_specs=[piece] * 3 + [ANY] * len(after),
            out_specs=piece,
        ),
        name="pivot_panel",
    )(info, front, own, other, *after)


def add_kernel(count, info_ref, front_ref, child_ref, out_ref):
    valid = info_ref[2 * ROWS + count + pl.program_id(0)] > 0
    for r in range(ROWS):
        span = slice(r * BS, (r + 1) * BS)
        source = info_ref[r]
        present = valid & (source >= 0) & (info_ref[ROWS + r] >= PIVOTS)
        taken = child_ref[pl.ds(jnp.maximum(source, 0) * BS, BS), :]
        out_ref[span, :] = front_ref[span, :] + jnp.where(present, taken, 0.0)


def add_columns(front, child, info):
    count = child.shape[1] // BS
    target = pl.BlockSpec((ROWS * BS, BS), lambda c, info: (0, info[2 * ROWS + c]))
    return pl.pallas_call(
        functools.partial(add_kernel, count),
        out_shape=jax.ShapeDtypeStruct(front.shape, jnp.float32),
        grid_spec=pltpu.PrefetchScalarGridSpec(
            num_scalar_prefetch=1,
            grid=(count,),
            in_specs=[target, pl.BlockSpec((ROWS * BS, BS), lambda c, info: (0, c))],
            out_specs=target,
        ),
        input_output_aliases={1: 0},
        compiler_params=pltpu.CompilerParams(vmem_limit_bytes=VMEM_LIMIT),
        name="add_columns",
    )(info, front, child)


def copy_kernel(in_ref, *refs):
    refs[-1][...] = in_ref[...]


def copy_after(array, after, low=0, high=None):
    rows, cols = array.shape
    high = cols if high is None else high
    wide = 2 * BS
    return pl.pallas_call(
        copy_kernel,
        out_shape=jax.ShapeDtypeStruct((rows, high - low), jnp.float32),
        grid=((high - low) // wide,),
        in_specs=[pl.BlockSpec((rows, wide), lambda c: (0, c + low // wide))] + [ANY] * len(after),
        out_specs=pl.BlockSpec((rows, wide), lambda c: (0, c)),
        name="copy_after",
    )(array, *after)


def spread_kernel(count, at_ref, *refs):
    pieces, out_ref, scratch = refs[:count], refs[-2], refs[-1]

    @pl.when(pl.program_id(0) == 0)
    def _():
        for step in range(count):
            turned = pieces[step][...].T
            for place in range(count):

                @pl.when(at_ref[0] == place ^ step)
                def _():
                    scratch[place] = turned

    out_ref[0] = scratch[...]


def spread(pieces, at, copies, after):
    count = len(pieces)
    shape = (count, WIDE, BS)
    return pl.pallas_call(
        functools.partial(spread_kernel, count),
        out_shape=jax.ShapeDtypeStruct((copies, *shape), jnp.float32),
        grid_spec=pltpu.PrefetchScalarGridSpec(
            num_scalar_prefetch=1,
            grid=(copies,),
            in_specs=[pl.BlockSpec((BS, WIDE), lambda c, at: (0, 0))] * count + [ANY] * len(after),
            out_specs=pl.BlockSpec((1, *shape), lambda c, at: (c, 0, 0, 0)),
            scratch_shapes=[pltpu.VMEM(shape, jnp.float32)],
        ),
        name="spread",
    )(at, *pieces, *after)


def send(block, route):
    pairs = [(a[0] * 4 + a[1], b[0] * 4 + b[1]) for a, b in route]
    return lax.ppermute(block, ("cube", "grid"), pairs)


def both_pivots(piece, cube_count, grid_at):
    got = []
    for step in (1, 2, 3):
        route = [((s, g), (s, g ^ step)) for s in range(cube_count) for g in (0, 1)]
        got.append(send(piece, route))
    near, far, cross = got
    first = jnp.where(grid_at == 0, piece, jnp.where(grid_at == 1, near, jnp.where(grid_at == 2, far, cross)))
    second = jnp.where(grid_at == 1, piece, jnp.where(grid_at == 0, near, jnp.where(grid_at == 3, far, cross)))
    return jnp.concatenate([first, second], -1)


def shifted(block, bit, sources, sub_size, cube_count, grids=None):
    route = []
    for base in range(0, cube_count, sub_size):
        for s in range(sub_size):
            for g in range(4):
                if sources(s, g):
                    route.append(((base + s, g), (base + (s ^ bit), g)))
    return send(block, route)


def class_rows(own_rows, sub_size, cube_count, cube_at, grid_at):
    quarter = cube_at % 4
    total = jnp.where(
        quarter == grid_at, lax.dynamic_index_in_dim(own_rows, quarter, 0, keepdims=False), 0.0
    )
    for step in (1, 2, 3):
        total = total + shifted(
            lax.dynamic_index_in_dim(own_rows, quarter ^ step, 0, keepdims=False),
            step,
            lambda s, g: s % 4 == g,
            sub_size,
            cube_count,
        )
    return total


def class_rows_direct(own_rows, cube_count, cube_at, grid_at):
    total = jnp.where(cube_at % 4 == grid_at, own_rows, 0.0)
    for step in (1, 2, 3):
        total = total + shifted(own_rows, step, lambda s, g: s == g, 4, cube_count)
    return total.transpose(0, 2, 1).reshape(ROWS, 1, 1, WIDE, BS)


def gathered(pieces, at, group, cube_count, after):
    groups = None
    if group < cube_count:
        groups = [[b + i for i in range(group)] for b in range(0, cube_count, group)]
    everything = lax.all_to_all(
        spread(pieces, at, group, after), "cube", 0, 0, axis_index_groups=groups
    )
    return everything.reshape(group // 4, 4, len(pieces), WIDE, BS)


def pivot_rows_everywhere(own_rows, sub_size, cube_count, slot, after):
    row = own_rows[0]
    got = shifted(row, 1, lambda s, g: s < 2, sub_size, cube_count)
    both = jnp.where(slot == 0, jnp.concatenate([row, got]), jnp.concatenate([got, row]))
    known = 2
    while known < sub_size:
        bits = (known,) if 4 * known > sub_size else (known, 2 * known, 3 * known)
        if after and known * (len(bits) + 1) == sub_size:
            both = copy_after(both, after)
        moved = [shifted(both, bit, lambda s, g: s < known, sub_size, cube_count) for bit in bits]
        both = jnp.where(slot < known, both, sum(moved[1:], moved[0]))
        known *= len(bits) + 1
    return both


def child_sources(table, child_size, cube_at, grid_at):
    parent_size = 2 * child_size
    slot = cube_at % parent_size
    front = cube_at // child_size
    maps = jnp.stack([table[front], table[front ^ 1]])
    rows = jnp.arange(ROWS) * parent_size + slot
    cols = jnp.arange(parent_size) * 4 + grid_at
    child_ids = jnp.arange(PIVOTS, ROWS * child_size)
    row_hit = maps[:, None, :] == rows[None, :, None]
    col_hit = maps[:, None, :] == cols[None, :, None]
    row_from = jnp.sum(jnp.where(row_hit, child_ids // child_size + 1, 0), 2) - 1
    col_from = jnp.sum(jnp.where(col_hit, child_ids // 4 + 1, 0), 2) - 1
    return jnp.concatenate([row_from, col_from], 1).astype(jnp.int32)


def column_targets(table, child_size, cube_at, grid_at, sources, count):
    mapping = table[(cube_at // child_size) ^ 1]
    child_ids = jnp.arange(count) * 4 + grid_at
    target = mapping[jnp.maximum(child_ids - PIVOTS, 0)]
    unused = jnp.argmax(sources[1, ROWS:] < 0)
    place = jnp.where(child_ids >= PIVOTS, target // 4, unused)
    valid = (child_ids >= PIVOTS) & (target >= PIVOTS)
    return place.astype(jnp.int32), valid.astype(jnp.int32)


def on_device(
    front_root, front_upper, front_middle, front_lower, place_upper, place_middle, place_lower
):
    cube_count = lax.axis_size("cube")
    cube_at = lax.axis_index("cube")
    grid_at = lax.axis_index("grid")
    stored = (front_root, front_upper, front_middle, front_lower)
    tables = (None, place_upper, place_middle, place_lower)
    factor_list = [None, None, None, None]
    own = other = rel = sources = None
    for depth in (3, 2, 1, 0):
        sub_size = cube_count >> depth
        half = sub_size // 2
        slot = cube_at % sub_size
        front = stored[depth]
        row_ids = jnp.arange(ROWS) * sub_size + slot
        col_ids = jnp.arange(sub_size) * 4 + grid_at
        info = jnp.concatenate([row_ids, col_ids]).astype(jnp.int32)
        children = ()
        if depth == 3:
            panel = front[:, :BS]
            arrived = ()
        else:
            got = shifted(rel, half, lambda s, g: g < 2, sub_size, cube_count)
            if depth > 0:
                sent = own
            else:
                sent = copy_after(own, (), 0, EARLY * BS)
            other = shifted(sent, half, lambda s, g: True, sub_size, cube_count)
            arrived = (other,)
            children = (own, other) if depth > 0 else (own,)
            moves = jnp.concatenate([sources.reshape(-1), info])
            panel = pivot_panel(front, rel, got, moves, (sent,))
            info = jnp.concatenate([sources[: len(children)].reshape(-1), info])
        if depth > 0:
            next_sources = child_sources(tables[depth], sub_size, cube_at, grid_at)
            info = jnp.concatenate([info, jnp.maximum(next_sources[0, ROWS : ROWS + 1], 0)])
        own_rows = both_pivots(panel, cube_count, grid_at)
        blocks = own_rows.reshape(ROWS, BS, WIDE)
        pivots = pivot_rows_everywhere(blocks, sub_size, cube_count, slot, arrived)
        low, inverse = pivot_factor(pivots)
        if depth == 3:
            panels = class_rows_direct(blocks, cube_count, cube_at, grid_at)
        else:
            share = class_rows(blocks, sub_size, cube_count, cube_at, grid_at)
            if depth > 0:
                zero = jnp.zeros((1,), jnp.int32)
                panels = gathered([share], zero, sub_size, cube_count, (pivots,))
            else:
                share = copy_after(share, arrived)
                pieces = [share] + [
                    shifted(share, bit, lambda s, g: True, sub_size, cube_count)
                    for bit in (8, 16, 24)
                ]
                plane = (cube_at // 8).astype(jnp.int32).reshape(1)
                panels = gathered(pieces, plane, 8, cube_count, (pivots,))
                panels = panels.reshape(2, 4, 4, WIDE, BS)
                late = copy_after(own, (pivots, *pieces[1:]), EARLY * BS)
                late = shifted(late, half, lambda s, g: True, sub_size, cube_count)
        solved = dot_nt(own_rows, inverse)
        pivot_slot = jnp.minimum(slot, PIVOTS - 1)
        head = jnp.where(
            slot < PIVOTS, lax.dynamic_slice_in_dim(low, pivot_slot * BS, BS, 0), solved[:BS]
        )
        solved = jnp.concatenate([head, solved[BS:]])
        factor_list[depth] = solved
        if depth > 0:
            rel = update_front(front, children, solved, panels, inverse, info, single=True)
            own = update_front(front, children, solved, panels, inverse, info, after=(rel,))
            sources = next_sources
        else:
            rest = update_front(front, children, solved, panels, inverse, info, is_root=True)
            count = own.shape[1] // BS
            place, valid = column_targets(tables[1], half, cube_at, grid_at, sources, count)
            row_part = jnp.concatenate([sources[1, :ROWS], row_ids]).astype(jnp.int32)
            for child, span in ((other, slice(0, EARLY)), (late, slice(EARLY, count))):
                rest = add_columns(
                    rest, child, jnp.concatenate([row_part, place[span], valid[span]])
                )
    return (factor_list[0], factor_list[1], factor_list[2], factor_list[3], rest)


def solution(mesh):
    return jax.shard_map(
        on_device,
        mesh=mesh,
        in_specs=(
            P("cube", "grid"),
            P("cube", "grid"),
            P("cube", "grid"),
            P("cube", "grid"),
            P(),
            P(),
            P(),
        ),
        out_specs=(
            P("cube", None),
            P("cube", None),
            P("cube", None),
            P("cube", None),
            P("cube", "grid"),
        ),
        check_vma=False,
    )
```

```python
import functools

import jax
import jax.numpy as jnp
from jax import lax
from jax.experimental import pallas as pl
from jax.experimental.pallas import tpu as pltpu
from jax.sharding import PartitionSpec as P

BS = 128
PIVOTS = 2
ROWS = 4
WIDE = PIVOTS * BS
HIGHEST = lax.Precision.HIGHEST
EARLY = 4
VMEM_LIMIT = 48 * 1024 * 1024


def dot_nn(a, b):
    return jnp.dot(a, b, precision=HIGHEST, preferred_element_type=jnp.float32)


def dot_nt(a, b):
    return lax.dot_general(
        a, b, (((1,), (1,)), ((), ())), precision=HIGHEST, preferred_element_type=jnp.float32
    )


def factor_block(block):
    n = BS
    rows = lax.broadcasted_iota(jnp.int32, (n, n), 0)
    eye = (rows == lax.broadcasted_iota(jnp.int32, (n, n), 1)).astype(jnp.float32)
    parts = [block, eye]
    for j in range(0, n, 2):
        c0 = jnp.broadcast_to(parts[0][:, j : j + 1], (n, n))
        c1 = jnp.broadcast_to(parts[0][:, j + 1 : j + 2], (n, n))
        d0, cross, d1 = c0[j : j + 1], c0[j + 1 : j + 2], c1[j + 1 : j + 2]
        r0 = 1.0 / d0
        ratio = cross * r0
        r1 = 1.0 / (d1 - ratio * cross)
        m0 = jnp.where(rows > j, c0 * r0, 0.0)
        m1 = jnp.where(rows > j + 1, (c1 - m0 * cross) * r1, 0.0)
        done = []
        for part in parts:
            first = part[j : j + 1]
            second = part[j + 1 : j + 2] - ratio * first
            done.append(part - m0 * first - m1 * second)
        parts = done
    diag = jnp.sum(jnp.where(eye > 0, parts[0], 0.0), 1, keepdims=True)
    scale = lax.rsqrt(diag)
    return (parts[0] * scale).T, parts[1] * scale


def pivot_kernel(rows_ref, low_ref, inv_ref):
    c0, i0 = factor_block(rows_ref[:BS, :BS])
    k10 = dot_nt(rows_ref[BS:, :BS], i0)
    c1, i1 = factor_block(rows_ref[BS:, BS:] - dot_nt(k10, k10))
    lane = lax.broadcasted_iota(jnp.int32, (BS, BS), 1)
    sub = lax.broadcasted_iota(jnp.int32, (BS, BS), 0)
    low = lane <= sub
    zero = jnp.zeros((BS, BS), jnp.float32)
    low_ref[:BS, :BS] = jnp.where(low, c0, 0.0)
    low_ref[:BS, BS:] = zero
    low_ref[BS:, :BS] = k10
    low_ref[BS:, BS:] = jnp.where(low, c1, 0.0)
    inv_ref[:BS, :BS] = i0
    inv_ref[:BS, BS:] = zero
    inv_ref[BS:, :BS] = -dot_nn(i1, dot_nn(k10, i0))
    inv_ref[BS:, BS:] = i1


def pivot_factor(pivot_rows):
    shape = jax.ShapeDtypeStruct((WIDE, WIDE), jnp.float32)
    whole = pl.BlockSpec(memory_space=pltpu.VMEM)
    return pl.pallas_call(
        pivot_kernel,
        out_shape=[shape, shape],
        in_specs=[whole],
        out_specs=[whole, whole],
        compiler_params=pltpu.CompilerParams(vmem_limit_bytes=VMEM_LIMIT),
        name="pivot_factor",
    )(pivot_rows)


ANY = pl.BlockSpec(memory_space=pl.ANY)


def parts_of(a):
    high = a.astype(jnp.bfloat16)
    return high, (a - high.astype(jnp.float32)).astype(jnp.bfloat16)


def split_left(a):
    high, low = parts_of(a)
    return jnp.concatenate([high, low, high], 1)


def split_right(a):
    high, low = parts_of(a)
    return jnp.concatenate([high, high, low], 0)


def dot_split(left, right):
    return jnp.dot(left, right, preferred_element_type=jnp.float32)


def update_kernel(cols, per, children, is_root, col_of, place_of, info_ref, *refs):
    front_ref, refs = refs[0], refs[1:]
    child_refs, refs = refs[: children * per], refs[children * per :]
    key_ref, panel_ref, inv_ref = refs[:3]
    out_ref, key_split, inv_split = refs[-3:]
    step = pl.program_id(0)

    @pl.when(step == 0)
    def _():
        key_split[...] = split_left(key_ref[...])
        inv_split[...] = split_left(inv_ref[...])

    panel = jnp.concatenate([panel_ref[place_of(t)] for t in range(per)], 1)
    solved = dot_split(inv_split[...], split_right(panel))
    terms = dot_split(key_split[...], split_right(solved))
    width = ROWS + cols
    places = children * width
    for t in range(per):
        at = col_of(step, info_ref) * per + t
        lanes = slice(t * BS, (t + 1) * BS)
        for r in range(ROWS):
            span = slice(r * BS, (r + 1) * BS)
            block = front_ref[span, lanes] - terms[span, lanes]
            for which in range(children):
                source = info_ref[which * width + r]
                present = (source >= 0) & (info_ref[which * width + ROWS + at] >= 0)
                taken = child_refs[which * per + t][pl.ds(jnp.maximum(source, 0) * BS, BS), :]
                block = block + jnp.where(present, taken, 0.0)
            if is_root:
                keep = (info_ref[places + r] >= PIVOTS) & (info_ref[places + ROWS + at] >= PIVOTS)
                block = jnp.where(keep, block, 0.0)
            out_ref[span, lanes] = block


def update_front(front, children, key, panels, inverse, info, is_root=False, single=False, after=()):
    cols = front.shape[1] // BS
    width = ROWS + cols
    height = ROWS * BS
    per = 1 if single else 4
    rel_at = (len(children) + 1) * width
    if single:
        col_of = lambda c, info: info[rel_at]
    else:
        col_of = lambda c, info: c
    outer, _, planes = panels.shape[:3]
    place_of = lambda t: (t % outer, t // outer, 0)
    if single:
        panel_dims = (1, 1, 1)
        panel_at = lambda c, info: (lax.rem(col_of(c, info), outer), lax.div(col_of(c, info), outer), 0, 0, 0)
    elif planes == 1:
        panel_dims = (outer, per // outer, 1)
        panel_at = lambda c, info: (0, c, 0, 0, 0)
    else:
        panel_dims = (outer, 1, per // outer)
        runs = planes * outer // per
        panel_at = lambda c, info: (0, lax.div(c, runs), lax.rem(c, runs), 0, 0)
        place_of = lambda t: (t % outer, 0, t // outer)

    column = pl.BlockSpec((height, per * BS), lambda c, info: (0, col_of(c, info)))
    specs, args = [column], [front]
    for which, child in enumerate(children):
        for t in range(per):
            specs.append(
                pl.BlockSpec(
                    (height, BS),
                    lambda c, info, which=which, t=t: (
                        0,
                        jnp.maximum(info[which * width + ROWS + col_of(c, info) * per + t], 0),
                    ),
                )
            )
            args.append(child)
    specs += [
        pl.BlockSpec((height, WIDE), lambda c, info: (0, 0)),
        pl.BlockSpec((*panel_dims, WIDE, BS), panel_at),
        pl.BlockSpec((WIDE, WIDE), lambda c, info: (0, 0)),
    ] + [ANY] * len(after)
    args += [key, panels, inverse, *after]
    steps = 1 if single else cols // per
    return pl.pallas_call(
        functools.partial(update_kernel, cols, per, len(children), is_root, col_of, place_of),
        out_shape=jax.ShapeDtypeStruct((height, steps * per * BS), jnp.float32),
        grid_spec=pltpu.PrefetchScalarGridSpec(
            num_scalar_prefetch=1,
            grid=(steps,),
            in_specs=specs,
            out_specs=pl.BlockSpec((height, per * BS), lambda c, info: (0, c)),
            scratch_shapes=[
                pltpu.VMEM((height, 3 * WIDE), jnp.bfloat16),
                pltpu.VMEM((WIDE, 3 * WIDE), jnp.bfloat16),
            ],
        ),
        compiler_params=pltpu.CompilerParams(vmem_limit_bytes=VMEM_LIMIT),
        cost_estimate=pl.CostEstimate(
            flops=2 * height * WIDE * steps * per * BS * 2,
            bytes_accessed=16 * height * steps * per * BS,
            transcendentals=0,
        ),
        name="update_front",
    )(info, *args)


def panel_kernel(width, info_ref, front_ref, own_ref, other_ref, *refs):
    out_ref = refs[-1]
    for r in range(ROWS):
        block = front_ref[r * BS : (r + 1) * BS, :]
        for which, child_ref in ((0, own_ref), (1, other_ref)):
            source = info_ref[which * width + r]
            present = (source >= 0) & (info_ref[which * width + ROWS] >= 0)
            taken = child_ref[pl.ds(jnp.maximum(source, 0) * BS, BS), :]
            block = block + jnp.where(present, taken, 0.0)
        out_ref[r * BS : (r + 1) * BS, :] = block


def pivot_panel(front, own, other, info, after):
    piece = pl.BlockSpec((ROWS * BS, BS), lambda c, info: (0, 0))
    return pl.pallas_call(
        functools.partial(panel_kernel, ROWS + front.shape[1] // BS),
        out_shape=jax.ShapeDtypeStruct((ROWS * BS, BS), jnp.float32),
        grid_spec=pltpu.PrefetchScalarGridSpec(
            num_scalar_prefetch=1,
            grid=(1,),
            in_specs=[piece] * 3 + [ANY] * len(after),
            out_specs=piece,
        ),
        name="pivot_panel",
    )(info, front, own, other, *after)


def add_kernel(count, info_ref, front_ref, child_ref, out_ref):
    valid = info_ref[2 * ROWS + count + pl.program_id(0)] > 0
    for r in range(ROWS):
        span = slice(r * BS, (r + 1) * BS)
        source = info_ref[r]
        present = valid & (source >= 0) & (info_ref[ROWS + r] >= PIVOTS)
        taken = child_ref[pl.ds(jnp.maximum(source, 0) * BS, BS), :]
        out_ref[span, :] = front_ref[span, :] + jnp.where(present, taken, 0.0)


def add_columns(front, child, info):
    count = child.shape[1] // BS
    target = pl.BlockSpec((ROWS * BS, BS), lambda c, info: (0, info[2 * ROWS + c]))
    return pl.pallas_call(
        functools.partial(add_kernel, count),
        out_shape=jax.ShapeDtypeStruct(front.shape, jnp.float32),
        grid_spec=pltpu.PrefetchScalarGridSpec(
            num_scalar_prefetch=1,
            grid=(count,),
            in_specs=[target, pl.BlockSpec((ROWS * BS, BS), lambda c, info: (0, c))],
            out_specs=target,
        ),
        input_output_aliases={1: 0},
        compiler_params=pltpu.CompilerParams(vmem_limit_bytes=VMEM_LIMIT),
        name="add_columns",
    )(info, front, child)


def copy_kernel(in_ref, *refs):
    refs[-1][...] = in_ref[...]


def copy_after(array, after, low=0, high=None):
    rows, cols = array.shape
    high = cols if high is None else high
    wide = 2 * BS
    return pl.pallas_call(
        copy_kernel,
        out_shape=jax.ShapeDtypeStruct((rows, high - low), jnp.float32),
        grid=((high - low) // wide,),
        in_specs=[pl.BlockSpec((rows, wide), lambda c: (0, c + low // wide))] + [ANY] * len(after),
        out_specs=pl.BlockSpec((rows, wide), lambda c: (0, c)),
        name="copy_after",
    )(array, *after)


def spread_kernel(count, at_ref, *refs):
    pieces, out_ref, scratch = refs[:count], refs[-2], refs[-1]

    @pl.when(pl.program_id(0) == 0)
    def _():
        for step in range(count):
            turned = pieces[step][...].T
            for place in range(count):

                @pl.when(at_ref[0] == place ^ step)
                def _():
                    scratch[place] = turned

    out_ref[0] = scratch[...]


def spread(pieces, at, copies, after):
    count = len(pieces)
    shape = (count, WIDE, BS)
    return pl.pallas_call(
        functools.partial(spread_kernel, count),
        out_shape=jax.ShapeDtypeStruct((copies, *shape), jnp.float32),
        grid_spec=pltpu.PrefetchScalarGridSpec(
            num_scalar_prefetch=1,
            grid=(copies,),
            in_specs=[pl.BlockSpec((BS, WIDE), lambda c, at: (0, 0))] * count + [ANY] * len(after),
            out_specs=pl.BlockSpec((1, *shape), lambda c, at: (c, 0, 0, 0)),
            scratch_shapes=[pltpu.VMEM(shape, jnp.float32)],
        ),
        name="spread",
    )(at, *pieces, *after)


def send(block, route):
    pairs = [(a[0] * 4 + a[1], b[0] * 4 + b[1]) for a, b in route]
    return lax.ppermute(block, ("cube", "grid"), pairs)


def both_pivots(piece, cube_count, grid_at):
    got = []
    for step in (1, 2, 3):
        route = [((s, g), (s, g ^ step)) for s in range(cube_count) for g in (0, 1)]
        got.append(send(piece, route))
    near, far, cross = got
    first = jnp.where(grid_at == 0, piece, jnp.where(grid_at == 1, near, jnp.where(grid_at == 2, far, cross)))
    second = jnp.where(grid_at == 1, piece, jnp.where(grid_at == 0, near, jnp.where(grid_at == 3, far, cross)))
    return jnp.concatenate([first, second], -1)


def shifted(block, bit, sources, sub_size, cube_count, grids=None):
    route = []
    for base in range(0, cube_count, sub_size):
        for s in range(sub_size):
            for g in range(4):
                if sources(s, g):
                    route.append(((base + s, g), (base + (s ^ bit), g)))
    return send(block, route)


def class_rows(panel, cube_count, cube_at, grid_at):
    blocks = panel.reshape(ROWS, BS, BS)
    got = []
    for turn in range(4):
        route = []
        for s in range(cube_count):
            for p in (0, 1):
                route.append(((s, p), (s - s % 4 + (turn ^ p), s % 4)))
        row = lax.dynamic_index_in_dim(blocks, (turn ^ grid_at) & 3, 0, keepdims=False)
        got.append(send(row, route))
    even, odd = got[0] + got[2], got[1] + got[3]
    return jnp.where(
        cube_at % 2 == 0, jnp.concatenate([even, odd], 1), jnp.concatenate([odd, even], 1)
    )


def class_rows_direct(own_rows, cube_count, cube_at, grid_at):
    total = jnp.where(cube_at % 4 == grid_at, own_rows, 0.0)
    for step in (1, 2, 3):
        total = total + shifted(own_rows, step, lambda s, g: s == g, 4, cube_count)
    return total.transpose(0, 2, 1).reshape(ROWS, 1, 1, WIDE, BS)


def gathered(pieces, at, group, cube_count, after):
    groups = None
    if group < cube_count:
        groups = [[b + i for i in range(group)] for b in range(0, cube_count, group)]
    everything = lax.all_to_all(
        spread(pieces, at, group, after), "cube", 0, 0, axis_index_groups=groups
    )
    return everything.reshape(group // 4, 4, len(pieces), WIDE, BS)


def pivot_rows_everywhere(own_rows, sub_size, cube_count, slot, after):
    row = own_rows[0]
    got = shifted(row, 1, lambda s, g: s < 2, sub_size, cube_count)
    both = jnp.where(slot == 0, jnp.concatenate([row, got]), jnp.concatenate([got, row]))
    known = 2
    while known < sub_size:
        bits = (known,) if 4 * known > sub_size else (known, 2 * known, 3 * known)
        before = both
        if after and known * (len(bits) + 1) == sub_size:
            both = copy_after(both, after)
        moved = [shifted(both, bit, lambda s, g: s < known, sub_size, cube_count) for bit in bits]
        both = jnp.where(slot < known, both, sum(moved[1:], moved[0]))
        known *= len(bits) + 1
    return both, before


def child_sources(table, child_size, cube_at, grid_at):
    parent_size = 2 * child_size
    slot = cube_at % parent_size
    front = cube_at // child_size
    maps = jnp.stack([table[front], table[front ^ 1]])
    rows = jnp.arange(ROWS) * parent_size + slot
    cols = jnp.arange(parent_size) * 4 + grid_at
    child_ids = jnp.arange(PIVOTS, ROWS * child_size)
    row_hit = maps[:, None, :] == rows[None, :, None]
    col_hit = maps[:, None, :] == cols[None, :, None]
    row_from = jnp.sum(jnp.where(row_hit, child_ids // child_size + 1, 0), 2) - 1
    col_from = jnp.sum(jnp.where(col_hit, child_ids // 4 + 1, 0), 2) - 1
    return jnp.concatenate([row_from, col_from], 1).astype(jnp.int32)


def column_targets(table, child_size, cube_at, grid_at, sources, count):
    mapping = table[(cube_at // child_size) ^ 1]
    child_ids = jnp.arange(count) * 4 + grid_at
    target = mapping[jnp.maximum(child_ids - PIVOTS, 0)]
    unused = jnp.argmax(sources[1, ROWS:] < 0)
    place = jnp.where(child_ids >= PIVOTS, target // 4, unused)
    valid = (child_ids >= PIVOTS) & (target >= PIVOTS)
    return place.astype(jnp.int32), valid.astype(jnp.int32)


def on_device(
    front_root, front_upper, front_middle, front_lower, place_upper, place_middle, place_lower
):
    cube_count = lax.axis_size("cube")
    cube_at = lax.axis_index("cube")
    grid_at = lax.axis_index("grid")
    stored = (front_root, front_upper, front_middle, front_lower)
    tables = (None, place_upper, place_middle, place_lower)
    factor_list = [None, None, None, None]
    own = other = rel = sources = None
    for depth in (3, 2, 1, 0):
        sub_size = cube_count >> depth
        half = sub_size // 2
        slot = cube_at % sub_size
        front = stored[depth]
        row_ids = jnp.arange(ROWS) * sub_size + slot
        col_ids = jnp.arange(sub_size) * 4 + grid_at
        info = jnp.concatenate([row_ids, col_ids]).astype(jnp.int32)
        arrived = ()
        if depth == 3:
            panel = front[:, :BS]
        else:
            got = shifted(rel, half, lambda s, g: g < 2, sub_size, cube_count)
            moves = jnp.concatenate([sources.reshape(-1), info])
            panel = pivot_panel(front, rel, got, moves, (own,))
            if depth < 2:
                sent = copy_after(own, (got,), 0, None if depth else EARLY * BS)
                other = shifted(sent, half, lambda s, g: True, sub_size, cube_count)
                arrived = (other,)
            if depth == 0:
                early = jnp.where(sources[1, ROWS:] < EARLY, sources[1, ROWS:], -1)
                sources_now = jnp.stack([sources[0], jnp.concatenate([sources[1, :ROWS], early])])
                info = jnp.concatenate([sources_now.reshape(-1), info])
            else:
                info = moves
        if depth > 0:
            next_sources = child_sources(tables[depth], sub_size, cube_at, grid_at)
            info = jnp.concatenate([info, jnp.maximum(next_sources[0, ROWS : ROWS + 1], 0)])
        own_rows = both_pivots(panel, cube_count, grid_at)
        blocks = own_rows.reshape(ROWS, BS, WIDE)
        pivots, nearly = pivot_rows_everywhere(blocks, sub_size, cube_count, slot, arrived)
        low, inverse = pivot_factor(pivots)
        if depth == 3:
            panels = class_rows_direct(blocks, cube_count, cube_at, grid_at)
        else:
            share = class_rows(panel, cube_count, cube_at, grid_at)
            if depth > 0:
                zero = jnp.zeros((1,), jnp.int32)
                panels = gathered([share], zero, sub_size, cube_count, (pivots,))
            else:
                share = copy_after(share, arrived)
                pieces = [share] + [
                    shifted(share, bit, lambda s, g: True, sub_size, cube_count)
                    for bit in (8, 16, 24)
                ]
                plane = (cube_at // 8).astype(jnp.int32).reshape(1)
                panels = gathered(pieces, plane, 8, cube_count, (nearly,))
                late = copy_after(own, (pivots, *pieces[1:]), EARLY * BS)
                late = shifted(late, half, lambda s, g: True, sub_size, cube_count)
        if depth == 2:
            sent = copy_after(own, (pivots,))
            other = shifted(sent, half, lambda s, g: True, sub_size, cube_count)
        children = () if depth == 3 else (own, other)
        solved = dot_nt(own_rows, inverse)
        pivot_slot = jnp.minimum(slot, PIVOTS - 1)
        head = jnp.where(
            slot < PIVOTS, lax.dynamic_slice_in_dim(low, pivot_slot * BS, BS, 0), solved[:BS]
        )
        solved = jnp.concatenate([head, solved[BS:]])
        factor_list[depth] = solved
        if depth > 0:
            rel = update_front(front, children, solved, panels, inverse, info, single=True)
            own = update_front(front, children, solved, panels, inverse, info, after=(rel,))
            sources = next_sources
        else:
            rest = update_front(front, children, solved, panels, inverse, info, is_root=True)
            count = own.shape[1] // BS
            place, valid = column_targets(tables[1], half, cube_at, grid_at, sources, count)
            row_part = jnp.concatenate([sources[1, :ROWS], row_ids]).astype(jnp.int32)
            rest = add_columns(
                rest, late, jnp.concatenate([row_part, place[EARLY:], valid[EARLY:]])
            )
    return (factor_list[0], factor_list[1], factor_list[2], factor_list[3], rest)


def solution(mesh):
    return jax.shard_map(
        on_device,
        mesh=mesh,
        in_specs=(
            P("cube", "grid"),
            P("cube", "grid"),
            P("cube", "grid"),
            P("cube", "grid"),
            P(),
            P(),
            P(),
        ),
        out_specs=(
            P("cube", None),
            P("cube", None),
            P("cube", None),
            P("cube", None),
            P("cube", "grid"),
        ),
        check_vma=False,
    )
```

```python
import functools

import jax
import jax.numpy as jnp
from jax import lax
from jax.experimental import pallas as pl
from jax.experimental.pallas import tpu as pltpu
from jax.sharding import PartitionSpec as P

BS = 128
PIVOTS = 2
ROWS = 4
WIDE = PIVOTS * BS
HIGHEST = lax.Precision.HIGHEST
EARLY = 4
VMEM_LIMIT = 48 * 1024 * 1024


def dot_nn(a, b):
    return jnp.dot(a, b, precision=HIGHEST, preferred_element_type=jnp.float32)


def dot_nt(a, b):
    return lax.dot_general(
        a, b, (((1,), (1,)), ((), ())), precision=HIGHEST, preferred_element_type=jnp.float32
    )


def factor_block(block):
    n = BS
    rows = lax.broadcasted_iota(jnp.int32, (n, n), 0)
    eye = (rows == lax.broadcasted_iota(jnp.int32, (n, n), 1)).astype(jnp.float32)
    parts = [block, eye]
    for j in range(0, n, 2):
        c0 = jnp.broadcast_to(parts[0][:, j : j + 1], (n, n))
        c1 = jnp.broadcast_to(parts[0][:, j + 1 : j + 2], (n, n))
        d0, cross, d1 = c0[j : j + 1], c0[j + 1 : j + 2], c1[j + 1 : j + 2]
        r0 = 1.0 / d0
        ratio = cross * r0
        r1 = 1.0 / (d1 - ratio * cross)
        m0 = jnp.where(rows > j, c0 * r0, 0.0)
        m1 = jnp.where(rows > j + 1, (c1 - m0 * cross) * r1, 0.0)
        done = []
        for part in parts:
            first = part[j : j + 1]
            second = part[j + 1 : j + 2] - ratio * first
            done.append(part - m0 * first - m1 * second)
        parts = done
    diag = jnp.sum(jnp.where(eye > 0, parts[0], 0.0), 1, keepdims=True)
    scale = lax.rsqrt(diag)
    return (parts[0] * scale).T, parts[1] * scale


def pivot_kernel(rows_ref, low_ref, inv_ref):
    c0, i0 = factor_block(rows_ref[:BS, :BS])
    k10 = dot_nt(rows_ref[BS:, :BS], i0)
    c1, i1 = factor_block(rows_ref[BS:, BS:] - dot_nt(k10, k10))
    lane = lax.broadcasted_iota(jnp.int32, (BS, BS), 1)
    sub = lax.broadcasted_iota(jnp.int32, (BS, BS), 0)
    low = lane <= sub
    zero = jnp.zeros((BS, BS), jnp.float32)
    low_ref[:BS, :BS] = jnp.where(low, c0, 0.0)
    low_ref[:BS, BS:] = zero
    low_ref[BS:, :BS] = k10
    low_ref[BS:, BS:] = jnp.where(low, c1, 0.0)
    inv_ref[:BS, :BS] = i0
    inv_ref[:BS, BS:] = zero
    inv_ref[BS:, :BS] = -dot_nn(i1, dot_nn(k10, i0))
    inv_ref[BS:, BS:] = i1


def pivot_factor(pivot_rows):
    shape = jax.ShapeDtypeStruct((WIDE, WIDE), jnp.float32)
    whole = pl.BlockSpec(memory_space=pltpu.VMEM)
    return pl.pallas_call(
        pivot_kernel,
        out_shape=[shape, shape],
        in_specs=[whole],
        out_specs=[whole, whole],
        compiler_params=pltpu.CompilerParams(vmem_limit_bytes=VMEM_LIMIT),
        name="pivot_factor",
    )(pivot_rows)


ANY = pl.BlockSpec(memory_space=pl.ANY)


def parts_of(a):
    high = a.astype(jnp.bfloat16)
    return high, (a - high.astype(jnp.float32)).astype(jnp.bfloat16)


def split_left(a):
    high, low = parts_of(a)
    return jnp.concatenate([high, low, high], 1)


def split_right(a):
    high, low = parts_of(a)
    return jnp.concatenate([high, high, low], 0)


def dot_split(left, right):
    return jnp.dot(left, right, preferred_element_type=jnp.float32)


def update_kernel(cols, per, children, is_root, col_of, place_of, info_ref, *refs):
    front_ref, refs = refs[0], refs[1:]
    child_refs, refs = refs[: children * per], refs[children * per :]
    key_ref, panel_ref, inv_ref = refs[:3]
    out_ref, key_split, inv_split = refs[-3:]
    step = pl.program_id(0)

    @pl.when(step == 0)
    def _():
        key_split[...] = split_left(key_ref[...])
        inv_split[...] = split_left(inv_ref[...])

    panel = jnp.concatenate([panel_ref[place_of(t)] for t in range(per)], 1)
    solved = dot_split(inv_split[...], split_right(panel))
    terms = dot_split(key_split[...], split_right(solved))
    width = ROWS + cols
    places = children * width
    for t in range(per):
        at = col_of(step, info_ref) * per + t
        lanes = slice(t * BS, (t + 1) * BS)
        for r in range(ROWS):
            span = slice(r * BS, (r + 1) * BS)
            block = front_ref[span, lanes] - terms[span, lanes]
            for which in range(children):
                source = info_ref[which * width + r]
                present = (source >= 0) & (info_ref[which * width + ROWS + at] >= 0)
                taken = child_refs[which * per + t][pl.ds(jnp.maximum(source, 0) * BS, BS), :]
                block = block + jnp.where(present, taken, 0.0)
            if is_root:
                keep = (info_ref[places + r] >= PIVOTS) & (info_ref[places + ROWS + at] >= PIVOTS)
                block = jnp.where(keep, block, 0.0)
            out_ref[span, lanes] = block


def update_front(front, children, key, panels, inverse, info, is_root=False, single=False, span=None, after=()):
    cols = front.shape[1] // BS
    width = ROWS + cols
    height = ROWS * BS
    per = 1 if single else 4
    rel_at = (len(children) + 1) * width
    first, steps = (0, 1) if single else span or (0, cols // per)
    if single:
        col_of = lambda c, info: info[rel_at]
    else:
        col_of = lambda c, info: c + first
    outer, _, planes = panels.shape[:3]
    place_of = lambda t: (t % outer, t // outer, 0)
    if single:
        panel_dims = (1, 1, 1)
        panel_at = lambda c, info: (lax.rem(col_of(c, info), outer), lax.div(col_of(c, info), outer), 0, 0, 0)
    elif planes == 1:
        panel_dims = (outer, per // outer, 1)
        panel_at = lambda c, info: (0, c + first, 0, 0, 0)
    else:
        panel_dims = (outer, 1, per // outer)
        runs = planes * outer // per
        panel_at = lambda c, info: (0, lax.div(c, runs), lax.rem(c, runs), 0, 0)
        place_of = lambda t: (t % outer, 0, t // outer)

    column = pl.BlockSpec((height, per * BS), lambda c, info: (0, col_of(c, info)))
    specs, args = [column], [front]
    for which, child in enumerate(children):
        for t in range(per):
            specs.append(
                pl.BlockSpec(
                    (height, BS),
                    lambda c, info, which=which, t=t: (
                        0,
                        jnp.maximum(info[which * width + ROWS + col_of(c, info) * per + t], 0),
                    ),
                )
            )
            args.append(child)
    specs += [
        pl.BlockSpec((height, WIDE), lambda c, info: (0, 0)),
        pl.BlockSpec((*panel_dims, WIDE, BS), panel_at),
        pl.BlockSpec((WIDE, WIDE), lambda c, info: (0, 0)),
    ] + [ANY] * len(after)
    args += [key, panels, inverse, *after]
    return pl.pallas_call(
        functools.partial(update_kernel, cols, per, len(children), is_root, col_of, place_of),
        out_shape=jax.ShapeDtypeStruct((height, steps * per * BS), jnp.float32),
        grid_spec=pltpu.PrefetchScalarGridSpec(
            num_scalar_prefetch=1,
            grid=(steps,),
            in_specs=specs,
            out_specs=pl.BlockSpec((height, per * BS), lambda c, info: (0, c)),
            scratch_shapes=[
                pltpu.VMEM((height, 3 * WIDE), jnp.bfloat16),
                pltpu.VMEM((WIDE, 3 * WIDE), jnp.bfloat16),
            ],
        ),
        compiler_params=pltpu.CompilerParams(vmem_limit_bytes=VMEM_LIMIT),
        cost_estimate=pl.CostEstimate(
            flops=2 * height * WIDE * steps * per * BS * 2,
            bytes_accessed=16 * height * steps * per * BS,
            transcendentals=0,
        ),
        name="update_front",
    )(info, *args)


def panel_kernel(width, info_ref, front_ref, own_ref, other_ref, *refs):
    out_ref = refs[-1]
    for r in range(ROWS):
        block = front_ref[r * BS : (r + 1) * BS, :]
        for which, child_ref in ((0, own_ref), (1, other_ref)):
            source = info_ref[which * width + r]
            present = (source >= 0) & (info_ref[which * width + ROWS] >= 0)
            taken = child_ref[pl.ds(jnp.maximum(source, 0) * BS, BS), :]
            block = block + jnp.where(present, taken, 0.0)
        out_ref[r * BS : (r + 1) * BS, :] = block


def pivot_panel(front, own, other, info, after):
    piece = pl.BlockSpec((ROWS * BS, BS), lambda c, info: (0, 0))
    return pl.pallas_call(
        functools.partial(panel_kernel, ROWS + front.shape[1] // BS),
        out_shape=jax.ShapeDtypeStruct((ROWS * BS, BS), jnp.float32),
        grid_spec=pltpu.PrefetchScalarGridSpec(
            num_scalar_prefetch=1,
            grid=(1,),
            in_specs=[piece] * 3 + [ANY] * len(after),
            out_specs=piece,
        ),
        name="pivot_panel",
    )(info, front, own, other, *after)


def add_kernel(count, info_ref, front_ref, child_ref, out_ref):
    valid = info_ref[2 * ROWS + count + pl.program_id(0)] > 0
    for r in range(ROWS):
        span = slice(r * BS, (r + 1) * BS)
        source = info_ref[r]
        present = valid & (source >= 0) & (info_ref[ROWS + r] >= PIVOTS)
        taken = child_ref[pl.ds(jnp.maximum(source, 0) * BS, BS), :]
        out_ref[span, :] = front_ref[span, :] + jnp.where(present, taken, 0.0)


def add_columns(front, child, info):
    count = child.shape[1] // BS
    target = pl.BlockSpec((ROWS * BS, BS), lambda c, info: (0, info[2 * ROWS + c]))
    return pl.pallas_call(
        functools.partial(add_kernel, count),
        out_shape=jax.ShapeDtypeStruct(front.shape, jnp.float32),
        grid_spec=pltpu.PrefetchScalarGridSpec(
            num_scalar_prefetch=1,
            grid=(count,),
            in_specs=[target, pl.BlockSpec((ROWS * BS, BS), lambda c, info: (0, c))],
            out_specs=target,
        ),
        input_output_aliases={1: 0},
        compiler_params=pltpu.CompilerParams(vmem_limit_bytes=VMEM_LIMIT),
        name="add_columns",
    )(info, front, child)


def copy_kernel(in_ref, *refs):
    refs[-1][...] = in_ref[...]


def copy_after(array, after, low=0, high=None):
    rows, cols = array.shape
    high = cols if high is None else high
    wide = WIDE
    return pl.pallas_call(
        copy_kernel,
        out_shape=jax.ShapeDtypeStruct((rows, high - low), jnp.float32),
        grid=((high - low) // wide,),
        in_specs=[pl.BlockSpec((rows, wide), lambda c: (0, c + low // wide))] + [ANY] * len(after),
        out_specs=pl.BlockSpec((rows, wide), lambda c: (0, c)),
        name="copy_after",
    )(array, *after)


def spread_kernel(count, at_ref, *refs):
    pieces, out_ref, scratch = refs[:count], refs[-2], refs[-1]

    @pl.when(pl.program_id(0) == 0)
    def _():
        for step in range(count):
            turned = pieces[step][...].T
            for place in range(count):

                @pl.when(at_ref[0] == place ^ step)
                def _():
                    scratch[place] = turned

    for t in range(out_ref.shape[0]):
        out_ref[t] = scratch[...]


def spread(pieces, at, copies, after):
    count = len(pieces)
    shape = (count, WIDE, BS)
    each = 4 if count == 1 else 2
    return pl.pallas_call(
        functools.partial(spread_kernel, count),
        out_shape=jax.ShapeDtypeStruct((copies, *shape), jnp.float32),
        grid_spec=pltpu.PrefetchScalarGridSpec(
            num_scalar_prefetch=1,
            grid=(copies // each,),
            in_specs=[pl.BlockSpec((BS, WIDE), lambda c, at: (0, 0))] * count + [ANY] * len(after),
            out_specs=pl.BlockSpec((each, *shape), lambda c, at: (c, 0, 0, 0)),
            scratch_shapes=[pltpu.VMEM(shape, jnp.float32)],
        ),
        compiler_params=pltpu.CompilerParams(vmem_limit_bytes=VMEM_LIMIT),
        name="spread",
    )(at, *pieces, *after)


def send(block, route):
    pairs = [(a[0] * 4 + a[1], b[0] * 4 + b[1]) for a, b in route]
    return lax.ppermute(block, ("cube", "grid"), pairs)


def both_pivots(piece, cube_count, grid_at):
    near = send(piece, [((s, g), (s, g ^ 1)) for s in range(cube_count) for g in (0, 1)])
    far = send(piece, [((s, g), (s, g ^ 2)) for s in range(cube_count) for g in (0, 1)])
    cross = send(far, [((s, g), (s, g ^ 1)) for s in range(cube_count) for g in (2, 3)])
    mine = jnp.where(grid_at < 2, piece, far)
    mate = jnp.where(grid_at < 2, near, cross)
    first = jnp.where(grid_at % 2 == 0, mine, mate)
    second = jnp.where(grid_at % 2 == 0, mate, mine)
    return jnp.concatenate([first, second], -1)


def shifted(block, bit, sources, sub_size, cube_count, grids=None):
    route = []
    for base in range(0, cube_count, sub_size):
        for s in range(sub_size):
            for g in range(4):
                if sources(s, g):
                    route.append(((base + s, g), (base + (s ^ bit), g)))
    return send(block, route)


def class_rows(panel, cube_count, cube_at, grid_at):
    blocks = panel.reshape(ROWS, BS, BS)
    got = []
    for turn in range(4):
        route = []
        for s in range(cube_count):
            for p in (0, 1):
                route.append(((s, p), (s - s % 4 + (turn ^ p), s % 4)))
        row = lax.dynamic_index_in_dim(blocks, (turn ^ grid_at) & 3, 0, keepdims=False)
        got.append(send(row, route))
    even, odd = got[0] + got[2], got[1] + got[3]
    return jnp.where(
        cube_at % 2 == 0, jnp.concatenate([even, odd], 1), jnp.concatenate([odd, even], 1)
    )


def class_rows_direct(own_rows, cube_count, cube_at, grid_at):
    total = jnp.where(cube_at % 4 == grid_at, own_rows, 0.0)
    for step in (1, 2, 3):
        total = total + shifted(own_rows, step, lambda s, g: s == g, 4, cube_count)
    return total.transpose(0, 2, 1).reshape(ROWS, 1, 1, WIDE, BS)


def gathered(pieces, at, group, cube_count, after):
    groups = None
    if group < cube_count:
        groups = [[b + i for i in range(group)] for b in range(0, cube_count, group)]
    everything = lax.all_to_all(
        spread(pieces, at, group, after), "cube", 0, 0, axis_index_groups=groups
    )
    return everything.reshape(group // 4, 4, len(pieces), WIDE, BS)


def pivot_rows_everywhere(own_rows, sub_size, cube_count, slot, first_after, last_after):
    row = own_rows[0]
    if first_after:
        row = copy_after(row, first_after)
    got = shifted(row, 1, lambda s, g: s < 2, sub_size, cube_count)
    both = jnp.where(slot == 0, jnp.concatenate([row, got]), jnp.concatenate([got, row]))
    known = 2
    while known < sub_size:
        bits = (known,) if 4 * known > sub_size else (known, 2 * known, 3 * known)
        if last_after and known * (len(bits) + 1) == sub_size:
            both = copy_after(both, last_after)
        moved = [shifted(both, bit, lambda s, g: s < known, sub_size, cube_count) for bit in bits]
        both = jnp.where(slot < known, both, sum(moved[1:], moved[0]))
        known *= len(bits) + 1
    return both


def child_sources(table, child_size, cube_at, grid_at):
    parent_size = 2 * child_size
    slot = cube_at % parent_size
    front = cube_at // child_size
    maps = jnp.stack([table[front], table[front ^ 1]])
    rows = jnp.arange(ROWS) * parent_size + slot
    cols = jnp.arange(parent_size) * 4 + grid_at
    child_ids = jnp.arange(PIVOTS, ROWS * child_size)
    row_hit = maps[:, None, :] == rows[None, :, None]
    col_hit = maps[:, None, :] == cols[None, :, None]
    row_from = jnp.sum(jnp.where(row_hit, child_ids // child_size + 1, 0), 2) - 1
    col_from = jnp.sum(jnp.where(col_hit, child_ids // 4 + 1, 0), 2) - 1
    return jnp.concatenate([row_from, col_from], 1).astype(jnp.int32)


def column_targets(table, child_size, cube_at, grid_at, sources, count):
    mapping = table[(cube_at // child_size) ^ 1]
    child_ids = jnp.arange(count) * 4 + grid_at
    target = mapping[jnp.maximum(child_ids - PIVOTS, 0)]
    unused = jnp.argmax(sources[1, ROWS:] < 0)
    place = jnp.where(child_ids >= PIVOTS, target // 4, unused)
    valid = (child_ids >= PIVOTS) & (target >= PIVOTS)
    return place.astype(jnp.int32), valid.astype(jnp.int32)


def on_device(
    front_root, front_upper, front_middle, front_lower, place_upper, place_middle, place_lower
):
    cube_count = lax.axis_size("cube")
    cube_at = lax.axis_index("cube")
    grid_at = lax.axis_index("grid")
    stored = (front_root, front_upper, front_middle, front_lower)
    tables = (None, place_upper, place_middle, place_lower)
    factor_list = [None, None, None, None]
    rel = sources = update = None
    everyone = lambda s, g: True
    for depth in (3, 2, 1, 0):
        sub_size = cube_count >> depth
        half = sub_size // 2
        slot = cube_at % sub_size
        front = stored[depth]
        row_ids = jnp.arange(ROWS) * sub_size + slot
        col_ids = jnp.arange(sub_size) * 4 + grid_at
        info = jnp.concatenate([row_ids, col_ids]).astype(jnp.int32)
        children, arrived = (), ()
        if depth == 3:
            panel = front[:, :BS]
        else:
            got = shifted(rel, half, lambda s, g: g < 2, sub_size, cube_count)
            moves = jnp.concatenate([sources.reshape(-1), info])
            panel = pivot_panel(front, rel, got, moves, ())
            if depth == 1:
                own = update(after=(got,))
                other = shifted(own, half, everyone, sub_size, cube_count)
                children = (own, other)
                arrived = (other,)
            if depth == 0:
                own_early = update(after=(got,), span=(0, 1))
                other_early = shifted(own_early, half, everyone, sub_size, cube_count)
                arrived = (other_early,)
                from_early = jnp.where(sources[:, ROWS:] < EARLY, sources[:, ROWS:], -1)
                from_late = jnp.maximum(sources[0, ROWS:] - EARLY, -1)
                info = jnp.concatenate(
                    [
                        sources[0, :ROWS],
                        from_early[0],
                        sources[0, :ROWS],
                        from_late,
                        sources[1, :ROWS],
                        from_early[1],
                        info,
                    ]
                )
            else:
                info = moves
        if depth > 0:
            next_sources = child_sources(tables[depth], sub_size, cube_at, grid_at)
            info = jnp.concatenate([info, jnp.maximum(next_sources[0, ROWS : ROWS + 1], 0)])
        own_rows = both_pivots(panel, cube_count, grid_at)
        blocks = own_rows.reshape(ROWS, BS, WIDE)
        if depth == 3:
            pivots = pivot_rows_everywhere(blocks, sub_size, cube_count, slot, (), ())
            panels = class_rows_direct(blocks, cube_count, cube_at, grid_at)
        else:
            share = class_rows(panel, cube_count, cube_at, grid_at)
            zero = jnp.zeros((1,), jnp.int32)
        if depth in (2, 1):
            pivots = pivot_rows_everywhere(blocks, sub_size, cube_count, slot, (share,), arrived)
            panels = gathered([share], zero, sub_size, cube_count, (pivots,))
        if depth == 2:
            own = update(after=(pivots,))
            other = shifted(own, half, everyone, sub_size, cube_count)
            children = (own, other)
        if depth == 0:
            both = pivot_rows_everywhere(blocks, 8, cube_count, cube_at % 8, (share,), ())
            load = copy_after(jnp.concatenate([share, both]), arrived)
            pieces = [load] + [
                shifted(load, bit, everyone, sub_size, cube_count) for bit in (8, 16, 24)
            ]
            plane = cube_at // 8
            pivots = pieces[0][BS:]
            for step in (1, 2, 3):
                pivots = jnp.where(plane == step, pieces[step][BS:], pivots)
            panels = gathered(pieces, plane.astype(jnp.int32).reshape(1), 8, cube_count, ())
            own_late = update(after=tuple(pieces[1:]), span=(1, 3))
            other_late = shifted(own_late, half, everyone, sub_size, cube_count)
            children = (own_early, own_late, other_early)
        low, inverse = pivot_factor(pivots)
        solved = dot_nt(own_rows, inverse)
        pivot_slot = jnp.minimum(slot, PIVOTS - 1)
        head = jnp.where(
            slot < PIVOTS, lax.dynamic_slice_in_dim(low, pivot_slot * BS, BS, 0), solved[:BS]
        )
        solved = jnp.concatenate([head, solved[BS:]])
        factor_list[depth] = solved
        update = functools.partial(update_front, front, children, solved, panels, inverse, info)
        if depth > 0:
            rel = update(single=True)
            sources = next_sources
    rest = update(is_root=True)
    count = sources.shape[1] // 2 - ROWS // 2
    place, valid = column_targets(tables[1], half, cube_at, grid_at, sources, count)
    row_part = jnp.concatenate([sources[1, :ROWS], row_ids]).astype(jnp.int32)
    rest = add_columns(
        rest, other_late, jnp.concatenate([row_part, place[EARLY:], valid[EARLY:]])
    )
    return (factor_list[0], factor_list[1], factor_list[2], factor_list[3], rest)


def solution(mesh):
    return jax.shard_map(
        on_device,
        mesh=mesh,
        in_specs=(
            P("cube", "grid"),
            P("cube", "grid"),
            P("cube", "grid"),
            P("cube", "grid"),
            P(),
            P(),
            P(),
        ),
        out_specs=(
            P("cube", None),
            P("cube", None),
            P("cube", None),
            P("cube", None),
            P("cube", "grid"),
        ),
        check_vma=False,
    )
```

```python
import functools

import jax
import jax.numpy as jnp
from jax import lax
from jax.experimental import pallas as pl
from jax.experimental.pallas import tpu as pltpu
from jax.sharding import PartitionSpec as P

BS = 128
PIVOTS = 2
ROWS = 4
WIDE = PIVOTS * BS
HIGHEST = lax.Precision.HIGHEST
EARLY = 4
GROUP = 8
VMEM_LIMIT = 48 * 1024 * 1024


def dot_nn(a, b):
    return jnp.dot(a, b, precision=HIGHEST, preferred_element_type=jnp.float32)


def dot_nt(a, b):
    return lax.dot_general(
        a, b, (((1,), (1,)), ((), ())), precision=HIGHEST, preferred_element_type=jnp.float32
    )


def factor_block(block):
    n = BS
    rows = lax.broadcasted_iota(jnp.int32, (n, n), 0)
    eye = (rows == lax.broadcasted_iota(jnp.int32, (n, n), 1)).astype(jnp.float32)
    parts = [block, eye]
    for j in range(0, n, GROUP):
        cols = [jnp.broadcast_to(parts[0][:, j + t : j + t + 1], (n, n)) for t in range(GROUP)]
        mults = []
        for t in range(GROUP):
            col = cols[t]
            mult = jnp.where(rows > j + t, col * (1.0 / col[j + t : j + t + 1]), 0.0)
            for u in range(t + 1, GROUP):
                cols[u] = cols[u] - mult * col[j + u : j + u + 1]
            mults.append(mult)
        done = []
        for part in parts:
            total, heads = part, []
            for t in range(GROUP):
                head = part[j + t : j + t + 1]
                for u in range(t):
                    head = head - mults[u][j + t : j + t + 1] * heads[u]
                heads.append(head)
                total = total - mults[t] * head
            done.append(total)
        parts = done
    diag = jnp.sum(jnp.where(eye > 0, parts[0], 0.0), 1, keepdims=True)
    scale = lax.rsqrt(diag)
    return (parts[0] * scale).T, parts[1] * scale


def pivot_kernel(rows_ref, low_ref, inv_ref):
    c0, i0 = factor_block(rows_ref[:BS, :BS])
    k10 = dot_nt(rows_ref[BS:, :BS], i0)
    c1, i1 = factor_block(rows_ref[BS:, BS:] - dot_nt(k10, k10))
    lane = lax.broadcasted_iota(jnp.int32, (BS, BS), 1)
    sub = lax.broadcasted_iota(jnp.int32, (BS, BS), 0)
    low = lane <= sub
    zero = jnp.zeros((BS, BS), jnp.float32)
    low_ref[:BS, :BS] = jnp.where(low, c0, 0.0)
    low_ref[:BS, BS:] = zero
    low_ref[BS:, :BS] = k10
    low_ref[BS:, BS:] = jnp.where(low, c1, 0.0)
    inv_ref[:BS, :BS] = i0
    inv_ref[:BS, BS:] = zero
    inv_ref[BS:, :BS] = -dot_nn(i1, dot_nn(k10, i0))
    inv_ref[BS:, BS:] = i1


def pivot_factor(pivot_rows):
    shape = jax.ShapeDtypeStruct((WIDE, WIDE), jnp.float32)
    whole = pl.BlockSpec(memory_space=pltpu.VMEM)
    return pl.pallas_call(
        pivot_kernel,
        out_shape=[shape, shape],
        in_specs=[whole],
        out_specs=[whole, whole],
        compiler_params=pltpu.CompilerParams(vmem_limit_bytes=VMEM_LIMIT),
        name="pivot_factor",
    )(pivot_rows)


ANY = pl.BlockSpec(memory_space=pl.ANY)


def parts_of(a):
    high = a.astype(jnp.bfloat16)
    return high, (a - high.astype(jnp.float32)).astype(jnp.bfloat16)


def split_left(a):
    high, low = parts_of(a)
    return jnp.concatenate([high, low, high], 1)


def split_right(a):
    high, low = parts_of(a)
    return jnp.concatenate([high, high, low], 0)


def dot_split(left, right):
    return jnp.dot(left, right, preferred_element_type=jnp.float32)


def update_kernel(cols, per, children, is_root, col_of, place_of, info_ref, *refs):
    front_ref, refs = refs[0], refs[1:]
    child_refs, refs = refs[: children * per], refs[children * per :]
    key_ref, panel_ref, inv_ref = refs[:3]
    out_ref, key_split, inv_split = refs[-3:]
    step = pl.program_id(0)

    @pl.when(step == 0)
    def _():
        key_split[...] = split_left(key_ref[...])
        inv_split[...] = split_left(inv_ref[...])

    panel = jnp.concatenate([panel_ref[place_of(t)] for t in range(per)], 1)
    solved = dot_split(inv_split[...], split_right(panel))
    terms = dot_split(key_split[...], split_right(solved))
    width = ROWS + cols
    places = children * width
    for t in range(per):
        at = col_of(step, info_ref) * per + t
        lanes = slice(t * BS, (t + 1) * BS)
        for r in range(ROWS):
            span = slice(r * BS, (r + 1) * BS)
            block = front_ref[span, lanes] - terms[span, lanes]
            for which in range(children):
                source = info_ref[which * width + r]
                present = (source >= 0) & (info_ref[which * width + ROWS + at] >= 0)
                taken = child_refs[which * per + t][pl.ds(jnp.maximum(source, 0) * BS, BS), :]
                block = block + jnp.where(present, taken, 0.0)
            if is_root:
                keep = (info_ref[places + r] >= PIVOTS) & (info_ref[places + ROWS + at] >= PIVOTS)
                block = jnp.where(keep, block, 0.0)
            out_ref[span, lanes] = block


def update_front(front, children, key, panels, inverse, info, is_root=False, single=False, span=None, after=()):
    cols = front.shape[1] // BS
    width = ROWS + cols
    height = ROWS * BS
    per = 1 if single else 4
    rel_at = (len(children) + 1) * width
    first, steps = (0, 1) if single else span or (0, cols // per)
    if single:
        col_of = lambda c, info: info[rel_at]
    else:
        col_of = lambda c, info: c + first
    outer, _, planes = panels.shape[:3]
    place_of = lambda t: (t % outer, t // outer, 0)
    if single:
        panel_dims = (1, 1, 1)
        panel_at = lambda c, info: (lax.rem(col_of(c, info), outer), lax.div(col_of(c, info), outer), 0, 0, 0)
    elif planes == 1:
        panel_dims = (outer, per // outer, 1)
        panel_at = lambda c, info: (0, c + first, 0, 0, 0)
    else:
        panel_dims = (outer, 1, per // outer)
        runs = planes * outer // per
        panel_at = lambda c, info: (0, lax.div(c, runs), lax.rem(c, runs), 0, 0)
        place_of = lambda t: (t % outer, 0, t // outer)

    column = pl.BlockSpec((height, per * BS), lambda c, info: (0, col_of(c, info)))
    specs, args = [column], [front]
    for which, child in enumerate(children):
        for t in range(per):
            specs.append(
                pl.BlockSpec(
                    (height, BS),
                    lambda c, info, which=which, t=t: (
                        0,
                        jnp.maximum(info[which * width + ROWS + col_of(c, info) * per + t], 0),
                    ),
                )
            )
            args.append(child)
    specs += [
        pl.BlockSpec((height, WIDE), lambda c, info: (0, 0)),
        pl.BlockSpec((*panel_dims, WIDE, BS), panel_at),
        pl.BlockSpec((WIDE, WIDE), lambda c, info: (0, 0)),
    ] + [ANY] * len(after)
    args += [key, panels, inverse, *after]
    return pl.pallas_call(
        functools.partial(update_kernel, cols, per, len(children), is_root, col_of, place_of),
        out_shape=jax.ShapeDtypeStruct((height, steps * per * BS), jnp.float32),
        grid_spec=pltpu.PrefetchScalarGridSpec(
            num_scalar_prefetch=1,
            grid=(steps,),
            in_specs=specs,
            out_specs=pl.BlockSpec((height, per * BS), lambda c, info: (0, c)),
            scratch_shapes=[
                pltpu.VMEM((height, 3 * WIDE), jnp.bfloat16),
                pltpu.VMEM((WIDE, 3 * WIDE), jnp.bfloat16),
            ],
        ),
        compiler_params=pltpu.CompilerParams(vmem_limit_bytes=VMEM_LIMIT),
        cost_estimate=pl.CostEstimate(
            flops=2 * height * WIDE * steps * per * BS * 2,
            bytes_accessed=16 * height * steps * per * BS,
            transcendentals=0,
        ),
        name="update_front",
    )(info, *args)


def panel_kernel(width, info_ref, front_ref, own_ref, other_ref, *refs):
    out_ref = refs[-1]
    for r in range(ROWS):
        block = front_ref[r * BS : (r + 1) * BS, :]
        for which, child_ref in ((0, own_ref), (1, other_ref)):
            source = info_ref[which * width + r]
            present = (source >= 0) & (info_ref[which * width + ROWS] >= 0)
            taken = child_ref[pl.ds(jnp.maximum(source, 0) * BS, BS), :]
            block = block + jnp.where(present, taken, 0.0)
        out_ref[r * BS : (r + 1) * BS, :] = block


def pivot_panel(front, own, other, info, after):
    piece = pl.BlockSpec((ROWS * BS, BS), lambda c, info: (0, 0))
    return pl.pallas_call(
        functools.partial(panel_kernel, ROWS + front.shape[1] // BS),
        out_shape=jax.ShapeDtypeStruct((ROWS * BS, BS), jnp.float32),
        grid_spec=pltpu.PrefetchScalarGridSpec(
            num_scalar_prefetch=1,
            grid=(1,),
            in_specs=[piece] * 3 + [ANY] * len(after),
            out_specs=piece,
        ),
        name="pivot_panel",
    )(info, front, own, other, *after)


def add_kernel(count, info_ref, front_ref, child_ref, out_ref):
    valid = info_ref[2 * ROWS + count + pl.program_id(0)] > 0
    for r in range(ROWS):
        span = slice(r * BS, (r + 1) * BS)
        source = info_ref[r]
        present = valid & (source >= 0) & (info_ref[ROWS + r] >= PIVOTS)
        taken = child_ref[pl.ds(jnp.maximum(source, 0) * BS, BS), :]
        out_ref[span, :] = front_ref[span, :] + jnp.where(present, taken, 0.0)


def add_columns(front, child, info):
    count = child.shape[1] // BS
    target = pl.BlockSpec((ROWS * BS, BS), lambda c, info: (0, info[2 * ROWS + c]))
    return pl.pallas_call(
        functools.partial(add_kernel, count),
        out_shape=jax.ShapeDtypeStruct(front.shape, jnp.float32),
        grid_spec=pltpu.PrefetchScalarGridSpec(
            num_scalar_prefetch=1,
            grid=(count,),
            in_specs=[target, pl.BlockSpec((ROWS * BS, BS), lambda c, info: (0, c))],
            out_specs=target,
        ),
        input_output_aliases={1: 0},
        compiler_params=pltpu.CompilerParams(vmem_limit_bytes=VMEM_LIMIT),
        name="add_columns",
    )(info, front, child)


def copy_kernel(in_ref, *refs):
    refs[-1][...] = in_ref[...]


def copy_after(array, after, low=0, high=None):
    rows, cols = array.shape
    high = cols if high is None else high
    wide = WIDE
    return pl.pallas_call(
        copy_kernel,
        out_shape=jax.ShapeDtypeStruct((rows, high - low), jnp.float32),
        grid=((high - low) // wide,),
        in_specs=[pl.BlockSpec((rows, wide), lambda c: (0, c + low // wide))] + [ANY] * len(after),
        out_specs=pl.BlockSpec((rows, wide), lambda c: (0, c)),
        name="copy_after",
    )(array, *after)


def spread_kernel(count, at_ref, *refs):
    pieces, out_ref, scratch = refs[:count], refs[-2], refs[-1]

    @pl.when(pl.program_id(0) == 0)
    def _():
        for step in range(count):
            turned = pieces[step][...].T
            for place in range(count):

                @pl.when(at_ref[0] == place ^ step)
                def _():
                    scratch[place] = turned

    for t in range(out_ref.shape[0]):
        out_ref[t] = scratch[...]


def spread(pieces, at, copies, after):
    count = len(pieces)
    shape = (count, WIDE, BS)
    each = 4 if count == 1 else 2
    return pl.pallas_call(
        functools.partial(spread_kernel, count),
        out_shape=jax.ShapeDtypeStruct((copies, *shape), jnp.float32),
        grid_spec=pltpu.PrefetchScalarGridSpec(
            num_scalar_prefetch=1,
            grid=(copies // each,),
            in_specs=[pl.BlockSpec((BS, WIDE), lambda c, at: (0, 0))] * count + [ANY] * len(after),
            out_specs=pl.BlockSpec((each, *shape), lambda c, at: (c, 0, 0, 0)),
            scratch_shapes=[pltpu.VMEM(shape, jnp.float32)],
        ),
        compiler_params=pltpu.CompilerParams(vmem_limit_bytes=VMEM_LIMIT),
        name="spread",
    )(at, *pieces, *after)


def send(block, route):
    pairs = [(a[0] * 4 + a[1], b[0] * 4 + b[1]) for a, b in route]
    return lax.ppermute(block, ("cube", "grid"), pairs)


def both_pivots(piece, cube_count, grid_at):
    near = send(piece, [((s, g), (s, g ^ 1)) for s in range(cube_count) for g in (0, 1)])
    far = send(piece, [((s, g), (s, g ^ 2)) for s in range(cube_count) for g in (0, 1)])
    cross = send(far, [((s, g), (s, g ^ 1)) for s in range(cube_count) for g in (2, 3)])
    mine = jnp.where(grid_at < 2, piece, far)
    mate = jnp.where(grid_at < 2, near, cross)
    first = jnp.where(grid_at % 2 == 0, mine, mate)
    second = jnp.where(grid_at % 2 == 0, mate, mine)
    return jnp.concatenate([first, second], -1)


def shifted(block, bit, sources, sub_size, cube_count, grids=None):
    route = []
    for base in range(0, cube_count, sub_size):
        for s in range(sub_size):
            for g in range(4):
                if sources(s, g):
                    route.append(((base + s, g), (base + (s ^ bit), g)))
    return send(block, route)


def class_rows(panel, cube_count, cube_at, grid_at):
    blocks = panel.reshape(ROWS, BS, BS)
    got = []
    for turn in range(4):
        route = []
        for s in range(cube_count):
            for p in (0, 1):
                route.append(((s, p), (s - s % 4 + (turn ^ p), s % 4)))
        row = lax.dynamic_index_in_dim(blocks, (turn ^ grid_at) & 3, 0, keepdims=False)
        got.append(send(row, route))
    even, odd = got[0] + got[2], got[1] + got[3]
    return jnp.where(
        cube_at % 2 == 0, jnp.concatenate([even, odd], 1), jnp.concatenate([odd, even], 1)
    )


def class_rows_direct(own_rows, cube_count, cube_at, grid_at):
    total = jnp.where(cube_at % 4 == grid_at, own_rows, 0.0)
    for step in (1, 2, 3):
        total = total + shifted(own_rows, step, lambda s, g: s == g, 4, cube_count)
    return total.transpose(0, 2, 1).reshape(ROWS, 1, 1, WIDE, BS)


def gathered(pieces, at, group, cube_count, after):
    groups = None
    if group < cube_count:
        groups = [[b + i for i in range(group)] for b in range(0, cube_count, group)]
    everything = lax.all_to_all(
        spread(pieces, at, group, after), "cube", 0, 0, axis_index_groups=groups
    )
    return everything.reshape(group // 4, 4, len(pieces), WIDE, BS)


def pivot_rows_everywhere(own_rows, sub_size, cube_count, cube_at, after):
    row = own_rows[0]
    near = min(sub_size, 8)
    sums = [None, None]
    for step in range(1, near):
        moved = shifted(row, step, lambda s, g: s < PIVOTS, sub_size, cube_count)
        sums[step % 2] = moved if sums[step % 2] is None else sums[step % 2] + moved
    even, odd = sums
    slot = cube_at % sub_size
    is_even = slot % 2 == 0
    first = jnp.where(slot == 0, row, jnp.where(is_even, even, odd))
    second = jnp.where(slot == 1, row, jnp.where(is_even, odd, even))
    both = jnp.concatenate([first, second])
    if sub_size == 16:
        both = copy_after(both, after)
        far = shifted(both, near, lambda s, g: s < near, sub_size, cube_count)
        both = jnp.where(slot < near, both, far)
    return both


def child_sources(table, child_size, cube_at, grid_at):
    parent_size = 2 * child_size
    slot = cube_at % parent_size
    front = cube_at // child_size
    maps = jnp.stack([table[front], table[front ^ 1]])
    rows = jnp.arange(ROWS) * parent_size + slot
    cols = jnp.arange(parent_size) * 4 + grid_at
    child_ids = jnp.arange(PIVOTS, ROWS * child_size)
    row_hit = maps[:, None, :] == rows[None, :, None]
    col_hit = maps[:, None, :] == cols[None, :, None]
    row_from = jnp.sum(jnp.where(row_hit, child_ids // child_size + 1, 0), 2) - 1
    col_from = jnp.sum(jnp.where(col_hit, child_ids // 4 + 1, 0), 2) - 1
    return jnp.concatenate([row_from, col_from], 1).astype(jnp.int32)


def column_targets(table, child_size, cube_at, grid_at, sources, count):
    mapping = table[(cube_at // child_size) ^ 1]
    child_ids = jnp.arange(count) * 4 + grid_at
    target = mapping[jnp.maximum(child_ids - PIVOTS, 0)]
    unused = jnp.argmax(sources[1, ROWS:] < 0)
    place = jnp.where(child_ids >= PIVOTS, target // 4, unused)
    valid = (child_ids >= PIVOTS) & (target >= PIVOTS)
    return place.astype(jnp.int32), valid.astype(jnp.int32)


def on_device(
    front_root, front_upper, front_middle, front_lower, place_upper, place_middle, place_lower
):
    cube_count = lax.axis_size("cube")
    cube_at = lax.axis_index("cube")
    grid_at = lax.axis_index("grid")
    stored = (front_root, front_upper, front_middle, front_lower)
    tables = (None, place_upper, place_middle, place_lower)
    factor_list = [None, None, None, None]
    rel = sources = update = None
    everyone = lambda s, g: True
    for depth in (3, 2, 1, 0):
        sub_size = cube_count >> depth
        half = sub_size // 2
        slot = cube_at % sub_size
        front = stored[depth]
        row_ids = jnp.arange(ROWS) * sub_size + slot
        col_ids = jnp.arange(sub_size) * 4 + grid_at
        info = jnp.concatenate([row_ids, col_ids]).astype(jnp.int32)
        children, arrived = (), ()
        if depth == 3:
            panel = front[:, :BS]
        else:
            got = shifted(rel, half, lambda s, g: g < 2, sub_size, cube_count)
            moves = jnp.concatenate([sources.reshape(-1), info])
            panel = pivot_panel(front, rel, got, moves, ())
            if depth == 1:
                own = update(after=(got,))
                other = shifted(own, half, everyone, sub_size, cube_count)
                children = (own, other)
                arrived = (other,)
            if depth == 0:
                own_early = update(after=(got,), span=(0, 1))
                other_early = shifted(own_early, half, everyone, sub_size, cube_count)
                arrived = (other_early,)
                from_early = jnp.where(sources[:, ROWS:] < EARLY, sources[:, ROWS:], -1)
                from_late = jnp.maximum(sources[0, ROWS:] - EARLY, -1)
                info = jnp.concatenate(
                    [
                        sources[0, :ROWS],
                        from_early[0],
                        sources[0, :ROWS],
                        from_late,
                        sources[1, :ROWS],
                        from_early[1],
                        info,
                    ]
                )
            else:
                info = moves
        if depth > 0:
            next_sources = child_sources(tables[depth], sub_size, cube_at, grid_at)
            info = jnp.concatenate([info, jnp.maximum(next_sources[0, ROWS : ROWS + 1], 0)])
        own_rows = both_pivots(panel, cube_count, grid_at)
        blocks = own_rows.reshape(ROWS, BS, WIDE)
        if depth == 3:
            pivots = pivot_rows_everywhere(blocks, sub_size, cube_count, cube_at, ())
            panels = class_rows_direct(blocks, cube_count, cube_at, grid_at)
        else:
            share = class_rows(panel, cube_count, cube_at, grid_at)
            zero = jnp.zeros((1,), jnp.int32)
        if depth in (2, 1):
            pivots = pivot_rows_everywhere(blocks, sub_size, cube_count, cube_at, arrived)
            panels = gathered([share], zero, sub_size, cube_count, (pivots,))
        if depth == 2:
            own = update(after=(pivots,))
            other = shifted(own, half, everyone, sub_size, cube_count)
            children = (own, other)
        if depth == 0:
            both = pivot_rows_everywhere(blocks, sub_size, cube_count, cube_at, ())
            load = copy_after(jnp.concatenate([share, both]), arrived)
            pieces = [load] + [
                shifted(load, bit, everyone, sub_size, cube_count) for bit in (8, 16, 24)
            ]
            plane = cube_at // 8
            pivots = pieces[0][BS:]
            for step in (1, 2, 3):
                pivots = jnp.where(plane == step, pieces[step][BS:], pivots)
            panels = gathered(pieces, plane.astype(jnp.int32).reshape(1), 8, cube_count, ())
            own_late = update(after=(load,), span=(1, 3))
            other_late = shifted(own_late, half, everyone, sub_size, cube_count)
            children = (own_early, own_late, other_early)
        low, inverse = pivot_factor(pivots)
        solved = dot_nt(own_rows, inverse)
        pivot_slot = jnp.minimum(slot, PIVOTS - 1)
        head = jnp.where(
            slot < PIVOTS, lax.dynamic_slice_in_dim(low, pivot_slot * BS, BS, 0), solved[:BS]
        )
        solved = jnp.concatenate([head, solved[BS:]])
        factor_list[depth] = solved
        update = functools.partial(update_front, front, children, solved, panels, inverse, info)
        if depth > 0:
            rel = update(single=True)
            sources = next_sources
    rest = update(is_root=True)
    count = sources.shape[1] // 2 - ROWS // 2
    place, valid = column_targets(tables[1], half, cube_at, grid_at, sources, count)
    row_part = jnp.concatenate([sources[1, :ROWS], row_ids]).astype(jnp.int32)
    rest = add_columns(
        rest, other_late, jnp.concatenate([row_part, place[EARLY:], valid[EARLY:]])
    )
    return (factor_list[0], factor_list[1], factor_list[2], factor_list[3], rest)


def solution(mesh):
    return jax.shard_map(
        on_device,
        mesh=mesh,
        in_specs=(
            P("cube", "grid"),
            P("cube", "grid"),
            P("cube", "grid"),
            P("cube", "grid"),
            P(),
            P(),
            P(),
        ),
        out_specs=(
            P("cube", None),
            P("cube", None),
            P("cube", None),
            P("cube", None),
            P("cube", "grid"),
        ),
        check_vma=False,
    )
```

```python
import functools

import jax
import jax.numpy as jnp
from jax import lax
from jax.experimental import pallas as pl
from jax.experimental.pallas import tpu as pltpu
from jax.sharding import PartitionSpec as P

BS = 128
PIVOTS = 2
ROWS = 4
WIDE = PIVOTS * BS
HIGHEST = lax.Precision.HIGHEST
EARLY = 4
GROUP = 8
VMEM_LIMIT = 48 * 1024 * 1024


def dot_nn(a, b):
    return jnp.dot(a, b, precision=HIGHEST, preferred_element_type=jnp.float32)


def dot_nt(a, b):
    return lax.dot_general(
        a, b, (((1,), (1,)), ((), ())), precision=HIGHEST, preferred_element_type=jnp.float32
    )


def factor_block(block):
    n = BS
    rows = lax.broadcasted_iota(jnp.int32, (n, n), 0)
    eye = (rows == lax.broadcasted_iota(jnp.int32, (n, n), 1)).astype(jnp.float32)
    parts = [block, eye]
    for j in range(0, n, GROUP):
        cols = [jnp.broadcast_to(parts[0][:, j + t : j + t + 1], (n, n)) for t in range(GROUP)]
        mults = []
        for t in range(GROUP):
            col = cols[t]
            mult = jnp.where(rows > j + t, col * (1.0 / col[j + t : j + t + 1]), 0.0)
            for u in range(t + 1, GROUP):
                cols[u] = cols[u] - mult * col[j + u : j + u + 1]
            mults.append(mult)
        done = []
        for part in parts:
            total, heads = part, []
            for t in range(GROUP):
                head = part[j + t : j + t + 1]
                for u in range(t):
                    head = head - mults[u][j + t : j + t + 1] * heads[u]
                heads.append(head)
                total = total - mults[t] * head
            done.append(total)
        parts = done
    diag = jnp.sum(jnp.where(eye > 0, parts[0], 0.0), 1, keepdims=True)
    scale = lax.rsqrt(diag)
    return (parts[0] * scale).T, parts[1] * scale


def pivot_kernel(rows_ref, low_ref, inv_ref):
    c0, i0 = factor_block(rows_ref[:BS, :BS])
    k10 = dot_nt(rows_ref[BS:, :BS], i0)
    c1, i1 = factor_block(rows_ref[BS:, BS:] - dot_nt(k10, k10))
    lane = lax.broadcasted_iota(jnp.int32, (BS, BS), 1)
    sub = lax.broadcasted_iota(jnp.int32, (BS, BS), 0)
    low = lane <= sub
    zero = jnp.zeros((BS, BS), jnp.float32)
    low_ref[:BS, :BS] = jnp.where(low, c0, 0.0)
    low_ref[:BS, BS:] = zero
    low_ref[BS:, :BS] = k10
    low_ref[BS:, BS:] = jnp.where(low, c1, 0.0)
    inv_ref[:BS, :BS] = i0
    inv_ref[:BS, BS:] = zero
    inv_ref[BS:, :BS] = -dot_nn(i1, dot_nn(k10, i0))
    inv_ref[BS:, BS:] = i1


def pivot_factor(pivot_rows):
    shape = jax.ShapeDtypeStruct((WIDE, WIDE), jnp.float32)
    whole = pl.BlockSpec(memory_space=pltpu.VMEM)
    return pl.pallas_call(
        pivot_kernel,
        out_shape=[shape, shape],
        in_specs=[whole],
        out_specs=[whole, whole],
        compiler_params=pltpu.CompilerParams(vmem_limit_bytes=VMEM_LIMIT),
        name="pivot_factor",
    )(pivot_rows)


ANY = pl.BlockSpec(memory_space=pl.ANY)


def parts_of(a):
    high = a.astype(jnp.bfloat16)
    return high, (a - high.astype(jnp.float32)).astype(jnp.bfloat16)


def split_left(a):
    high, low = parts_of(a)
    return jnp.concatenate([high, low, high], 1)


def split_right(a):
    high, low = parts_of(a)
    return jnp.concatenate([high, high, low], 0)


def dot_split(left, right):
    return jnp.dot(left, right, preferred_element_type=jnp.float32)


def update_kernel(cols, per, children, is_root, col_of, place_of, info_ref, *refs):
    front_ref, refs = refs[0], refs[1:]
    child_refs, refs = refs[: children * per], refs[children * per :]
    key_ref, panel_ref, inv_ref = refs[:3]
    out_ref, key_split, inv_split = refs[-3:]
    step = pl.program_id(0)

    @pl.when(step == 0)
    def _():
        key_split[...] = split_left(key_ref[...])
        inv_split[...] = split_left(inv_ref[...])

    panel = jnp.concatenate([panel_ref[place_of(t)] for t in range(per)], 1)
    solved = dot_split(inv_split[...], split_right(panel))
    terms = dot_split(key_split[...], split_right(solved))
    width = ROWS + cols
    places = children * width
    for t in range(per):
        at = col_of(step, info_ref) * per + t
        lanes = slice(t * BS, (t + 1) * BS)
        for r in range(ROWS):
            span = slice(r * BS, (r + 1) * BS)
            block = front_ref[span, lanes] - terms[span, lanes]
            for which in range(children):
                source = info_ref[which * width + r]
                present = (source >= 0) & (info_ref[which * width + ROWS + at] >= 0)
                taken = child_refs[which * per + t][pl.ds(jnp.maximum(source, 0) * BS, BS), :]
                block = block + jnp.where(present, taken, 0.0)
            if is_root:
                keep = (info_ref[places + r] >= PIVOTS) & (info_ref[places + ROWS + at] >= PIVOTS)
                block = jnp.where(keep, block, 0.0)
            out_ref[span, lanes] = block


def update_front(front, children, key, panels, inverse, info, is_root=False, single=False, span=None, after=()):
    cols = front.shape[1] // BS
    width = ROWS + cols
    height = ROWS * BS
    per = 1 if single else 4
    rel_at = (len(children) + 1) * width
    first, steps = (0, 1) if single else span or (0, cols // per)
    if single:
        col_of = lambda c, info: info[rel_at]
    else:
        col_of = lambda c, info: c + first
    outer, _, planes = panels.shape[:3]
    place_of = lambda t: (t % outer, t // outer, 0)
    if single:
        panel_dims = (1, 1, 1)
        panel_at = lambda c, info: (lax.rem(col_of(c, info), outer), lax.div(col_of(c, info), outer), 0, 0, 0)
    elif planes == 1:
        panel_dims = (outer, per // outer, 1)
        panel_at = lambda c, info: (0, c + first, 0, 0, 0)
    else:
        panel_dims = (outer, 1, per // outer)
        runs = planes * outer // per
        panel_at = lambda c, info: (0, lax.div(c, runs), lax.rem(c, runs), 0, 0)
        place_of = lambda t: (t % outer, 0, t // outer)

    column = pl.BlockSpec((height, per * BS), lambda c, info: (0, col_of(c, info)))
    specs, args = [column], [front]
    for which, child in enumerate(children):
        for t in range(per):
            specs.append(
                pl.BlockSpec(
                    (height, BS),
                    lambda c, info, which=which, t=t: (
                        0,
                        jnp.maximum(info[which * width + ROWS + col_of(c, info) * per + t], 0),
                    ),
                )
            )
            args.append(child)
    specs += [
        pl.BlockSpec((height, WIDE), lambda c, info: (0, 0)),
        pl.BlockSpec((*panel_dims, WIDE, BS), panel_at),
        pl.BlockSpec((WIDE, WIDE), lambda c, info: (0, 0)),
    ] + [ANY] * len(after)
    args += [key, panels, inverse, *after]
    return pl.pallas_call(
        functools.partial(update_kernel, cols, per, len(children), is_root, col_of, place_of),
        out_shape=jax.ShapeDtypeStruct((height, steps * per * BS), jnp.float32),
        grid_spec=pltpu.PrefetchScalarGridSpec(
            num_scalar_prefetch=1,
            grid=(steps,),
            in_specs=specs,
            out_specs=pl.BlockSpec((height, per * BS), lambda c, info: (0, c)),
            scratch_shapes=[
                pltpu.VMEM((height, 3 * WIDE), jnp.bfloat16),
                pltpu.VMEM((WIDE, 3 * WIDE), jnp.bfloat16),
            ],
        ),
        compiler_params=pltpu.CompilerParams(vmem_limit_bytes=VMEM_LIMIT),
        cost_estimate=pl.CostEstimate(
            flops=2 * height * WIDE * steps * per * BS * 2,
            bytes_accessed=16 * height * steps * per * BS,
            transcendentals=0,
        ),
        name="update_front",
    )(info, *args)


def panel_kernel(width, info_ref, front_ref, own_ref, other_ref, *refs):
    out_ref = refs[-1]
    for r in range(ROWS):
        block = front_ref[r * BS : (r + 1) * BS, :]
        for which, child_ref in ((0, own_ref), (1, other_ref)):
            source = info_ref[which * width + r]
            present = (source >= 0) & (info_ref[which * width + ROWS] >= 0)
            taken = child_ref[pl.ds(jnp.maximum(source, 0) * BS, BS), :]
            block = block + jnp.where(present, taken, 0.0)
        out_ref[r * BS : (r + 1) * BS, :] = block


def pivot_panel(front, own, other, info, after):
    piece = pl.BlockSpec((ROWS * BS, BS), lambda c, info: (0, 0))
    return pl.pallas_call(
        functools.partial(panel_kernel, ROWS + front.shape[1] // BS),
        out_shape=jax.ShapeDtypeStruct((ROWS * BS, BS), jnp.float32),
        grid_spec=pltpu.PrefetchScalarGridSpec(
            num_scalar_prefetch=1,
            grid=(1,),
            in_specs=[piece] * 3 + [ANY] * len(after),
            out_specs=piece,
        ),
        name="pivot_panel",
    )(info, front, own, other, *after)


def add_kernel(count, info_ref, front_ref, child_ref, out_ref):
    valid = info_ref[2 * ROWS + count + pl.program_id(0)] > 0
    for r in range(ROWS):
        span = slice(r * BS, (r + 1) * BS)
        source = info_ref[r]
        present = valid & (source >= 0) & (info_ref[ROWS + r] >= PIVOTS)
        taken = child_ref[pl.ds(jnp.maximum(source, 0) * BS, BS), :]
        out_ref[span, :] = front_ref[span, :] + jnp.where(present, taken, 0.0)


def add_columns(front, child, info):
    count = child.shape[1] // BS
    target = pl.BlockSpec((ROWS * BS, BS), lambda c, info: (0, info[2 * ROWS + c]))
    return pl.pallas_call(
        functools.partial(add_kernel, count),
        out_shape=jax.ShapeDtypeStruct(front.shape, jnp.float32),
        grid_spec=pltpu.PrefetchScalarGridSpec(
            num_scalar_prefetch=1,
            grid=(count,),
            in_specs=[target, pl.BlockSpec((ROWS * BS, BS), lambda c, info: (0, c))],
            out_specs=target,
        ),
        input_output_aliases={1: 0},
        compiler_params=pltpu.CompilerParams(vmem_limit_bytes=VMEM_LIMIT),
        name="add_columns",
    )(info, front, child)


def copy_kernel(in_ref, *refs):
    refs[-1][...] = in_ref[...]


def copy_after(array, after, low=0, high=None):
    rows, cols = array.shape
    high = cols if high is None else high
    wide = WIDE
    return pl.pallas_call(
        copy_kernel,
        out_shape=jax.ShapeDtypeStruct((rows, high - low), jnp.float32),
        grid=((high - low) // wide,),
        in_specs=[pl.BlockSpec((rows, wide), lambda c: (0, c + low // wide))] + [ANY] * len(after),
        out_specs=pl.BlockSpec((rows, wide), lambda c: (0, c)),
        name="copy_after",
    )(array, *after)


def spread_kernel(count, at_ref, *refs):
    pieces, out_ref, scratch = refs[:count], refs[-2], refs[-1]

    @pl.when(pl.program_id(0) == 0)
    def _():
        for step in range(count):
            turned = pieces[step][...].T
            for place in range(count):

                @pl.when(at_ref[0] == place ^ step)
                def _():
                    scratch[place] = turned

    for t in range(out_ref.shape[0]):
        out_ref[t] = scratch[...]


def spread(pieces, at, copies, after):
    count = len(pieces)
    shape = (count, WIDE, BS)
    each = 4 if count == 1 else 2
    return pl.pallas_call(
        functools.partial(spread_kernel, count),
        out_shape=jax.ShapeDtypeStruct((copies, *shape), jnp.float32),
        grid_spec=pltpu.PrefetchScalarGridSpec(
            num_scalar_prefetch=1,
            grid=(copies // each,),
            in_specs=[pl.BlockSpec((BS, WIDE), lambda c, at: (0, 0))] * count + [ANY] * len(after),
            out_specs=pl.BlockSpec((each, *shape), lambda c, at: (c, 0, 0, 0)),
            scratch_shapes=[pltpu.VMEM(shape, jnp.float32)],
        ),
        compiler_params=pltpu.CompilerParams(vmem_limit_bytes=VMEM_LIMIT),
        name="spread",
    )(at, *pieces, *after)


def send(block, route):
    pairs = [(a[0] * 4 + a[1], b[0] * 4 + b[1]) for a, b in route]
    return lax.ppermute(block, ("cube", "grid"), pairs)


def both_pivots(piece, cube_count, grid_at):
    near = send(piece, [((s, g), (s, g ^ 1)) for s in range(cube_count) for g in (0, 1)])
    far = send(piece, [((s, g), (s, g ^ 2)) for s in range(cube_count) for g in (0, 1)])
    cross = send(far, [((s, g), (s, g ^ 1)) for s in range(cube_count) for g in (2, 3)])
    mine = jnp.where(grid_at < 2, piece, far)
    mate = jnp.where(grid_at < 2, near, cross)
    first = jnp.where(grid_at % 2 == 0, mine, mate)
    second = jnp.where(grid_at % 2 == 0, mate, mine)
    return jnp.concatenate([first, second], -1)


def shifted(block, bit, sources, sub_size, cube_count, grids=None):
    route = []
    for base in range(0, cube_count, sub_size):
        for s in range(sub_size):
            for g in range(4):
                if sources(s, g):
                    route.append(((base + s, g), (base + (s ^ bit), g)))
    return send(block, route)


def quad_exchange(own_rows, cube_count, grid_at):
    load = jnp.stack([own_rows, jnp.broadcast_to(own_rows[:1], own_rows.shape)], 1)
    quads = [[b + i for i in range(4)] for b in range(0, cube_count, 4)]
    got = lax.all_to_all(load, "cube", 0, 0, axis_index_groups=quads)
    share = lax.dynamic_index_in_dim(got[:, 0], grid_at, 0, keepdims=False)
    return share, got[:PIVOTS, 1].reshape(WIDE, WIDE)


def passed_on(both, known, sub_size, cube_count, slot):
    moved = shifted(both, known, lambda s, g: s < known, sub_size, cube_count)
    return jnp.where(slot < known, both, moved)


def class_rows_direct(own_rows, cube_count, cube_at, grid_at):
    total = jnp.where(cube_at % 4 == grid_at, own_rows, 0.0)
    for step in (1, 2, 3):
        total = total + shifted(own_rows, step, lambda s, g: s == g, 4, cube_count)
    return total.transpose(0, 2, 1).reshape(ROWS, 1, 1, WIDE, BS)


def gathered(pieces, at, group, cube_count, after):
    groups = None
    if group < cube_count:
        groups = [[b + i for i in range(group)] for b in range(0, cube_count, group)]
    everything = lax.all_to_all(
        spread(pieces, at, group, after), "cube", 0, 0, axis_index_groups=groups
    )
    return everything.reshape(group // 4, 4, len(pieces), WIDE, BS)


def pivot_rows_everywhere(own_rows, cube_count, slot):
    row = own_rows[0]
    got = shifted(row, 1, lambda s, g: s < 2, 4, cube_count)
    both = jnp.where(slot == 0, jnp.concatenate([row, got]), jnp.concatenate([got, row]))
    return passed_on(both, 2, 4, cube_count, slot)


def child_sources(table, child_size, cube_at, grid_at):
    parent_size = 2 * child_size
    slot = cube_at % parent_size
    front = cube_at // child_size
    maps = jnp.stack([table[front], table[front ^ 1]])
    rows = jnp.arange(ROWS) * parent_size + slot
    cols = jnp.arange(parent_size) * 4 + grid_at
    child_ids = jnp.arange(PIVOTS, ROWS * child_size)
    row_hit = maps[:, None, :] == rows[None, :, None]
    col_hit = maps[:, None, :] == cols[None, :, None]
    row_from = jnp.sum(jnp.where(row_hit, child_ids // child_size + 1, 0), 2) - 1
    col_from = jnp.sum(jnp.where(col_hit, child_ids // 4 + 1, 0), 2) - 1
    return jnp.concatenate([row_from, col_from], 1).astype(jnp.int32)


def column_targets(table, child_size, cube_at, grid_at, sources, count):
    mapping = table[(cube_at // child_size) ^ 1]
    child_ids = jnp.arange(count) * 4 + grid_at
    target = mapping[jnp.maximum(child_ids - PIVOTS, 0)]
    unused = jnp.argmax(sources[1, ROWS:] < 0)
    place = jnp.where(child_ids >= PIVOTS, target // 4, unused)
    valid = (child_ids >= PIVOTS) & (target >= PIVOTS)
    return place.astype(jnp.int32), valid.astype(jnp.int32)


def on_device(
    front_root, front_upper, front_middle, front_lower, place_upper, place_middle, place_lower
):
    cube_count = lax.axis_size("cube")
    cube_at = lax.axis_index("cube")
    grid_at = lax.axis_index("grid")
    stored = (front_root, front_upper, front_middle, front_lower)
    tables = (None, place_upper, place_middle, place_lower)
    factor_list = [None, None, None, None]
    rel = sources = update = None
    everyone = lambda s, g: True
    for depth in (3, 2, 1, 0):
        sub_size = cube_count >> depth
        half = sub_size // 2
        slot = cube_at % sub_size
        front = stored[depth]
        row_ids = jnp.arange(ROWS) * sub_size + slot
        col_ids = jnp.arange(sub_size) * 4 + grid_at
        info = jnp.concatenate([row_ids, col_ids]).astype(jnp.int32)
        children = ()
        if depth == 3:
            panel = front[:, :BS]
        else:
            got = shifted(rel, half, lambda s, g: g < 2, sub_size, cube_count)
            moves = jnp.concatenate([sources.reshape(-1), info])
            panel = pivot_panel(front, rel, got, moves, ())
            if depth == 1:
                own = update(after=(got,))
                other = shifted(own, half, everyone, sub_size, cube_count)
                children = (own, other)
            if depth == 0:
                own_early = update(after=(got,), span=(0, 1))
                other_early = shifted(own_early, half, everyone, sub_size, cube_count)
                arrived = (other_early,)
                from_early = jnp.where(sources[:, ROWS:] < EARLY, sources[:, ROWS:], -1)
                from_late = jnp.maximum(sources[0, ROWS:] - EARLY, -1)
                info = jnp.concatenate(
                    [
                        sources[0, :ROWS],
                        from_early[0],
                        sources[0, :ROWS],
                        from_late,
                        sources[1, :ROWS],
                        from_early[1],
                        info,
                    ]
                )
            else:
                info = moves
        if depth > 0:
            next_sources = child_sources(tables[depth], sub_size, cube_at, grid_at)
            info = jnp.concatenate([info, jnp.maximum(next_sources[0, ROWS : ROWS + 1], 0)])
        own_rows = both_pivots(panel, cube_count, grid_at)
        blocks = own_rows.reshape(ROWS, BS, WIDE)
        if depth == 3:
            pivots = pivot_rows_everywhere(blocks, cube_count, slot)
            panels = class_rows_direct(blocks, cube_count, cube_at, grid_at)
        else:
            share, pivots = quad_exchange(blocks, cube_count, grid_at)
            pivots = passed_on(pivots, 4, sub_size, cube_count, slot)
            zero = jnp.zeros((1,), jnp.int32)
        if depth == 1:
            pivots = passed_on(pivots, 8, sub_size, cube_count, slot)
        if depth in (2, 1):
            panels = gathered([share], zero, sub_size, cube_count, (pivots,))
        if depth == 2:
            own = update(after=(pivots,))
            other = shifted(own, half, everyone, sub_size, cube_count)
            children = (own, other)
        if depth == 0:
            load = copy_after(jnp.concatenate([share, pivots]), arrived)
            pieces = [load] + [
                shifted(load, bit, everyone, sub_size, cube_count) for bit in (8, 16, 24)
            ]
            plane = cube_at // 8
            pivots = pieces[0][BS:]
            for step in (1, 2, 3):
                pivots = jnp.where(plane == step, pieces[step][BS:], pivots)
            panels = gathered(pieces, plane.astype(jnp.int32).reshape(1), 8, cube_count, ())
            own_late = update(after=(load,), span=(1, 3))
            other_late = shifted(own_late, half, everyone, sub_size, cube_count)
            children = (own_early, own_late, other_early)
        low, inverse = pivot_factor(pivots)
        solved = dot_nt(own_rows, inverse)
        pivot_slot = jnp.minimum(slot, PIVOTS - 1)
        head = jnp.where(
            slot < PIVOTS, lax.dynamic_slice_in_dim(low, pivot_slot * BS, BS, 0), solved[:BS]
        )
        solved = jnp.concatenate([head, solved[BS:]])
        factor_list[depth] = solved
        update = functools.partial(update_front, front, children, solved, panels, inverse, info)
        if depth > 0:
            rel = update(single=True)
            sources = next_sources
    rest = update(is_root=True)
    count = sources.shape[1] // 2 - ROWS // 2
    place, valid = column_targets(tables[1], half, cube_at, grid_at, sources, count)
    row_part = jnp.concatenate([sources[1, :ROWS], row_ids]).astype(jnp.int32)
    rest = add_columns(
        rest, other_late, jnp.concatenate([row_part, place[EARLY:], valid[EARLY:]])
    )
    return (factor_list[0], factor_list[1], factor_list[2], factor_list[3], rest)


def solution(mesh):
    return jax.shard_map(
        on_device,
        mesh=mesh,
        in_specs=(
            P("cube", "grid"),
            P("cube", "grid"),
            P("cube", "grid"),
            P("cube", "grid"),
            P(),
            P(),
            P(),
        ),
        out_specs=(
            P("cube", None),
            P("cube", None),
            P("cube", None),
            P("cube", None),
            P("cube", "grid"),
        ),
        check_vma=False,
    )
```

```python
import functools

import jax
import jax.numpy as jnp
from jax import lax
from jax.experimental import pallas as pl
from jax.experimental.pallas import tpu as pltpu
from jax.sharding import PartitionSpec as P

BS = 128
PIVOTS = 2
ROWS = 4
WIDE = PIVOTS * BS
HIGHEST = lax.Precision.HIGHEST
EARLY = 4
GROUP = 8
VMEM_LIMIT = 48 * 1024 * 1024


def dot_nn(a, b):
    return jnp.dot(a, b, precision=HIGHEST, preferred_element_type=jnp.float32)


def dot_nt(a, b):
    return lax.dot_general(
        a, b, (((1,), (1,)), ((), ())), precision=HIGHEST, preferred_element_type=jnp.float32
    )


def factor_block(block):
    n = BS
    rows = lax.broadcasted_iota(jnp.int32, (n, n), 0)
    eye = (rows == lax.broadcasted_iota(jnp.int32, (n, n), 1)).astype(jnp.float32)
    parts = [block, eye]
    for j in range(0, n, GROUP):
        cols = [jnp.broadcast_to(parts[0][:, j + t : j + t + 1], (n, n)) for t in range(GROUP)]
        mults = []
        for t in range(GROUP):
            col = cols[t]
            mult = jnp.where(rows > j + t, col * (1.0 / col[j + t : j + t + 1]), 0.0)
            for u in range(t + 1, GROUP):
                cols[u] = cols[u] - mult * col[j + u : j + u + 1]
            mults.append(mult)
        done = []
        for part in parts:
            total, heads = part, []
            for t in range(GROUP):
                head = part[j + t : j + t + 1]
                for u in range(t):
                    head = head - mults[u][j + t : j + t + 1] * heads[u]
                heads.append(head)
                total = total - mults[t] * head
            done.append(total)
        parts = done
    diag = jnp.sum(jnp.where(eye > 0, parts[0], 0.0), 1, keepdims=True)
    scale = lax.rsqrt(diag)
    return (parts[0] * scale).T, parts[1] * scale


def pivot_kernel(rows_ref, low_ref, inv_ref):
    c0, i0 = factor_block(rows_ref[:BS, :BS])
    k10 = dot_nt(rows_ref[BS:, :BS], i0)
    c1, i1 = factor_block(rows_ref[BS:, BS:] - dot_nt(k10, k10))
    lane = lax.broadcasted_iota(jnp.int32, (BS, BS), 1)
    sub = lax.broadcasted_iota(jnp.int32, (BS, BS), 0)
    low = lane <= sub
    zero = jnp.zeros((BS, BS), jnp.float32)
    low_ref[:BS, :BS] = jnp.where(low, c0, 0.0)
    low_ref[:BS, BS:] = zero
    low_ref[BS:, :BS] = k10
    low_ref[BS:, BS:] = jnp.where(low, c1, 0.0)
    inv_ref[:BS, :BS] = i0
    inv_ref[:BS, BS:] = zero
    inv_ref[BS:, :BS] = -dot_nn(i1, dot_nn(k10, i0))
    inv_ref[BS:, BS:] = i1


def pivot_factor(pivot_rows):
    shape = jax.ShapeDtypeStruct((WIDE, WIDE), jnp.float32)
    whole = pl.BlockSpec(memory_space=pltpu.VMEM)
    return pl.pallas_call(
        pivot_kernel,
        out_shape=[shape, shape],
        in_specs=[whole],
        out_specs=[whole, whole],
        compiler_params=pltpu.CompilerParams(vmem_limit_bytes=VMEM_LIMIT),
        name="pivot_factor",
    )(pivot_rows)


ANY = pl.BlockSpec(memory_space=pl.ANY)


def parts_of(a):
    high = a.astype(jnp.bfloat16)
    return high, (a - high.astype(jnp.float32)).astype(jnp.bfloat16)


def split_left(a):
    high, low = parts_of(a)
    return jnp.concatenate([high, low, high], 1)


def split_right(a):
    high, low = parts_of(a)
    return jnp.concatenate([high, high, low], 0)


def dot_split(left, right):
    return jnp.dot(left, right, preferred_element_type=jnp.float32)


def update_kernel(cols, per, children, is_root, col_of, place_of, info_ref, *refs):
    front_ref, refs = refs[0], refs[1:]
    child_refs, refs = refs[: children * per], refs[children * per :]
    key_ref, panel_ref, inv_ref = refs[:3]
    out_ref, key_split, inv_split = refs[-3:]
    step = pl.program_id(0)

    @pl.when(step == 0)
    def _():
        key_split[...] = split_left(key_ref[...])
        inv_split[...] = split_left(inv_ref[...])

    panel = jnp.concatenate([panel_ref[place_of(t)] for t in range(per)], 1)
    solved = dot_split(inv_split[...], split_right(panel))
    terms = dot_split(key_split[...], split_right(solved))
    width = ROWS + cols
    places = children * width
    for t in range(per):
        at = col_of(step, info_ref) * per + t
        lanes = slice(t * BS, (t + 1) * BS)
        for r in range(ROWS):
            span = slice(r * BS, (r + 1) * BS)
            block = front_ref[span, lanes] - terms[span, lanes]
            for which in range(children):
                source = info_ref[which * width + r]
                present = (source >= 0) & (info_ref[which * width + ROWS + at] >= 0)
                taken = child_refs[which * per + t][pl.ds(jnp.maximum(source, 0) * BS, BS), :]
                block = block + jnp.where(present, taken, 0.0)
            if is_root:
                keep = (info_ref[places + r] >= PIVOTS) & (info_ref[places + ROWS + at] >= PIVOTS)
                block = jnp.where(keep, block, 0.0)
            out_ref[span, lanes] = block


def update_front(front, children, key, panels, inverse, info, is_root=False, single=False, span=None, after=()):
    cols = front.shape[1] // BS
    width = ROWS + cols
    height = ROWS * BS
    per = 1 if single else 4
    rel_at = (len(children) + 1) * width
    first, steps = (0, 1) if single else span or (0, cols // per)
    if single:
        col_of = lambda c, info: info[rel_at]
    else:
        col_of = lambda c, info: c + first
    outer, _, planes = panels.shape[:3]
    place_of = lambda t: (t % outer, t // outer, 0)
    if single:
        panel_dims = (1, 1, 1)
        panel_at = lambda c, info: (lax.rem(col_of(c, info), outer), lax.div(col_of(c, info), outer), 0, 0, 0)
    elif planes == 1:
        panel_dims = (outer, per // outer, 1)
        panel_at = lambda c, info: (0, c + first, 0, 0, 0)
    else:
        panel_dims = (outer, 1, per // outer)
        runs = planes * outer // per
        panel_at = lambda c, info: (0, lax.div(c, runs), lax.rem(c, runs), 0, 0)
        place_of = lambda t: (t % outer, 0, t // outer)

    column = pl.BlockSpec((height, per * BS), lambda c, info: (0, col_of(c, info)))
    specs, args = [column], [front]
    for which, child in enumerate(children):
        for t in range(per):
            specs.append(
                pl.BlockSpec(
                    (height, BS),
                    lambda c, info, which=which, t=t: (
                        0,
                        jnp.maximum(info[which * width + ROWS + col_of(c, info) * per + t], 0),
                    ),
                )
            )
            args.append(child)
    specs += [
        pl.BlockSpec((height, WIDE), lambda c, info: (0, 0)),
        pl.BlockSpec((*panel_dims, WIDE, BS), panel_at),
        pl.BlockSpec((WIDE, WIDE), lambda c, info: (0, 0)),
    ] + [ANY] * len(after)
    args += [key, panels, inverse, *after]
    return pl.pallas_call(
        functools.partial(update_kernel, cols, per, len(children), is_root, col_of, place_of),
        out_shape=jax.ShapeDtypeStruct((height, steps * per * BS), jnp.float32),
        grid_spec=pltpu.PrefetchScalarGridSpec(
            num_scalar_prefetch=1,
            grid=(steps,),
            in_specs=specs,
            out_specs=pl.BlockSpec((height, per * BS), lambda c, info: (0, c)),
            scratch_shapes=[
                pltpu.VMEM((height, 3 * WIDE), jnp.bfloat16),
                pltpu.VMEM((WIDE, 3 * WIDE), jnp.bfloat16),
            ],
        ),
        compiler_params=pltpu.CompilerParams(vmem_limit_bytes=VMEM_LIMIT),
        cost_estimate=pl.CostEstimate(
            flops=2 * height * WIDE * steps * per * BS * 2,
            bytes_accessed=16 * height * steps * per * BS,
            transcendentals=0,
        ),
        name="update_front",
    )(info, *args)


def panel_kernel(width, info_ref, front_ref, own_ref, other_ref, *refs):
    out_ref = refs[-1]
    for r in range(ROWS):
        block = front_ref[r * BS : (r + 1) * BS, :]
        for which, child_ref in ((0, own_ref), (1, other_ref)):
            source = info_ref[which * width + r]
            present = (source >= 0) & (info_ref[which * width + ROWS] >= 0)
            taken = child_ref[pl.ds(jnp.maximum(source, 0) * BS, BS), :]
            block = block + jnp.where(present, taken, 0.0)
        out_ref[r * BS : (r + 1) * BS, :] = block


def pivot_panel(front, own, other, info, after):
    piece = pl.BlockSpec((ROWS * BS, BS), lambda c, info: (0, 0))
    return pl.pallas_call(
        functools.partial(panel_kernel, ROWS + front.shape[1] // BS),
        out_shape=jax.ShapeDtypeStruct((ROWS * BS, BS), jnp.float32),
        grid_spec=pltpu.PrefetchScalarGridSpec(
            num_scalar_prefetch=1,
            grid=(1,),
            in_specs=[piece] * 3 + [ANY] * len(after),
            out_specs=piece,
        ),
        name="pivot_panel",
    )(info, front, own, other, *after)


def add_kernel(count, info_ref, front_ref, child_ref, out_ref):
    valid = info_ref[2 * ROWS + count + pl.program_id(0)] > 0
    for r in range(ROWS):
        span = slice(r * BS, (r + 1) * BS)
        source = info_ref[r]
        present = valid & (source >= 0) & (info_ref[ROWS + r] >= PIVOTS)
        taken = child_ref[pl.ds(jnp.maximum(source, 0) * BS, BS), :]
        out_ref[span, :] = front_ref[span, :] + jnp.where(present, taken, 0.0)


def add_columns(front, child, info):
    count = child.shape[1] // BS
    target = pl.BlockSpec((ROWS * BS, BS), lambda c, info: (0, info[2 * ROWS + c]))
    return pl.pallas_call(
        functools.partial(add_kernel, count),
        out_shape=jax.ShapeDtypeStruct(front.shape, jnp.float32),
        grid_spec=pltpu.PrefetchScalarGridSpec(
            num_scalar_prefetch=1,
            grid=(count,),
            in_specs=[target, pl.BlockSpec((ROWS * BS, BS), lambda c, info: (0, c))],
            out_specs=target,
        ),
        input_output_aliases={1: 0},
        compiler_params=pltpu.CompilerParams(vmem_limit_bytes=VMEM_LIMIT),
        name="add_columns",
    )(info, front, child)


def copy_kernel(in_ref, *refs):
    refs[-1][...] = in_ref[...]


def copy_after(array, after, low=0, high=None):
    rows, cols = array.shape
    high = cols if high is None else high
    wide = WIDE
    return pl.pallas_call(
        copy_kernel,
        out_shape=jax.ShapeDtypeStruct((rows, high - low), jnp.float32),
        grid=((high - low) // wide,),
        in_specs=[pl.BlockSpec((rows, wide), lambda c: (0, c + low // wide))] + [ANY] * len(after),
        out_specs=pl.BlockSpec((rows, wide), lambda c: (0, c)),
        name="copy_after",
    )(array, *after)


def spread_kernel(count, at_ref, *refs):
    pieces, out_ref, scratch = refs[:count], refs[-2], refs[-1]

    @pl.when(pl.program_id(0) == 0)
    def _():
        for step in range(count):
            turned = pieces[step][...].T
            for place in range(count):

                @pl.when(at_ref[0] == place ^ step)
                def _():
                    scratch[place] = turned

    for t in range(out_ref.shape[0]):
        out_ref[t] = scratch[...]


def spread(pieces, at, copies, after):
    count = len(pieces)
    shape = (count, WIDE, BS)
    each = 4 if count == 1 else 2
    return pl.pallas_call(
        functools.partial(spread_kernel, count),
        out_shape=jax.ShapeDtypeStruct((copies, *shape), jnp.float32),
        grid_spec=pltpu.PrefetchScalarGridSpec(
            num_scalar_prefetch=1,
            grid=(copies // each,),
            in_specs=[pl.BlockSpec((BS, WIDE), lambda c, at: (0, 0))] * count + [ANY] * len(after),
            out_specs=pl.BlockSpec((each, *shape), lambda c, at: (c, 0, 0, 0)),
            scratch_shapes=[pltpu.VMEM(shape, jnp.float32)],
        ),
        compiler_params=pltpu.CompilerParams(vmem_limit_bytes=VMEM_LIMIT),
        name="spread",
    )(at, *pieces, *after)


def send(block, route):
    pairs = [(a[0] * 4 + a[1], b[0] * 4 + b[1]) for a, b in route]
    return lax.ppermute(block, ("cube", "grid"), pairs)


def both_pivots(piece, cube_count, grid_at):
    near = send(piece, [((s, g), (s, g ^ 1)) for s in range(cube_count) for g in (0, 1)])
    far = send(piece, [((s, g), (s, g ^ 2)) for s in range(cube_count) for g in (0, 1)])
    cross = send(far, [((s, g), (s, g ^ 1)) for s in range(cube_count) for g in (2, 3)])
    mine = jnp.where(grid_at < 2, piece, far)
    mate = jnp.where(grid_at < 2, near, cross)
    first = jnp.where(grid_at % 2 == 0, mine, mate)
    second = jnp.where(grid_at % 2 == 0, mate, mine)
    return jnp.concatenate([first, second], -1)


def shifted(block, bit, sources, sub_size, cube_count, grids=None):
    route = []
    for base in range(0, cube_count, sub_size):
        for s in range(sub_size):
            for g in range(4):
                if sources(s, g):
                    route.append(((base + s, g), (base + (s ^ bit), g)))
    return send(block, route)


def quad_exchange(own_rows, cube_count, grid_at):
    load = jnp.stack([own_rows, jnp.broadcast_to(own_rows[:1], own_rows.shape)], 1)
    quads = [[b + i for i in range(4)] for b in range(0, cube_count, 4)]
    got = lax.all_to_all(load, "cube", 0, 0, axis_index_groups=quads)
    share = lax.dynamic_index_in_dim(got[:, 0], grid_at, 0, keepdims=False)
    return share, got[:PIVOTS, 1].reshape(WIDE, WIDE)


def passed_on(both, known, sub_size, cube_count, slot):
    moved = shifted(both, known, lambda s, g: s < known, sub_size, cube_count)
    return jnp.where(slot < known, both, moved)


def class_rows_direct(own_rows, cube_count, cube_at, grid_at):
    total = jnp.where(cube_at % 4 == grid_at, own_rows, 0.0)
    for step in (1, 2, 3):
        total = total + shifted(own_rows, step, lambda s, g: s == g, 4, cube_count)
    return total.transpose(0, 2, 1).reshape(ROWS, 1, 1, WIDE, BS)


def gathered(pieces, at, group, cube_count, after):
    groups = None
    if group < cube_count:
        groups = [[b + i for i in range(group)] for b in range(0, cube_count, group)]
    everything = lax.all_to_all(
        spread(pieces, at, group, after), "cube", 0, 0, axis_index_groups=groups
    )
    return everything.reshape(group // 4, 4, len(pieces), WIDE, BS)


def pivot_rows_everywhere(own_rows, cube_count, slot):
    row = own_rows[0]
    got = shifted(row, 1, lambda s, g: s < 2, 4, cube_count)
    both = jnp.where(slot == 0, jnp.concatenate([row, got]), jnp.concatenate([got, row]))
    return passed_on(both, 2, 4, cube_count, slot)


def child_sources(table, child_size, cube_at, grid_at):
    parent_size = 2 * child_size
    slot = cube_at % parent_size
    front = cube_at // child_size
    maps = jnp.stack([table[front], table[front ^ 1]])
    rows = jnp.arange(ROWS) * parent_size + slot
    cols = jnp.arange(parent_size) * 4 + grid_at
    child_ids = jnp.arange(PIVOTS, ROWS * child_size)
    row_hit = maps[:, None, :] == rows[None, :, None]
    col_hit = maps[:, None, :] == cols[None, :, None]
    row_from = jnp.sum(jnp.where(row_hit, child_ids // child_size + 1, 0), 2) - 1
    col_from = jnp.sum(jnp.where(col_hit, child_ids // 4 + 1, 0), 2) - 1
    return jnp.concatenate([row_from, col_from], 1).astype(jnp.int32)


def column_targets(table, child_size, cube_at, grid_at, sources, count):
    mapping = table[(cube_at // child_size) ^ 1]
    child_ids = jnp.arange(count) * 4 + grid_at
    target = mapping[jnp.maximum(child_ids - PIVOTS, 0)]
    unused = jnp.argmax(sources[1, ROWS:] < 0)
    place = jnp.where(child_ids >= PIVOTS, target // 4, unused)
    valid = (child_ids >= PIVOTS) & (target >= PIVOTS)
    return place.astype(jnp.int32), valid.astype(jnp.int32)


def on_device(
    front_root, front_upper, front_middle, front_lower, place_upper, place_middle, place_lower
):
    cube_count = lax.axis_size("cube")
    cube_at = lax.axis_index("cube")
    grid_at = lax.axis_index("grid")
    stored = (front_root, front_upper, front_middle, front_lower)
    tables = (None, place_upper, place_middle, place_lower)
    factor_list = [None, None, None, None]
    rel = sources = update = None
    everyone = lambda s, g: True
    for depth in (3, 2, 1, 0):
        sub_size = cube_count >> depth
        half = sub_size // 2
        slot = cube_at % sub_size
        front = stored[depth]
        row_ids = jnp.arange(ROWS) * sub_size + slot
        col_ids = jnp.arange(sub_size) * 4 + grid_at
        info = jnp.concatenate([row_ids, col_ids]).astype(jnp.int32)
        children = ()
        if depth == 3:
            panel = front[:, :BS]
        else:
            got = shifted(rel, half, lambda s, g: g < 2, sub_size, cube_count)
            moves = jnp.concatenate([sources.reshape(-1), info])
            panel = pivot_panel(front, rel, got, moves, ())
            if depth == 1:
                own = update(after=(got,))
                other = shifted(own, half, everyone, sub_size, cube_count)
                children = (own, other)
            if depth == 0:
                own_early = update(after=(got,), span=(0, 1))
                other_early = shifted(own_early, half, everyone, sub_size, cube_count)
                arrived = (other_early,)
                from_early = jnp.where(sources[:, ROWS:] < EARLY, sources[:, ROWS:], -1)
                from_late = jnp.maximum(sources[0, ROWS:] - EARLY, -1)
                info = jnp.concatenate(
                    [
                        sources[0, :ROWS],
                        from_early[0],
                        sources[0, :ROWS],
                        from_late,
                        sources[1, :ROWS],
                        from_early[1],
                        info,
                    ]
                )
            else:
                info = moves
        if depth > 0:
            next_sources = child_sources(tables[depth], sub_size, cube_at, grid_at)
            info = jnp.concatenate([info, jnp.maximum(next_sources[0, ROWS : ROWS + 1], 0)])
        own_rows = both_pivots(panel, cube_count, grid_at)
        blocks = own_rows.reshape(ROWS, BS, WIDE)
        if depth == 3:
            pivots = pivot_rows_everywhere(blocks, cube_count, slot)
            panels = class_rows_direct(blocks, cube_count, cube_at, grid_at)
        else:
            share, pivots = quad_exchange(blocks, cube_count, grid_at)
            pivots = passed_on(pivots, 4, sub_size, cube_count, slot)
            zero = jnp.zeros((1,), jnp.int32)
        if depth == 1:
            pivots = passed_on(copy_after(pivots, (other,)), 8, sub_size, cube_count, slot)
        if depth in (2, 1):
            panels = gathered([share], zero, sub_size, cube_count, (pivots,) if depth == 1 else ())
        if depth == 2:
            own = update(after=(pivots,))
            other = shifted(own, half, everyone, sub_size, cube_count)
            children = (own, other)
        if depth == 0:
            load = copy_after(jnp.concatenate([share, pivots]), arrived)
            pieces = [load] + [
                shifted(load, bit, everyone, sub_size, cube_count) for bit in (8, 16, 24)
            ]
            plane = cube_at // 8
            pivots = pieces[0][BS:]
            for step in (1, 2, 3):
                pivots = jnp.where(plane == step, pieces[step][BS:], pivots)
            own_late = update(after=(load,), span=(1, 3))
            panels = gathered(
                pieces, plane.astype(jnp.int32).reshape(1), 8, cube_count, (own_late,)
            )
            other_late = shifted(own_late, half, everyone, sub_size, cube_count)
            children = (own_early, own_late, other_early)
        low, inverse = pivot_factor(pivots)
        solved = dot_nt(own_rows, inverse)
        pivot_slot = jnp.minimum(slot, PIVOTS - 1)
        head = jnp.where(
            slot < PIVOTS, lax.dynamic_slice_in_dim(low, pivot_slot * BS, BS, 0), solved[:BS]
        )
        solved = jnp.concatenate([head, solved[BS:]])
        factor_list[depth] = solved
        update = functools.partial(update_front, front, children, solved, panels, inverse, info)
        if depth > 0:
            rel = update(single=True)
            sources = next_sources
    rest = update(is_root=True)
    count = sources.shape[1] // 2 - ROWS // 2
    place, valid = column_targets(tables[1], half, cube_at, grid_at, sources, count)
    row_part = jnp.concatenate([sources[1, :ROWS], row_ids]).astype(jnp.int32)
    rest = add_columns(
        rest, other_late, jnp.concatenate([row_part, place[EARLY:], valid[EARLY:]])
    )
    return (factor_list[0], factor_list[1], factor_list[2], factor_list[3], rest)


def solution(mesh):
    return jax.shard_map(
        on_device,
        mesh=mesh,
        in_specs=(
            P("cube", "grid"),
            P("cube", "grid"),
            P("cube", "grid"),
            P("cube", "grid"),
            P(),
            P(),
            P(),
        ),
        out_specs=(
            P("cube", None),
            P("cube", None),
            P("cube", None),
            P("cube", None),
            P("cube", "grid"),
        ),
        check_vma=False,
    )
```

```python
import functools

import jax
import jax.numpy as jnp
from jax import lax
from jax.experimental import pallas as pl
from jax.experimental.pallas import tpu as pltpu
from jax.sharding import PartitionSpec as P

BS = 128
PIVOTS = 2
ROWS = 4
WIDE = PIVOTS * BS
HIGHEST = lax.Precision.HIGHEST
EARLY = 4
GROUP = 8
VMEM_LIMIT = 48 * 1024 * 1024


def dot_nn(a, b):
    return jnp.dot(a, b, precision=HIGHEST, preferred_element_type=jnp.float32)


def dot_nt(a, b):
    return lax.dot_general(
        a, b, (((1,), (1,)), ((), ())), precision=HIGHEST, preferred_element_type=jnp.float32
    )


def factor_block(block):
    n = BS
    rows = lax.broadcasted_iota(jnp.int32, (n, n), 0)
    eye = (rows == lax.broadcasted_iota(jnp.int32, (n, n), 1)).astype(jnp.float32)
    parts = [block, eye]
    for j in range(0, n, GROUP):
        cols = [jnp.broadcast_to(parts[0][:, j + t : j + t + 1], (n, n)) for t in range(GROUP)]
        mults = []
        for t in range(GROUP):
            col = cols[t]
            mult = jnp.where(rows > j + t, col * (1.0 / col[j + t : j + t + 1]), 0.0)
            for u in range(t + 1, GROUP):
                cols[u] = cols[u] - mult * col[j + u : j + u + 1]
            mults.append(mult)
        done = []
        for part in parts:
            total, heads = part, []
            for t in range(GROUP):
                head = part[j + t : j + t + 1]
                for u in range(t):
                    head = head - mults[u][j + t : j + t + 1] * heads[u]
                heads.append(head)
                total = total - mults[t] * head
            done.append(total)
        parts = done
    diag = jnp.sum(jnp.where(eye > 0, parts[0], 0.0), 1, keepdims=True)
    scale = lax.rsqrt(diag)
    return (parts[0] * scale).T, parts[1] * scale


def pivot_kernel(rows_ref, low_ref, inv_ref):
    c0, i0 = factor_block(rows_ref[:BS, :BS])
    k10 = dot_nt(rows_ref[BS:, :BS], i0)
    c1, i1 = factor_block(rows_ref[BS:, BS:] - dot_nt(k10, k10))
    lane = lax.broadcasted_iota(jnp.int32, (BS, BS), 1)
    sub = lax.broadcasted_iota(jnp.int32, (BS, BS), 0)
    low = lane <= sub
    zero = jnp.zeros((BS, BS), jnp.float32)
    low_ref[:BS, :BS] = jnp.where(low, c0, 0.0)
    low_ref[:BS, BS:] = zero
    low_ref[BS:, :BS] = k10
    low_ref[BS:, BS:] = jnp.where(low, c1, 0.0)
    inv_ref[:BS, :BS] = i0
    inv_ref[:BS, BS:] = zero
    inv_ref[BS:, :BS] = -dot_nn(i1, dot_nn(k10, i0))
    inv_ref[BS:, BS:] = i1


def pivot_factor(pivot_rows):
    shape = jax.ShapeDtypeStruct((WIDE, WIDE), jnp.float32)
    whole = pl.BlockSpec(memory_space=pltpu.VMEM)
    return pl.pallas_call(
        pivot_kernel,
        out_shape=[shape, shape],
        in_specs=[whole],
        out_specs=[whole, whole],
        compiler_params=pltpu.CompilerParams(vmem_limit_bytes=VMEM_LIMIT),
        name="pivot_factor",
    )(pivot_rows)


ANY = pl.BlockSpec(memory_space=pl.ANY)


def parts_of(a):
    high = a.astype(jnp.bfloat16)
    return high, (a - high.astype(jnp.float32)).astype(jnp.bfloat16)


def split_left(a):
    high, low = parts_of(a)
    return jnp.concatenate([high, low, high], 1)


def split_right(a):
    high, low = parts_of(a)
    return jnp.concatenate([high, high, low], 0)


def dot_split(left, right):
    return jnp.dot(left, right, preferred_element_type=jnp.float32)


def update_kernel(cols, per, children, is_root, col_of, place_of, info_ref, *refs):
    front_ref, refs = refs[0], refs[1:]
    child_refs, refs = refs[: children * per], refs[children * per :]
    key_ref, panel_ref, inv_ref = refs[:3]
    out_ref, key_split, inv_split = refs[-3:]
    step = pl.program_id(0)

    @pl.when(step == 0)
    def _():
        key_split[...] = split_left(key_ref[...])
        inv_split[...] = split_left(inv_ref[...])

    panel = jnp.concatenate([panel_ref[place_of(t)] for t in range(per)], 1)
    solved = dot_split(inv_split[...], split_right(panel))
    terms = dot_split(key_split[...], split_right(solved))
    width = ROWS + cols
    places = children * width
    for t in range(per):
        at = col_of(step, info_ref) * per + t
        lanes = slice(t * BS, (t + 1) * BS)
        for r in range(ROWS):
            span = slice(r * BS, (r + 1) * BS)
            block = front_ref[span, lanes] - terms[span, lanes]
            for which in range(children):
                source = info_ref[which * width + r]
                present = (source >= 0) & (info_ref[which * width + ROWS + at] >= 0)
                taken = child_refs[which * per + t][pl.ds(jnp.maximum(source, 0) * BS, BS), :]
                block = block + jnp.where(present, taken, 0.0)
            if is_root:
                keep = (info_ref[places + r] >= PIVOTS) & (info_ref[places + ROWS + at] >= PIVOTS)
                block = jnp.where(keep, block, 0.0)
            out_ref[span, lanes] = block


def update_front(front, children, key, panels, inverse, info, is_root=False, single=False, span=None, after=()):
    cols = front.shape[1] // BS
    width = ROWS + cols
    height = ROWS * BS
    per = 1 if single else 4
    rel_at = (len(children) + 1) * width
    first, steps = (0, 1) if single else span or (0, cols // per)
    if single:
        col_of = lambda c, info: info[rel_at]
    else:
        col_of = lambda c, info: c + first
    outer, _, planes = panels.shape[:3]
    place_of = lambda t: (t % outer, t // outer, 0)
    if single:
        panel_dims = (1, 1, 1)
        panel_at = lambda c, info: (lax.rem(col_of(c, info), outer), lax.div(col_of(c, info), outer), 0, 0, 0)
    elif planes == 1:
        panel_dims = (outer, per // outer, 1)
        panel_at = lambda c, info: (0, c + first, 0, 0, 0)
    else:
        panel_dims = (outer, 1, per // outer)
        runs = planes * outer // per
        panel_at = lambda c, info: (0, lax.div(c, runs), lax.rem(c, runs), 0, 0)
        place_of = lambda t: (t % outer, 0, t // outer)

    column = pl.BlockSpec((height, per * BS), lambda c, info: (0, col_of(c, info)))
    specs, args = [column], [front]
    for which, child in enumerate(children):
        for t in range(per):
            specs.append(
                pl.BlockSpec(
                    (height, BS),
                    lambda c, info, which=which, t=t: (
                        0,
                        jnp.maximum(info[which * width + ROWS + col_of(c, info) * per + t], 0),
                    ),
                )
            )
            args.append(child)
    specs += [
        pl.BlockSpec((height, WIDE), lambda c, info: (0, 0)),
        pl.BlockSpec((*panel_dims, WIDE, BS), panel_at),
        pl.BlockSpec((WIDE, WIDE), lambda c, info: (0, 0)),
    ] + [ANY] * len(after)
    args += [key, panels, inverse, *after]
    return pl.pallas_call(
        functools.partial(update_kernel, cols, per, len(children), is_root, col_of, place_of),
        out_shape=jax.ShapeDtypeStruct((height, steps * per * BS), jnp.float32),
        grid_spec=pltpu.PrefetchScalarGridSpec(
            num_scalar_prefetch=1,
            grid=(steps,),
            in_specs=specs,
            out_specs=pl.BlockSpec((height, per * BS), lambda c, info: (0, c)),
            scratch_shapes=[
                pltpu.VMEM((height, 3 * WIDE), jnp.bfloat16),
                pltpu.VMEM((WIDE, 3 * WIDE), jnp.bfloat16),
            ],
        ),
        compiler_params=pltpu.CompilerParams(vmem_limit_bytes=VMEM_LIMIT),
        cost_estimate=pl.CostEstimate(
            flops=2 * height * WIDE * steps * per * BS * 2,
            bytes_accessed=16 * height * steps * per * BS,
            transcendentals=0,
        ),
        name="update_front",
    )(info, *args)


def panel_kernel(width, info_ref, front_ref, own_ref, other_ref, *refs):
    out_ref = refs[-1]
    for r in range(ROWS):
        block = front_ref[r * BS : (r + 1) * BS, :]
        for which, child_ref in ((0, own_ref), (1, other_ref)):
            source = info_ref[which * width + r]
            present = (source >= 0) & (info_ref[which * width + ROWS] >= 0)
            taken = child_ref[pl.ds(jnp.maximum(source, 0) * BS, BS), :]
            block = block + jnp.where(present, taken, 0.0)
        out_ref[r * BS : (r + 1) * BS, :] = block


def pivot_panel(front, own, other, info, after):
    piece = pl.BlockSpec((ROWS * BS, BS), lambda c, info: (0, 0))
    return pl.pallas_call(
        functools.partial(panel_kernel, ROWS + front.shape[1] // BS),
        out_shape=jax.ShapeDtypeStruct((ROWS * BS, BS), jnp.float32),
        grid_spec=pltpu.PrefetchScalarGridSpec(
            num_scalar_prefetch=1,
            grid=(1,),
            in_specs=[piece] * 3 + [ANY] * len(after),
            out_specs=piece,
        ),
        name="pivot_panel",
    )(info, front, own, other, *after)


def add_kernel(count, info_ref, front_ref, child_ref, out_ref):
    valid = info_ref[2 * ROWS + count + pl.program_id(0)] > 0
    for r in range(ROWS):
        span = slice(r * BS, (r + 1) * BS)
        source = info_ref[r]
        present = valid & (source >= 0) & (info_ref[ROWS + r] >= PIVOTS)
        taken = child_ref[pl.ds(jnp.maximum(source, 0) * BS, BS), :]
        out_ref[span, :] = front_ref[span, :] + jnp.where(present, taken, 0.0)


def add_columns(front, child, info):
    count = child.shape[1] // BS
    target = pl.BlockSpec((ROWS * BS, BS), lambda c, info: (0, info[2 * ROWS + c]))
    return pl.pallas_call(
        functools.partial(add_kernel, count),
        out_shape=jax.ShapeDtypeStruct(front.shape, jnp.float32),
        grid_spec=pltpu.PrefetchScalarGridSpec(
            num_scalar_prefetch=1,
            grid=(count,),
            in_specs=[target, pl.BlockSpec((ROWS * BS, BS), lambda c, info: (0, c))],
            out_specs=target,
        ),
        input_output_aliases={1: 0},
        compiler_params=pltpu.CompilerParams(vmem_limit_bytes=VMEM_LIMIT),
        name="add_columns",
    )(info, front, child)


def copy_kernel(in_ref, *refs):
    refs[-1][...] = in_ref[...]


def copy_after(array, after, low=0, high=None):
    rows, cols = array.shape
    high = cols if high is None else high
    wide = WIDE
    return pl.pallas_call(
        copy_kernel,
        out_shape=jax.ShapeDtypeStruct((rows, high - low), jnp.float32),
        grid=((high - low) // wide,),
        in_specs=[pl.BlockSpec((rows, wide), lambda c: (0, c + low // wide))] + [ANY] * len(after),
        out_specs=pl.BlockSpec((rows, wide), lambda c: (0, c)),
        name="copy_after",
    )(array, *after)


def spread_kernel(count, at_ref, *refs):
    pieces, out_ref, scratch = refs[:count], refs[-2], refs[-1]

    @pl.when(pl.program_id(0) == 0)
    def _():
        for step in range(count):
            turned = pieces[step][...].T
            for place in range(count):

                @pl.when(at_ref[0] == place ^ step)
                def _():
                    scratch[place] = turned

    for t in range(out_ref.shape[0]):
        out_ref[t] = scratch[...]


def spread(pieces, at, copies, after):
    count = len(pieces)
    shape = (count, WIDE, BS)
    each = 4 if count == 1 else 2
    return pl.pallas_call(
        functools.partial(spread_kernel, count),
        out_shape=jax.ShapeDtypeStruct((copies, *shape), jnp.float32),
        grid_spec=pltpu.PrefetchScalarGridSpec(
            num_scalar_prefetch=1,
            grid=(copies // each,),
            in_specs=[pl.BlockSpec((BS, WIDE), lambda c, at: (0, 0))] * count + [ANY] * len(after),
            out_specs=pl.BlockSpec((each, *shape), lambda c, at: (c, 0, 0, 0)),
            scratch_shapes=[pltpu.VMEM(shape, jnp.float32)],
        ),
        compiler_params=pltpu.CompilerParams(vmem_limit_bytes=VMEM_LIMIT),
        name="spread",
    )(at, *pieces, *after)


def send(block, route):
    pairs = [(a[0] * 4 + a[1], b[0] * 4 + b[1]) for a, b in route]
    return lax.ppermute(block, ("cube", "grid"), pairs)


def both_pivots(piece, cube_count, grid_at):
    near = send(piece, [((s, g), (s, g ^ 1)) for s in range(cube_count) for g in (0, 1)])
    far = send(piece, [((s, g), (s, g ^ 2)) for s in range(cube_count) for g in (0, 1)])
    cross = send(far, [((s, g), (s, g ^ 1)) for s in range(cube_count) for g in (2, 3)])
    mine = jnp.where(grid_at < 2, piece, far)
    mate = jnp.where(grid_at < 2, near, cross)
    first = jnp.where(grid_at % 2 == 0, mine, mate)
    second = jnp.where(grid_at % 2 == 0, mate, mine)
    return jnp.concatenate([first, second], -1)


def shifted(block, bit, sources, sub_size, cube_count, grids=None):
    route = []
    for base in range(0, cube_count, sub_size):
        for s in range(sub_size):
            for g in range(4):
                if sources(s, g):
                    route.append(((base + s, g), (base + (s ^ bit), g)))
    return send(block, route)


def quad_exchange(own_rows, cube_count, grid_at):
    load = jnp.stack([own_rows, jnp.broadcast_to(own_rows[:1], own_rows.shape)], 1)
    quads = [[b + i for i in range(4)] for b in range(0, cube_count, 4)]
    got = lax.all_to_all(load, "cube", 0, 0, axis_index_groups=quads)
    share = lax.dynamic_index_in_dim(got[:, 0], grid_at, 0, keepdims=False)
    return share, got[:PIVOTS, 1].reshape(WIDE, WIDE)


def passed_on(both, known, sub_size, cube_count, slot):
    moved = shifted(both, known, lambda s, g: s < known, sub_size, cube_count)
    return jnp.where(slot < known, both, moved)


def class_rows_direct(own_rows, cube_count, cube_at, grid_at):
    total = jnp.where(cube_at % 4 == grid_at, own_rows, 0.0)
    for step in (1, 2, 3):
        total = total + shifted(own_rows, step, lambda s, g: s == g, 4, cube_count)
    return total.transpose(0, 2, 1).reshape(ROWS, 1, 1, WIDE, BS)


def gathered(pieces, at, group, cube_count, after):
    groups = None
    if group < cube_count:
        groups = [[b + i for i in range(group)] for b in range(0, cube_count, group)]
    everything = lax.all_to_all(
        spread(pieces, at, group, after), "cube", 0, 0, axis_index_groups=groups
    )
    return everything.reshape(group // 4, 4, len(pieces), WIDE, BS)


def pivot_rows_everywhere(own_rows, cube_count, slot):
    row = own_rows[0]
    got = shifted(row, 1, lambda s, g: s < 2, 4, cube_count)
    both = jnp.where(slot == 0, jnp.concatenate([row, got]), jnp.concatenate([got, row]))
    return passed_on(both, 2, 4, cube_count, slot)


def child_sources(table, child_size, cube_at, grid_at):
    parent_size = 2 * child_size
    slot = cube_at % parent_size
    front = cube_at // child_size
    maps = jnp.stack([table[front], table[front ^ 1]])
    rows = jnp.arange(ROWS) * parent_size + slot
    cols = jnp.arange(parent_size) * 4 + grid_at
    child_ids = jnp.arange(PIVOTS, ROWS * child_size)
    row_hit = maps[:, None, :] == rows[None, :, None]
    col_hit = maps[:, None, :] == cols[None, :, None]
    row_from = jnp.sum(jnp.where(row_hit, child_ids // child_size + 1, 0), 2) - 1
    col_from = jnp.sum(jnp.where(col_hit, child_ids // 4 + 1, 0), 2) - 1
    return jnp.concatenate([row_from, col_from], 1).astype(jnp.int32)


def column_targets(table, child_size, cube_at, grid_at, sources, count):
    mapping = table[(cube_at // child_size) ^ 1]
    child_ids = jnp.arange(count) * 4 + grid_at
    target = mapping[jnp.maximum(child_ids - PIVOTS, 0)]
    unused = jnp.argmax(sources[1, ROWS:] < 0)
    place = jnp.where(child_ids >= PIVOTS, target // 4, unused)
    valid = (child_ids >= PIVOTS) & (target >= PIVOTS)
    return place.astype(jnp.int32), valid.astype(jnp.int32)


def on_device(
    front_root, front_upper, front_middle, front_lower, place_upper, place_middle, place_lower
):
    cube_count = lax.axis_size("cube")
    cube_at = lax.axis_index("cube")
    grid_at = lax.axis_index("grid")
    stored = (front_root, front_upper, front_middle, front_lower)
    tables = (None, place_upper, place_middle, place_lower)
    factor_list = [None, None, None, None]
    rel = sources = update = None
    everyone = lambda s, g: True
    for depth in (3, 2, 1, 0):
        sub_size = cube_count >> depth
        half = sub_size // 2
        slot = cube_at % sub_size
        front = stored[depth]
        row_ids = jnp.arange(ROWS) * sub_size + slot
        col_ids = jnp.arange(sub_size) * 4 + grid_at
        info = jnp.concatenate([row_ids, col_ids]).astype(jnp.int32)
        children = ()
        if depth == 3:
            panel = front[:, :BS]
        else:
            got = shifted(rel, half, lambda s, g: g < 2, sub_size, cube_count)
            moves = jnp.concatenate([sources.reshape(-1), info])
            panel = pivot_panel(front, rel, got, moves, ())
            if depth == 1:
                own = update(after=(got,))
                other = shifted(own, half, everyone, sub_size, cube_count)
                children = (own, other)
            if depth == 0:
                own_early = update(after=(got,), span=(0, 1))
                other_early = shifted(own_early, half, everyone, sub_size, cube_count)
                from_early = jnp.where(sources[:, ROWS:] < EARLY, sources[:, ROWS:], -1)
                from_late = jnp.maximum(sources[0, ROWS:] - EARLY, -1)
                info = jnp.concatenate(
                    [
                        sources[0, :ROWS],
                        from_early[0],
                        sources[0, :ROWS],
                        from_late,
                        sources[1, :ROWS],
                        from_early[1],
                        info,
                    ]
                )
            else:
                info = moves
        if depth > 0:
            next_sources = child_sources(tables[depth], sub_size, cube_at, grid_at)
            info = jnp.concatenate([info, jnp.maximum(next_sources[0, ROWS : ROWS + 1], 0)])
        own_rows = both_pivots(panel, cube_count, grid_at)
        blocks = own_rows.reshape(ROWS, BS, WIDE)
        if depth == 3:
            pivots = pivot_rows_everywhere(blocks, cube_count, slot)
            panels = class_rows_direct(blocks, cube_count, cube_at, grid_at)
        else:
            share, pivots = quad_exchange(blocks, cube_count, grid_at)
            if depth == 1:
                pivots = copy_after(pivots, (other,))
            pivots = passed_on(pivots, 4, sub_size, cube_count, slot)
            zero = jnp.zeros((1,), jnp.int32)
        if depth == 1:
            pivots = passed_on(pivots, 8, sub_size, cube_count, slot)
        if depth in (2, 1):
            panels = gathered([share], zero, sub_size, cube_count, ())
        if depth == 2:
            own = update(after=(pivots,))
            other = shifted(own, half, everyone, sub_size, cube_count)
            children = (own, other)
        if depth == 0:
            load = jnp.concatenate([share, pivots])
            pieces = [load] + [
                shifted(load, bit, everyone, sub_size, cube_count) for bit in (8, 16, 24)
            ]
            plane = cube_at // 8
            pivots = pieces[0][BS:]
            for step in (1, 2, 3):
                pivots = jnp.where(plane == step, pieces[step][BS:], pivots)
            own_late = update(after=(load, other_early), span=(1, 3))
            panels = gathered(
                pieces, plane.astype(jnp.int32).reshape(1), 8, cube_count, (own_late,)
            )
            other_late = shifted(own_late, half, everyone, sub_size, cube_count)
            children = (own_early, own_late, other_early)
        low, inverse = pivot_factor(pivots)
        solved = dot_nt(own_rows, inverse)
        pivot_slot = jnp.minimum(slot, PIVOTS - 1)
        head = jnp.where(
            slot < PIVOTS, lax.dynamic_slice_in_dim(low, pivot_slot * BS, BS, 0), solved[:BS]
        )
        solved = jnp.concatenate([head, solved[BS:]])
        factor_list[depth] = solved
        update = functools.partial(update_front, front, children, solved, panels, inverse, info)
        if depth > 0:
            rel = update(single=True)
            sources = next_sources
    rest = update(is_root=True)
    count = sources.shape[1] // 2 - ROWS // 2
    place, valid = column_targets(tables[1], half, cube_at, grid_at, sources, count)
    row_part = jnp.concatenate([sources[1, :ROWS], row_ids]).astype(jnp.int32)
    rest = add_columns(
        rest, other_late, jnp.concatenate([row_part, place[EARLY:], valid[EARLY:]])
    )
    return (factor_list[0], factor_list[1], factor_list[2], factor_list[3], rest)


def solution(mesh):
    return jax.shard_map(
        on_device,
        mesh=mesh,
        in_specs=(
            P("cube", "grid"),
            P("cube", "grid"),
            P("cube", "grid"),
            P("cube", "grid"),
            P(),
            P(),
            P(),
        ),
        out_specs=(
            P("cube", None),
            P("cube", None),
            P("cube", None),
            P("cube", None),
            P("cube", "grid"),
        ),
        check_vma=False,
    )
```

```python
import functools

import jax
import jax.numpy as jnp
from jax import lax
from jax.experimental import pallas as pl
from jax.experimental.pallas import tpu as pltpu
from jax.sharding import PartitionSpec as P

BS = 128
PIVOTS = 2
ROWS = 4
WIDE = PIVOTS * BS
HIGHEST = lax.Precision.HIGHEST
EARLY = 4
GROUP = 8
VMEM_LIMIT = 48 * 1024 * 1024


def dot_nn(a, b):
    return jnp.dot(a, b, precision=HIGHEST, preferred_element_type=jnp.float32)


def dot_nt(a, b):
    return lax.dot_general(
        a, b, (((1,), (1,)), ((), ())), precision=HIGHEST, preferred_element_type=jnp.float32
    )


def factor_block(block):
    n = BS
    rows = lax.broadcasted_iota(jnp.int32, (n, n), 0)
    eye = (rows == lax.broadcasted_iota(jnp.int32, (n, n), 1)).astype(jnp.float32)
    parts = [block, eye]
    for j in range(0, n, GROUP):
        cols = [jnp.broadcast_to(parts[0][:, j + t : j + t + 1], (n, n)) for t in range(GROUP)]
        mults = []
        for t in range(GROUP):
            col = cols[t]
            mult = jnp.where(rows > j + t, col * (1.0 / col[j + t : j + t + 1]), 0.0)
            for u in range(t + 1, GROUP):
                cols[u] = cols[u] - mult * col[j + u : j + u + 1]
            mults.append(mult)
        done = []
        for part in parts:
            total, heads = part, []
            for t in range(GROUP):
                head = part[j + t : j + t + 1]
                for u in range(t):
                    head = head - mults[u][j + t : j + t + 1] * heads[u]
                heads.append(head)
                total = total - mults[t] * head
            done.append(total)
        parts = done
    diag = jnp.sum(jnp.where(eye > 0, parts[0], 0.0), 1, keepdims=True)
    scale = lax.rsqrt(diag)
    return (parts[0] * scale).T, parts[1] * scale


def pivot_kernel(rows_ref, low_ref, inv_ref):
    c0, i0 = factor_block(rows_ref[:BS, :BS])
    k10 = dot_nt(rows_ref[BS:, :BS], i0)
    c1, i1 = factor_block(rows_ref[BS:, BS:] - dot_nt(k10, k10))
    lane = lax.broadcasted_iota(jnp.int32, (BS, BS), 1)
    sub = lax.broadcasted_iota(jnp.int32, (BS, BS), 0)
    low = lane <= sub
    zero = jnp.zeros((BS, BS), jnp.float32)
    low_ref[:BS, :BS] = jnp.where(low, c0, 0.0)
    low_ref[:BS, BS:] = zero
    low_ref[BS:, :BS] = k10
    low_ref[BS:, BS:] = jnp.where(low, c1, 0.0)
    inv_ref[:BS, :BS] = i0
    inv_ref[:BS, BS:] = zero
    inv_ref[BS:, :BS] = -dot_nn(i1, dot_nn(k10, i0))
    inv_ref[BS:, BS:] = i1


def pivot_factor(pivot_rows):
    shape = jax.ShapeDtypeStruct((WIDE, WIDE), jnp.float32)
    whole = pl.BlockSpec(memory_space=pltpu.VMEM)
    return pl.pallas_call(
        pivot_kernel,
        out_shape=[shape, shape],
        in_specs=[whole],
        out_specs=[whole, whole],
        compiler_params=pltpu.CompilerParams(vmem_limit_bytes=VMEM_LIMIT),
        name="pivot_factor",
    )(pivot_rows)


ANY = pl.BlockSpec(memory_space=pl.ANY)


def parts_of(a):
    high = a.astype(jnp.bfloat16)
    return high, (a - high.astype(jnp.float32)).astype(jnp.bfloat16)


def split_left(a):
    high, low = parts_of(a)
    return jnp.concatenate([high, low, high], 1)


def split_right(a):
    high, low = parts_of(a)
    return jnp.concatenate([high, high, low], 0)


def dot_split(left, right):
    return jnp.dot(left, right, preferred_element_type=jnp.float32)


def update_kernel(cols, per, children, is_root, col_of, place_of, info_ref, *refs):
    front_ref, refs = refs[0], refs[1:]
    child_refs, refs = refs[: children * per], refs[children * per :]
    key_ref, panel_ref, inv_ref = refs[:3]
    out_ref, key_split, inv_split = refs[-3:]
    step = pl.program_id(0)

    @pl.when(step == 0)
    def _():
        key_split[...] = split_left(key_ref[...])
        inv_split[...] = split_left(inv_ref[...])

    panel = jnp.concatenate([panel_ref[place_of(t)] for t in range(per)], 1)
    solved = dot_split(inv_split[...], split_right(panel))
    terms = dot_split(key_split[...], split_right(solved))
    width = ROWS + cols
    places = children * width
    for t in range(per):
        at = col_of(step, info_ref) * per + t
        lanes = slice(t * BS, (t + 1) * BS)
        for r in range(ROWS):
            span = slice(r * BS, (r + 1) * BS)
            block = front_ref[span, lanes] - terms[span, lanes]
            for which in range(children):
                source = info_ref[which * width + r]
                present = (source >= 0) & (info_ref[which * width + ROWS + at] >= 0)
                taken = child_refs[which * per + t][pl.ds(jnp.maximum(source, 0) * BS, BS), :]
                block = block + jnp.where(present, taken, 0.0)
            if is_root:
                keep = (info_ref[places + r] >= PIVOTS) & (info_ref[places + ROWS + at] >= PIVOTS)
                block = jnp.where(keep, block, 0.0)
            out_ref[span, lanes] = block


def update_front(front, children, key, panels, inverse, info, is_root=False, single=False, span=None, after=()):
    cols = front.shape[1] // BS
    width = ROWS + cols
    height = ROWS * BS
    per = 1 if single else 4
    rel_at = (len(children) + 1) * width
    first, steps = (0, 1) if single else span or (0, cols // per)
    if single:
        col_of = lambda c, info: info[rel_at]
    else:
        col_of = lambda c, info: c + first
    outer, _, planes = panels.shape[:3]
    place_of = lambda t: (t % outer, t // outer, 0)
    if single:
        panel_dims = (1, 1, 1)
        panel_at = lambda c, info: (lax.rem(col_of(c, info), outer), lax.div(col_of(c, info), outer), 0, 0, 0)
    elif planes == 1:
        panel_dims = (outer, per // outer, 1)
        panel_at = lambda c, info: (0, c + first, 0, 0, 0)
    else:
        panel_dims = (outer, 1, per // outer)
        runs = planes * outer // per
        panel_at = lambda c, info: (0, lax.div(c, runs), lax.rem(c, runs), 0, 0)
        place_of = lambda t: (t % outer, 0, t // outer)

    column = pl.BlockSpec((height, per * BS), lambda c, info: (0, col_of(c, info)))
    specs, args = [column], [front]
    for which, child in enumerate(children):
        for t in range(per):
            specs.append(
                pl.BlockSpec(
                    (height, BS),
                    lambda c, info, which=which, t=t: (
                        0,
                        jnp.maximum(info[which * width + ROWS + col_of(c, info) * per + t], 0),
                    ),
                )
            )
            args.append(child)
    specs += [
        pl.BlockSpec((height, WIDE), lambda c, info: (0, 0)),
        pl.BlockSpec((*panel_dims, WIDE, BS), panel_at),
        pl.BlockSpec((WIDE, WIDE), lambda c, info: (0, 0)),
    ] + [ANY] * len(after)
    args += [key, panels, inverse, *after]
    return pl.pallas_call(
        functools.partial(update_kernel, cols, per, len(children), is_root, col_of, place_of),
        out_shape=jax.ShapeDtypeStruct((height, steps * per * BS), jnp.float32),
        grid_spec=pltpu.PrefetchScalarGridSpec(
            num_scalar_prefetch=1,
            grid=(steps,),
            in_specs=specs,
            out_specs=pl.BlockSpec((height, per * BS), lambda c, info: (0, c)),
            scratch_shapes=[
                pltpu.VMEM((height, 3 * WIDE), jnp.bfloat16),
                pltpu.VMEM((WIDE, 3 * WIDE), jnp.bfloat16),
            ],
        ),
        compiler_params=pltpu.CompilerParams(vmem_limit_bytes=VMEM_LIMIT),
        cost_estimate=pl.CostEstimate(
            flops=2 * height * WIDE * steps * per * BS * 2,
            bytes_accessed=16 * height * steps * per * BS,
            transcendentals=0,
        ),
        name="update_front",
    )(info, *args)


def panel_kernel(width, info_ref, front_ref, own_ref, other_ref, *refs):
    out_ref = refs[-1]
    for r in range(ROWS):
        block = front_ref[r * BS : (r + 1) * BS, :]
        for which, child_ref in ((0, own_ref), (1, other_ref)):
            source = info_ref[which * width + r]
            present = (source >= 0) & (info_ref[which * width + ROWS] >= 0)
            taken = child_ref[pl.ds(jnp.maximum(source, 0) * BS, BS), :]
            block = block + jnp.where(present, taken, 0.0)
        out_ref[r * BS : (r + 1) * BS, :] = block


def pivot_panel(front, own, other, info, after):
    piece = pl.BlockSpec((ROWS * BS, BS), lambda c, info: (0, 0))
    return pl.pallas_call(
        functools.partial(panel_kernel, ROWS + front.shape[1] // BS),
        out_shape=jax.ShapeDtypeStruct((ROWS * BS, BS), jnp.float32),
        grid_spec=pltpu.PrefetchScalarGridSpec(
            num_scalar_prefetch=1,
            grid=(1,),
            in_specs=[piece] * 3 + [ANY] * len(after),
            out_specs=piece,
        ),
        name="pivot_panel",
    )(info, front, own, other, *after)


def add_kernel(count, info_ref, front_ref, child_ref, out_ref):
    valid = info_ref[2 * ROWS + count + pl.program_id(0)] > 0
    for r in range(ROWS):
        span = slice(r * BS, (r + 1) * BS)
        source = info_ref[r]
        present = valid & (source >= 0) & (info_ref[ROWS + r] >= PIVOTS)
        taken = child_ref[pl.ds(jnp.maximum(source, 0) * BS, BS), :]
        out_ref[span, :] = front_ref[span, :] + jnp.where(present, taken, 0.0)


def add_columns(front, child, info):
    count = child.shape[1] // BS
    target = pl.BlockSpec((ROWS * BS, BS), lambda c, info: (0, info[2 * ROWS + c]))
    return pl.pallas_call(
        functools.partial(add_kernel, count),
        out_shape=jax.ShapeDtypeStruct(front.shape, jnp.float32),
        grid_spec=pltpu.PrefetchScalarGridSpec(
            num_scalar_prefetch=1,
            grid=(count,),
            in_specs=[target, pl.BlockSpec((ROWS * BS, BS), lambda c, info: (0, c))],
            out_specs=target,
        ),
        input_output_aliases={1: 0},
        compiler_params=pltpu.CompilerParams(vmem_limit_bytes=VMEM_LIMIT),
        name="add_columns",
    )(info, front, child)


def copy_kernel(in_ref, *refs):
    refs[-1][...] = in_ref[...]


def copy_after(array, after, low=0, high=None):
    rows, cols = array.shape
    high = cols if high is None else high
    wide = WIDE
    return pl.pallas_call(
        copy_kernel,
        out_shape=jax.ShapeDtypeStruct((rows, high - low), jnp.float32),
        grid=((high - low) // wide,),
        in_specs=[pl.BlockSpec((rows, wide), lambda c: (0, c + low // wide))] + [ANY] * len(after),
        out_specs=pl.BlockSpec((rows, wide), lambda c: (0, c)),
        name="copy_after",
    )(array, *after)


def spread_kernel(count, at_ref, *refs):
    pieces, out_ref, scratch = refs[:count], refs[-2], refs[-1]

    @pl.when(pl.program_id(0) == 0)
    def _():
        for step in range(count):
            turned = pieces[step][...].T
            for place in range(count):

                @pl.when(at_ref[0] == place ^ step)
                def _():
                    scratch[place] = turned

    for t in range(out_ref.shape[0]):
        out_ref[t] = scratch[...]


def spread(pieces, at, copies, after):
    count = len(pieces)
    shape = (count, WIDE, BS)
    each = 4 if count == 1 else 2
    return pl.pallas_call(
        functools.partial(spread_kernel, count),
        out_shape=jax.ShapeDtypeStruct((copies, *shape), jnp.float32),
        grid_spec=pltpu.PrefetchScalarGridSpec(
            num_scalar_prefetch=1,
            grid=(copies // each,),
            in_specs=[pl.BlockSpec((BS, WIDE), lambda c, at: (0, 0))] * count + [ANY] * len(after),
            out_specs=pl.BlockSpec((each, *shape), lambda c, at: (c, 0, 0, 0)),
            scratch_shapes=[pltpu.VMEM(shape, jnp.float32)],
        ),
        compiler_params=pltpu.CompilerParams(vmem_limit_bytes=VMEM_LIMIT),
        name="spread",
    )(at, *pieces, *after)


def send(block, route):
    pairs = [(a[0] * 4 + a[1], b[0] * 4 + b[1]) for a, b in route]
    return lax.ppermute(block, ("cube", "grid"), pairs)


def both_pivots(piece, cube_count, grid_at):
    near = send(piece, [((s, g), (s, g ^ 1)) for s in range(cube_count) for g in (0, 1)])
    far = send(piece, [((s, g), (s, g ^ 2)) for s in range(cube_count) for g in (0, 1)])
    cross = send(far, [((s, g), (s, g ^ 1)) for s in range(cube_count) for g in (2, 3)])
    mine = jnp.where(grid_at < 2, piece, far)
    mate = jnp.where(grid_at < 2, near, cross)
    first = jnp.where(grid_at % 2 == 0, mine, mate)
    second = jnp.where(grid_at % 2 == 0, mate, mine)
    return jnp.concatenate([first, second], -1)


def shifted(block, bit, sources, sub_size, cube_count, grids=None):
    route = []
    for base in range(0, cube_count, sub_size):
        for s in range(sub_size):
            for g in range(4):
                if sources(s, g):
                    route.append(((base + s, g), (base + (s ^ bit), g)))
    return send(block, route)


def quad_exchange(own_rows, cube_count, grid_at):
    load = jnp.stack([own_rows, jnp.broadcast_to(own_rows[:1], own_rows.shape)], 1)
    quads = [[b + i for i in range(4)] for b in range(0, cube_count, 4)]
    got = lax.all_to_all(load, "cube", 0, 0, axis_index_groups=quads)
    share = lax.dynamic_index_in_dim(got[:, 0], grid_at, 0, keepdims=False)
    return share, got[:PIVOTS, 1].reshape(WIDE, WIDE)


def passed_on(both, known, sub_size, cube_count, slot):
    moved = shifted(both, known, lambda s, g: s < known, sub_size, cube_count)
    return jnp.where(slot < known, both, moved)


def class_rows_direct(own_rows, cube_count, cube_at, grid_at):
    total = jnp.where(cube_at % 4 == grid_at, own_rows, 0.0)
    for step in (1, 2, 3):
        total = total + shifted(own_rows, step, lambda s, g: s == g, 4, cube_count)
    return total.transpose(0, 2, 1).reshape(ROWS, 1, 1, WIDE, BS)


def gathered(pieces, at, group, cube_count, after):
    groups = None
    if group < cube_count:
        groups = [[b + i for i in range(group)] for b in range(0, cube_count, group)]
    everything = lax.all_to_all(
        spread(pieces, at, group, after), "cube", 0, 0, axis_index_groups=groups
    )
    return everything.reshape(group // 4, 4, len(pieces), WIDE, BS)


def pivot_rows_everywhere(own_rows, cube_count, slot):
    row = own_rows[0]
    got = shifted(row, 1, lambda s, g: s < 2, 4, cube_count)
    both = jnp.where(slot == 0, jnp.concatenate([row, got]), jnp.concatenate([got, row]))
    return passed_on(both, 2, 4, cube_count, slot)


def child_sources(table, child_size, cube_at, grid_at):
    parent_size = 2 * child_size
    slot = cube_at % parent_size
    front = cube_at // child_size
    maps = jnp.stack([table[front], table[front ^ 1]])
    rows = jnp.arange(ROWS) * parent_size + slot
    cols = jnp.arange(parent_size) * 4 + grid_at
    child_ids = jnp.arange(PIVOTS, ROWS * child_size)
    row_hit = maps[:, None, :] == rows[None, :, None]
    col_hit = maps[:, None, :] == cols[None, :, None]
    row_from = jnp.sum(jnp.where(row_hit, child_ids // child_size + 1, 0), 2) - 1
    col_from = jnp.sum(jnp.where(col_hit, child_ids // 4 + 1, 0), 2) - 1
    return jnp.concatenate([row_from, col_from], 1).astype(jnp.int32)


def column_targets(table, child_size, cube_at, grid_at, sources, count):
    mapping = table[(cube_at // child_size) ^ 1]
    child_ids = jnp.arange(count) * 4 + grid_at
    target = mapping[jnp.maximum(child_ids - PIVOTS, 0)]
    unused = jnp.argmax(sources[1, ROWS:] < 0)
    place = jnp.where(child_ids >= PIVOTS, target // 4, unused)
    valid = (child_ids >= PIVOTS) & (target >= PIVOTS)
    return place.astype(jnp.int32), valid.astype(jnp.int32)


def on_device(
    front_root, front_upper, front_middle, front_lower, place_upper, place_middle, place_lower
):
    cube_count = lax.axis_size("cube")
    cube_at = lax.axis_index("cube")
    grid_at = lax.axis_index("grid")
    stored = (front_root, front_upper, front_middle, front_lower)
    tables = (None, place_upper, place_middle, place_lower)
    factor_list = [None, None, None, None]
    rel = sources = update = None
    everyone = lambda s, g: True
    for depth in (3, 2, 1, 0):
        sub_size = cube_count >> depth
        half = sub_size // 2
        slot = cube_at % sub_size
        front = stored[depth]
        row_ids = jnp.arange(ROWS) * sub_size + slot
        col_ids = jnp.arange(sub_size) * 4 + grid_at
        info = jnp.concatenate([row_ids, col_ids]).astype(jnp.int32)
        children = ()
        if depth == 3:
            panel = front[:, :BS]
        else:
            got = shifted(rel, half, lambda s, g: g < 2, sub_size, cube_count)
            moves = jnp.concatenate([sources.reshape(-1), info])
            panel = pivot_panel(front, rel, got, moves, ())
            if depth > 0:
                own = update(after=(got,))
                other = shifted(own, half, everyone, sub_size, cube_count)
                children = (own, other)
            if depth == 0:
                own_early = update(after=(got,), span=(0, 1))
                other_early = shifted(own_early, half, everyone, sub_size, cube_count)
                from_early = jnp.where(sources[:, ROWS:] < EARLY, sources[:, ROWS:], -1)
                from_late = jnp.maximum(sources[0, ROWS:] - EARLY, -1)
                info = jnp.concatenate(
                    [
                        sources[0, :ROWS],
                        from_early[0],
                        sources[0, :ROWS],
                        from_late,
                        sources[1, :ROWS],
                        from_early[1],
                        info,
                    ]
                )
            else:
                info = moves
        if depth > 0:
            next_sources = child_sources(tables[depth], sub_size, cube_at, grid_at)
            info = jnp.concatenate([info, jnp.maximum(next_sources[0, ROWS : ROWS + 1], 0)])
        own_rows = both_pivots(panel, cube_count, grid_at)
        blocks = own_rows.reshape(ROWS, BS, WIDE)
        if depth == 3:
            pivots = pivot_rows_everywhere(blocks, cube_count, slot)
            panels = class_rows_direct(blocks, cube_count, cube_at, grid_at)
        else:
            share, pivots = quad_exchange(blocks, cube_count, grid_at)
            if depth > 0:
                pivots = copy_after(pivots, (other,))
            pivots = passed_on(pivots, 4, sub_size, cube_count, slot)
            zero = jnp.zeros((1,), jnp.int32)
        if depth == 1:
            pivots = passed_on(pivots, 8, sub_size, cube_count, slot)
        if depth in (2, 1):
            panels = gathered([share], zero, sub_size, cube_count, ())
        if depth == 0:
            load = jnp.concatenate([share, pivots])
            pieces = [load] + [
                shifted(load, bit, everyone, sub_size, cube_count) for bit in (8, 16, 24)
            ]
            plane = cube_at // 8
            pivots = pieces[0][BS:]
            for step in (1, 2, 3):
                pivots = jnp.where(plane == step, pieces[step][BS:], pivots)
            own_late = update(after=(load, other_early), span=(1, 3))
            panels = gathered(
                pieces, plane.astype(jnp.int32).reshape(1), 8, cube_count, (own_late,)
            )
            other_late = shifted(own_late, half, everyone, sub_size, cube_count)
            children = (own_early, own_late, other_early)
        low, inverse = pivot_factor(pivots)
        solved = dot_nt(own_rows, inverse)
        pivot_slot = jnp.minimum(slot, PIVOTS - 1)
        head = jnp.where(
            slot < PIVOTS, lax.dynamic_slice_in_dim(low, pivot_slot * BS, BS, 0), solved[:BS]
        )
        solved = jnp.concatenate([head, solved[BS:]])
        factor_list[depth] = solved
        update = functools.partial(update_front, front, children, solved, panels, inverse, info)
        if depth > 0:
            rel = update(single=True)
            sources = next_sources
    rest = update(is_root=True)
    count = sources.shape[1] // 2 - ROWS // 2
    place, valid = column_targets(tables[1], half, cube_at, grid_at, sources, count)
    row_part = jnp.concatenate([sources[1, :ROWS], row_ids]).astype(jnp.int32)
    rest = add_columns(
        rest, other_late, jnp.concatenate([row_part, place[EARLY:], valid[EARLY:]])
    )
    return (factor_list[0], factor_list[1], factor_list[2], factor_list[3], rest)


def solution(mesh):
    return jax.shard_map(
        on_device,
        mesh=mesh,
        in_specs=(
            P("cube", "grid"),
            P("cube", "grid"),
            P("cube", "grid"),
            P("cube", "grid"),
            P(),
            P(),
            P(),
        ),
        out_specs=(
            P("cube", None),
            P("cube", None),
            P("cube", None),
            P("cube", None),
            P("cube", "grid"),
        ),
        check_vma=False,
    )
```
